32 devices in a mesh: pipe: 2 (over y), tensor: 4 (over x, core), dp: 4 (over z).
Axes of the slice: x: 2, y: 2, z: 4, core: 2. Of those that a mesh axis runs over, the one named last changes fastest.
Arguments:
- frames: bfloat16 [4, 8, 197, 768], P('dp'), may hold values from -6 to 6
- video_group: int32 [4], replicated, may hold values from 0 to 1, as said below
- msg_w: bfloat16 [768, 768], replicated, may hold values from -0.21875 to 0.21875
- msg_bias: float32 [768], replicated, may hold values from -3 to 3
- norm_gain: float32 [2, 768], P('pipe'), may hold values from 0.5 to 1.5
- norm_shift: float32 [2, 768], P('pipe'), may hold values from -1 to 1
- attn_in: bfloat16 [2, 768, 3, 768], P('pipe', None, None, 'tensor'), may hold values from -0.21875 to 0.21875
- qv_bias: float32 [2, 2, 768], P('pipe', None, 'tensor'), may hold values from -1.5 to 1.5
- attn_out: bfloat16 [2, 768, 768], P('pipe', 'tensor'), may hold values from -1.25 to 1.25
- out_bias: float32 [2, 768], P('pipe'), may hold values from -1 to 1
- norm2_gain: float32 [768], replicated, may hold values from 0.5 to 1.5
- norm2_shift: float32 [768], replicated, may hold values from -1 to 1
- fc_in: bfloat16 [768, 3072], P(None, 'tensor'), may hold values from -0.21875 to 0.21875
- fc_in_bias: float32 [3072], P('tensor'), may hold values from -1.5 to 1.5
- fc_out: bfloat16 [3072, 768], P('tensor'), may hold values from -0.109375 to 0.109375
- fc_out_bias: float32 [768], replicated, may hold values from -1 to 1
- cotangent: bfloat16 [4, 8, 197, 768], P('dp'), may hold values from -6 to 6
Outputs:
- block_out: bfloat16 [4, 8, 197, 768], P('dp', 'pipe', None, 'tensor')
- frames_grad: bfloat16 [4, 8, 197, 768], P('dp', 'pipe', None, 'tensor')
- msg_w_grad: float32 [768, 768], P(None, 'tensor')
- msg_bias_grad: float32 [768], replicated
- norm_gain_grad: float32 [2, 768], P('pipe')
- norm_shift_grad: float32 [2, 768], P('pipe')
- attn_in_grad: float32 [2, 768, 3, 768], P('pipe', None, None, 'tensor')
- qv_bias_grad: float32 [2, 2, 768], P('pipe', None, 'tensor')
- attn_out_grad: float32 [2, 768, 768], P('pipe', 'tensor')
- out_bias_grad: float32 [2, 768], P('pipe')
- norm2_gain_grad: float32 [768], replicated
- norm2_shift_grad: float32 [768], replicated
- fc_in_grad: float32 [768, 3072], P(None, 'tensor')
- fc_in_bias_grad: float32 [3072], P('tensor')
- fc_out_grad: float32 [3072, 768], P('tensor')
- fc_out_bias_grad: float32 [768], replicated
The draws below stay inside these ranges and needn't reach their ends.
Inputs may be any that keep to these rules, and one draw needn't show every extreme that they name: `video_group`: the message tokens of a clip attend to the message tokens of every clip of the same video; the first, the middle and the last clip share one video.
All inputs are finite; a program needn't handle non-finite values.
Results may differ from the reference program's by a relative error of at most 0.039.
Values may be sent and summed in bfloat16 or wider, within the bound.
No kernel may reach another device: no remote copies, remote signals or barrier semaphores. Data moves between devices by JAX's collectives and lax.ppermute only.
A program may use at most 192 MiB of HBM per device.

```python
import jax
import jax.numpy as jnp
from jax import lax

D = 768
HEADS = 12
HEAD_DIM = 64
FF = 3072
PATCH = 197
FRAMES = 8
CLIPS = 4
GROUPS = 2


def draw_video_group(key, part):
    key = jax.random.fold_in(key, 7)
    label_key, leader_key = jax.random.split(key)
    labels = jax.random.randint(label_key, (CLIPS,), 0, GROUPS, dtype=jnp.int32)
    leader = jax.random.randint(leader_key, (), 0, GROUPS, dtype=jnp.int32)
    labels = labels.at[1].set(jnp.where(leader == 0, GROUPS - 1, 0).astype(jnp.int32))
    labels = labels.at[CLIPS // 2 - 1].set(jnp.where(leader == GROUPS - 1, 0, GROUPS - 1).astype(jnp.int32))
    labels = labels.at[0].set(leader)
    labels = labels.at[CLIPS // 2].set(leader)
    labels = labels.at[CLIPS - 1].set(leader)
    return labels.astype(jnp.int32)


def level_of(key, extent, shards, least, top_value):
    loudness = 1.0
    for dim, shards_of in shards:
        steps = jax.random.uniform(jax.random.fold_in(jax.random.fold_in(key, 6), dim), (shards_of,), jnp.float32, least / len(shards), top_value / len(shards))
        loudness = loudness * jnp.repeat(jnp.exp(steps), extent[dim] // shards_of).reshape((-1,) + (1,) * (len(extent) - 1 - dim))
    return loudness


def normal_values(rng, extent, scale, bound, pieces=(), kind=jnp.bfloat16):
    level = level_of(rng, extent, pieces, -0.22, 0.18) if pieces else 1.0
    entries = jax.random.normal(rng, extent, jnp.float32) * scale * level
    return jnp.minimum(jnp.maximum(entries, -bound), bound).astype(kind)


def setup_inputs(seed: int = 0) -> dict:
    arg_keys = jax.random.split(jax.random.key(seed), 18)
    return {
        "frames": normal_values(arg_keys[0], (CLIPS, FRAMES, PATCH, D), 1.0, 6.0, ((0, 4),)),
        "video_group": draw_video_group(jax.random.fold_in(arg_keys[17], 71), 0),
        "msg_w": normal_values(arg_keys[2], (D, D), D ** -0.5, 0.21875),
        "msg_bias": normal_values(arg_keys[3], (D,), 0.5, 3.0, (), jnp.float32),
        "norm_gain": jnp.clip(1.0 + 0.1 * jax.random.normal(arg_keys[4], (2, D), jnp.float32), 0.5, 1.5),
        "norm_shift": normal_values(arg_keys[5], (2, D), 0.2, 1.0, ((0, 2),), jnp.float32),
        "attn_in": normal_values(arg_keys[6], (2, D, 3, D), D ** -0.5, 0.21875, ((0, 2), (3, 4))),
        "qv_bias": normal_values(arg_keys[7], (2, 2, D), 0.3, 1.5, ((0, 2), (2, 4)), jnp.float32),
        "attn_out": normal_values(arg_keys[8], (2, D, D), (D // 32) ** -0.5, 1.25, ((0, 2), (1, 4))),
        "out_bias": normal_values(arg_keys[9], (2, D), 0.2, 1.0, ((0, 2),), jnp.float32),
        "norm2_gain": jnp.clip(1.0 + 0.1 * jax.random.normal(arg_keys[10], (D,), jnp.float32), 0.5, 1.5),
        "norm2_shift": normal_values(arg_keys[11], (D,), 0.2, 1.0, (), jnp.float32),
        "fc_in": normal_values(arg_keys[12], (D, FF), D ** -0.5, 0.21875, ((1, 4),)),
        "fc_in_bias": normal_values(arg_keys[13], (FF,), 0.3, 1.5, ((0, 4),), jnp.float32),
        "fc_out": normal_values(arg_keys[14], (FF, D), FF ** -0.5, 0.109375, ((0, 4),)),
        "fc_out_bias": normal_values(arg_keys[15], (D,), 0.2, 1.0, (), jnp.float32),
        "cotangent": normal_values(arg_keys[16], (CLIPS, FRAMES, PATCH, D), 1.0, 6.0, ((0, 4),)),
    }


@jax.custom_vjp
def low(v):
    return lax.optimization_barrier(v.astype(jnp.bfloat16)).astype(jnp.float32)

@jax.custom_vjp
def low_back(v):
    return v

def low_keep(v):
    return (low(v), None)

def low_pass(kept, grad):
    return (grad,)

def back_keep(v):
    return (v, None)

def back_low(kept, grad):
    return (low(grad),)
low.defvjp(low_keep, low_pass)
low_back.defvjp(back_keep, back_low)
HIGHEST = lax.Precision.HIGHEST

def both_ways(values_in):
    return low_back(low(values_in))

def product(left, right):
    return jnp.dot(left, right, precision=HIGHEST)

def layer_norm(values_in, gain_in, offset_in):
    centred = values_in - lax.optimization_barrier(jnp.mean(values_in, axis=-1, keepdims=True))
    variance = lax.optimization_barrier(jnp.mean(centred * centred, axis=-1, keepdims=True))
    return centred * lax.rsqrt(variance + 1e-05) * gain_in + offset_in

def softmax_rows(scores):
    highest = lax.optimization_barrier(jnp.max(scores, axis=-1, keepdims=True))
    exponent = jnp.exp(scores - highest)
    return exponent / lax.optimization_barrier(jnp.sum(exponent, axis=-1, keepdims=True))

def split_heads(values_in):
    return values_in.reshape(values_in.shape[:-1] + (HEADS, HEAD_DIM))

def message_layer(cls_rows, same_video, msg_w, msg_bias, gain_in, offset_in, weight_in, bias_pair, weight_out, bias_out):
    first_msg = product(cls_rows, msg_w) + msg_bias
    normed = low(layer_norm(first_msg, gain_in, offset_in))
    projected = product(normed, weight_in.reshape(D, 3 * D)).reshape(-1, 3, D)
    queries = split_heads(both_ways(projected[:, 0] + bias_pair[0]))
    keys_all = split_heads(both_ways(projected[:, 1]))
    values_all = split_heads(both_ways(projected[:, 2] + bias_pair[1]))
    raw_scores = jnp.einsum('qhe,khe->hqk', queries, keys_all, precision=HIGHEST)
    scores = low_back(raw_scores * HEAD_DIM ** (-0.5))
    scores = jnp.where(same_video[None], scores, -jnp.inf)
    probabilities = low(softmax_rows(scores))
    mixed_heads = both_ways(jnp.einsum('hqk,khe->qhe', probabilities, values_all, precision=HIGHEST).reshape(-1, D))
    return first_msg + product(mixed_heads, weight_out) + bias_out

def block_clip(patches_in, message_in, weights):
    gain_in, offset_in, weight_in, bias_pair, weight_out, bias_out, gain_two, offset_two, fc_weight_in, fc_bias_in, fc_weight_out, fc_bias_out = weights
    tokens = jnp.concatenate([patches_in, message_in[:, None, :]], axis=1)
    normed = low(layer_norm(tokens, gain_in, offset_in))
    projected = jnp.einsum('frd,dck->frck', normed, weight_in, precision=HIGHEST)
    queries = split_heads(both_ways(projected[:, :, 0] + bias_pair[0]))
    keys_all = split_heads(both_ways(projected[:, :, 1]))
    values_all = split_heads(both_ways(projected[:, :, 2] + bias_pair[1]))
    scores = low_back(jnp.einsum('fihe,fjhe->fhij', queries, keys_all, precision=HIGHEST) * HEAD_DIM ** (-0.5))
    probabilities = low(softmax_rows(scores))
    mixed_heads = both_ways(jnp.einsum('fhij,fjhe->fihe', probabilities, values_all, precision=HIGHEST).reshape(FRAMES, PATCH + 1, D))
    branch = low_back(jnp.einsum('frk,kd->frd', mixed_heads, weight_out, precision=HIGHEST) + bias_out)
    residual = patches_in + branch[:, :PATCH]
    normed_two = low(layer_norm(residual, gain_two, offset_two))
    hidden_in = low_back(jnp.einsum('fpd,dk->fpk', normed_two, fc_weight_in, precision=HIGHEST) + fc_bias_in)
    hidden = low(hidden_in * jax.nn.sigmoid(1.702 * hidden_in))
    return residual + jnp.einsum('fpk,kd->fpd', hidden, fc_weight_out, precision=HIGHEST) + fc_bias_out

def forward(frames, video_group, msg_w, msg_bias, norm_gain, norm_shift, attn_in, qv_bias, attn_out, out_bias, norm2_gain, norm2_shift, fc_in, fc_in_bias, fc_out, fc_out_bias):
    cls_rows = frames[:, :, 0, :].reshape(CLIPS * FRAMES, D)
    owner_ids = jnp.repeat(video_group, FRAMES)
    same_video = owner_ids[:, None] == owner_ids[None, :]
    message = message_layer(cls_rows, same_video, msg_w, msg_bias, norm_gain[0], norm_shift[0], attn_in[0], qv_bias[0], attn_out[0], out_bias[0])
    message = both_ways(message).reshape(CLIPS, FRAMES, D)
    weights = (norm_gain[1], norm_shift[1], attn_in[1], qv_bias[1], attn_out[1], out_bias[1], norm2_gain, norm2_shift, fc_in, fc_in_bias, fc_out, fc_out_bias)

    def one_clip(clip_pair):
        return block_clip(clip_pair[0], clip_pair[1], weights)
    return lax.map(jax.checkpoint(one_clip), (frames, message))

def reference(frames, video_group, msg_w, msg_bias, norm_gain, norm_shift, attn_in, qv_bias, attn_out, out_bias, norm2_gain, norm2_shift, fc_in, fc_in_bias, fc_out, fc_out_bias, cotangent):
    floats = tuple((array_in.astype(jnp.float32) for array_in in (frames, msg_w, msg_bias, norm_gain, norm_shift, attn_in, qv_bias, attn_out, out_bias, norm2_gain, norm2_shift, fc_in, fc_in_bias, fc_out, fc_out_bias)))

    def run_layer(frames_in, *params):
        return forward(frames_in, video_group, *params)
    outputs, pullback = jax.vjp(run_layer, *floats)
    gradients = pullback(cotangent.astype(jnp.float32))
    return (outputs.astype(jnp.bfloat16), gradients[0].astype(jnp.bfloat16), gradients[1], gradients[2], gradients[3], gradients[4], gradients[5], gradients[6], gradients[7], gradients[8], gradients[9], gradients[10], gradients[11], gradients[12], gradients[13], gradients[14])
```

```python
import functools

import jax
import jax.numpy as jnp
from jax import lax
from jax.experimental import pallas as pl
from jax.experimental.pallas import tpu as pltpu
from jax.sharding import PartitionSpec as P

HEAD_DIM = 64
EPSILON = 1e-05
QUICK_GELU = 1.702
F32 = jnp.float32
BF16 = jnp.bfloat16
VMEM_BYTES = 56 * 1024 * 1024


def nn(left, right):
    return lax.dot_general(left, right, (((1,), (0,)), ((), ())), preferred_element_type=F32)


def nt(left, right):
    return lax.dot_general(left, right, (((1,), (1,)), ((), ())), preferred_element_type=F32)


def tn(left, right):
    return lax.dot_general(left, right, (((0,), (0,)), ((), ())), preferred_element_type=F32)


def norm_parts(values_in):
    centred = values_in - jnp.mean(values_in, axis=-1, keepdims=True)
    inverse = lax.rsqrt(jnp.mean(centred * centred, axis=-1, keepdims=True) + EPSILON)
    return centred * inverse, inverse


def norm_back(incoming, normed, inverse, gain):
    weighted = incoming * gain
    centred = weighted - jnp.mean(weighted, axis=-1, keepdims=True)
    return inverse * (centred - normed * jnp.mean(weighted * normed, axis=-1, keepdims=True))


def row_sum(values_in):
    return jnp.sum(values_in, axis=0, keepdims=True)


def block_of(shape, place):
    return pl.BlockSpec(shape, lambda i, info: place)


def run(kernel, info, ins, outs, scratch=(), flops=0):
    arrays, specs, moved = [], [], 0
    for item in ins:
        if isinstance(item, tuple):
            array, shape, place = item
        else:
            array, shape, place = item, item.shape, (0,) * item.ndim
        arrays.append(array)
        specs.append(block_of(shape, place))
        size = array.dtype.itemsize
        for n in shape:
            size *= n
        moved += size
    out_specs = [block_of(o.shape, (0,) * len(o.shape)) for o in outs]
    return pl.pallas_call(
        kernel,
        out_shape=outs,
        grid_spec=pltpu.PrefetchScalarGridSpec(
            num_scalar_prefetch=1,
            grid=(1,),
            in_specs=specs,
            out_specs=out_specs,
            scratch_shapes=list(scratch),
        ),
        compiler_params=pltpu.CompilerParams(vmem_limit_bytes=VMEM_BYTES),
        cost_estimate=pl.CostEstimate(flops=flops, bytes_accessed=moved, transcendentals=0),
    )(info, *arrays)


def shape_of(shape, kind):
    return jax.ShapeDtypeStruct(shape, kind)


def body(
    frames,
    video_group,
    msg_w,
    msg_bias,
    norm_gain,
    norm_shift,
    attn_in,
    qv_bias,
    attn_out,
    out_bias,
    norm2_gain,
    norm2_shift,
    fc_in,
    fc_in_bias,
    fc_out,
    fc_out_bias,
    cotangent,
):
    _, frame_count, patch, model = frames.shape
    width = attn_in.shape[-1]
    hidden_width = fc_in.shape[-1]
    heads = width // HEAD_DIM
    clips = lax.axis_size("dp")
    half = frame_count // 2
    rows = -(-(patch + 1) // 16) * 16
    all_rows = clips * frame_count
    scale = HEAD_DIM ** (-0.5)
    pipe = lax.axis_index("pipe")
    tensor = lax.axis_index("tensor")
    clip = lax.axis_index("dp")
    ring = clips == 4
    info = jnp.stack([pipe, tensor, clip if ring else jnp.zeros_like(clip)]).astype(jnp.int32)
    first_section = pipe == 0

    def core_swap(v):
        return lax.ppermute(v, "tensor", [(i, i ^ 1) for i in range(4)])

    def x_swap(v):
        return lax.ppermute(v, "tensor", [(i, i ^ 2) for i in range(4)])

    def y_swap(v):
        return lax.ppermute(v, "pipe", [(0, 1), (1, 0)])

    def y_late(v):
        return lax.ppermute(v, "pipe", [(0, 1)])

    def y_early(v):
        return lax.ppermute(v, "pipe", [(1, 0)])

    def z_up(v, distance=1):
        return lax.ppermute(v, "dp", [(i, (i + distance) % clips) for i in range(clips)])

    def z_down(v):
        return lax.ppermute(v, "dp", [(i, (i - 1) % clips) for i in range(clips)])

    def gather_clips(v):
        if ring:
            return jnp.stack([v, z_down(v), z_up(v, 2), z_up(v)])
        every = lax.all_gather(v, "dp")
        return lax.dynamic_slice_in_dim(jnp.concatenate([every, every]), clip, clips, 0)

    own_in = jnp.transpose(attn_in[0], (1, 2, 0))
    own_out = attn_out[0]
    vectors = jnp.concatenate(
        [norm_gain, norm_shift, out_bias, jnp.pad(qv_bias[0], ((0, 0), (0, model - width)))]
    )

    cls_rows = frames[0, :, 0, :]
    cls_all = gather_clips(cls_rows).reshape(all_rows, model)
    w_in = jnp.where(first_section, y_early(own_in), own_in)
    w_out = jnp.where(first_section, y_early(own_out), own_out)
    vec = jnp.where(first_section, y_early(vectors), vectors)
    owner = jnp.repeat(
        video_group[(clip + jnp.arange(clips)) % clips], frame_count
    )

    msg_bias_row = msg_bias[None]
    gain_two, shift_two = norm2_gain[None], norm2_shift[None]
    fc_in_bias_row, fc_out_bias_row = fc_in_bias[None], fc_out_bias[None]

    def head_masks(n):
        lane = lax.broadcasted_iota(jnp.int32, (n, width), 1)
        return [(lane >= h * HEAD_DIM) & (lane < (h + 1) * HEAD_DIM) for h in range(heads)]

    def only(mask, v):
        return jnp.where(mask, v, jnp.zeros_like(v))

    def message_forward(
        info_ref, cls, mw, mb, gain, shift, w, bias, wo, ob, col, line,
        first_o, low_o, q_o, k_o, v_o, probs_o, mixed_o, part_o,
    ):
        first = nn(cls[...], mw[...]) + mb[...]
        first_o[...] = first
        normed, _ = norm_parts(first)
        low = (normed * gain[...] + shift[...]).astype(BF16)
        low_o[...] = low
        q = (nt(low, w[0]) + bias[0, 0:1]).astype(BF16)
        k = nt(low, w[1]).astype(BF16)
        v = (nt(low, w[2]) + bias[0, 1:2]).astype(BF16)
        q_o[...] = q
        k_o[...] = k
        v_o[...] = v
        allowed = col[...] == line[...]
        mixed = jnp.zeros((all_rows, width), F32)
        for h, mask in enumerate(head_masks(all_rows)):
            scores = jnp.where(allowed, nt(only(mask, q), k) * scale, -jnp.inf)
            exponent = jnp.exp(scores - jnp.max(scores, axis=-1, keepdims=True))
            probs = exponent / jnp.sum(exponent, axis=-1, keepdims=True)
            probs_o[h] = probs
            mixed = mixed + only(mask, nn(probs.astype(BF16), v))
        mixed = mixed.astype(BF16)
        mixed_o[...] = mixed
        part = nn(mixed, wo[...]) + jnp.where(info_ref[1] == 0, ob[...], 0.0)
        part_o[...] = part[:frame_count]

    (first_msg, low_zero, q_zero, k_zero, v_zero, probs_zero, mixed_zero, part_zero) = run(
        message_forward,
        info,
        [
            cls_all, msg_w, msg_bias_row, norm_gain, norm_shift, own_in, qv_bias, own_out, out_bias,
            owner[:, None], owner[None, :],
        ],
        [
            shape_of((all_rows, model), F32),
            shape_of((all_rows, model), BF16),
            shape_of((all_rows, width), BF16),
            shape_of((all_rows, width), BF16),
            shape_of((all_rows, width), BF16),
            shape_of((heads, all_rows, all_rows), F32),
            shape_of((all_rows, width), BF16),
            shape_of((frame_count, model), F32),
        ],
    )
    part_zero = part_zero + core_swap(part_zero)
    part_zero = part_zero + x_swap(part_zero)
    part_late = y_late(part_zero)

    def slots(v):
        picked = [
            lax.dynamic_index_in_dim(v[0], pipe * half + (tensor ^ s), 0, keepdims=False)
            for s in range(half)
        ]
        return jnp.pad(jnp.stack(picked), ((0, 0), (0, rows - patch), (0, 0)))

    x_slots = slots(frames)
    g_slots = slots(cotangent)

    def grad_hidden_kernel(info_ref, g, w, out):
        for s in range(half):
            out[s] = nt(g[s], w[...]).astype(BF16)

    (g_hidden,) = run(
        grad_hidden_kernel, info, [g_slots, fc_out],
        [shape_of((half, rows, hidden_width), BF16)],
        flops=2 * half * rows * model * hidden_width,
    )

    def project_kernel(info_ref, x, w, v, q_o, k_o, v_o):
        gain, shift = v[0:1], v[1:2]
        for s in range(half):
            normed, _ = norm_parts(x[s].astype(F32))
            low = (normed * gain + shift).astype(BF16)
            q_o[s] = (nt(low, w[0]) + v[3:4, :width]).astype(BF16)
            k_o[s] = nt(low, w[1]).astype(BF16)
            v_o[s] = (nt(low, w[2]) + v[4:5, :width]).astype(BF16)

    q_one, k_one, v_one = run(
        project_kernel, info, [x_slots, w_in, vec],
        [shape_of((half, rows, width), BF16)] * 3,
        flops=2 * half * rows * model * 3 * width,
    )

    def attend_kernel(
        base, info_ref, q, k, v, first, part, late, w, vrow, wo,
        pa_o, pb_o, mixed_o, probs_o, k_o, v_o, msg_o,
    ):
        sec, ten = info_ref[0], info_ref[1]
        msg_o[...] = jnp.zeros_like(msg_o)
        for j in range(2):
            at = pl.ds(sec * half + (ten ^ (base + j)), 1)
            summed = jnp.where(sec == 0, part[at, :], late[at, :])
            msg_o[j : j + 1, :] = (first[at, :] + summed).astype(BF16).astype(F32)
        normed, _ = norm_parts(msg_o[...])
        low = (normed * vrow[0:1] + vrow[1:2]).astype(BF16)
        k_msg = nt(low, w[1])
        v_msg = nt(low, w[2]) + vrow[4:5, :width]
        here = lax.broadcasted_iota(jnp.int32, (rows, width), 0) == patch
        key_here = lax.broadcasted_iota(jnp.int32, (rows, rows), 1) <= patch
        masks = head_masks(rows)
        for j in (1, 0):
            kk = jnp.where(here, k_msg[j : j + 1], k[j].astype(F32)).astype(BF16)
            vv = jnp.where(here, v_msg[j : j + 1], v[j].astype(F32)).astype(BF16)
            k_o[j] = kk
            v_o[j] = vv
            mixed = jnp.zeros((rows, width), F32)
            for h in range(heads):
                scores = nt(only(masks[h], q[j]), kk) * scale
                scores = jnp.where(key_here, scores, -jnp.inf)
                exponent = jnp.exp(scores - jnp.max(scores, axis=-1, keepdims=True))
                probs = exponent * (1.0 / jnp.sum(exponent, axis=-1, keepdims=True))
                probs = probs.astype(BF16)
                probs_o[j, h] = probs
                mixed = mixed + only(masks[h], nn(probs, vv))
            mixed = mixed.astype(BF16)
            mixed_o[j] = mixed
            (pa_o, pb_o)[j][...] = nn(mixed, wo[...]).astype(BF16)

    def attend(pair):
        return run(
            functools.partial(attend_kernel, 2 * pair),
            info,
            [
                (q_one, (2, rows, width), (pair, 0, 0)),
                (k_one, (2, rows, width), (pair, 0, 0)),
                (v_one, (2, rows, width), (pair, 0, 0)),
                first_msg, part_zero, part_late, w_in, vec, w_out,
            ],
            [
                shape_of((rows, model), BF16),
                shape_of((rows, model), BF16),
                shape_of((2, rows, width), BF16),
                shape_of((2, heads, rows, rows), BF16),
                shape_of((2, rows, width), BF16),
                shape_of((2, rows, width), BF16),
                shape_of((16, model), F32),
            ],
            flops=2 * 2 * rows * (width * model + 2 * heads * rows * HEAD_DIM),
        )

    def own_sum(part0, part1, part2, part3):
        two = part2 + core_swap(part3)
        return part0, core_swap(part1), x_swap(two)

    def spread(own):
        one = core_swap(own)
        two = x_swap(own)
        return own, one, two, core_swap(two)

    part2, part3, mixed23, probs23, k23, v23, msg23 = attend(1)
    part0, part1, mixed01, probs01, k01, v01, msg01 = attend(0)
    branch_parts = own_sum(part0, part1, part2, part3)

    def residual_kernel(info_ref, a, b, c, x, vrow, gain, shift, resid_o, low_o):
        summed = a[...].astype(F32) + b[...].astype(F32) + c[...].astype(F32)
        resid = x[0].astype(F32) + summed + vrow[2:3]
        resid_o[...] = resid
        normed, _ = norm_parts(resid)
        low_o[...] = (normed * gain[...] + shift[...]).astype(BF16)

    resid_own, low_own = run(
        residual_kernel, info,
        [*branch_parts, (x_slots, (1, rows, model), (0, 0, 0)), vec, gain_two, shift_two],
        [shape_of((rows, model), F32), shape_of((rows, model), BF16)],
    )
    low_two = spread(low_own)

    def feed_kernel(info_ref, low_a, low_b, gh, w, bias, hid_o, pre_o, ga_o, gb_o):
        for j in (1, 0):
            hidden_in = nn((low_a, low_b)[j][...], w[...]) + bias[...]
            sig = 1.0 / (1.0 + jnp.exp(-QUICK_GELU * hidden_in))
            hid_o[j] = (hidden_in * sig).astype(BF16)
            slope = sig + QUICK_GELU * hidden_in * sig * (1.0 - sig)
            pre = (gh[j].astype(F32) * slope).astype(BF16)
            pre_o[j] = pre
            (ga_o, gb_o)[j][...] = nt(pre, w[...]).astype(BF16)

    def feed(pair):
        return run(
            feed_kernel, info,
            [
                low_two[2 * pair], low_two[2 * pair + 1],
                (g_hidden, (2, rows, hidden_width), (pair, 0, 0)),
                fc_in, fc_in_bias_row,
            ],
            [
                shape_of((2, rows, hidden_width), BF16),
                shape_of((2, rows, hidden_width), BF16),
                shape_of((rows, model), BF16),
                shape_of((rows, model), BF16),
            ],
            flops=2 * 4 * rows * model * hidden_width,
        )

    hid01, pre01, gl0, gl1 = feed(0)
    hid23, pre23, gl2, gl3 = feed(1)
    low_parts = own_sum(gl0, gl1, gl2, gl3)

    def residual_back_kernel(info_ref, a, b, c, resid, g, gain, grad_o, low_o, small_o):
        incoming = a[...].astype(F32) + b[...].astype(F32) + c[...].astype(F32)
        normed, inverse = norm_parts(resid[...])
        real = lax.broadcasted_iota(jnp.int32, (rows, model), 0) < patch
        incoming = jnp.where(real, incoming, 0.0)
        grad = g[0].astype(F32) + norm_back(incoming, normed, inverse, gain[...])
        grad = jnp.where(real, grad, 0.0)
        grad_o[...] = grad
        low = grad.astype(BF16)
        low_o[...] = low
        small_o[...] = jnp.zeros_like(small_o)
        small_o[0:1, :] = row_sum(incoming * normed)
        small_o[1:2, :] = row_sum(incoming)
        small_o[2:3, :] = row_sum(low.astype(F32))
        small_o[3:4, :] = row_sum(g[0].astype(F32))

    grad_resid, grad_low, small_two = run(
        residual_back_kernel, info,
        [*low_parts, resid_own, (g_slots, (1, rows, model), (0, 0, 0)), gain_two],
        [shape_of((rows, model), F32), shape_of((rows, model), BF16), shape_of((8, model), F32)],
    )
    branch = spread(grad_low)

    quarter = hidden_width // 4
    assert quarter == width

    def chunks_out(acc, info_ref, outs):
        def chunk(r):
            start = pl.multiple_of(((info_ref[2] + r) & 3) * quarter, quarter)
            return acc[pl.ds(start, quarter), :].astype(BF16)

        m0, m1, m2t, m2b, m3 = outs
        m0[...] = chunk(0)
        m1[...] = chunk(1)
        m2 = chunk(2)
        m2t[...] = m2[: quarter // 2]
        m2b[...] = m2[quarter // 2 :]
        m3[...] = chunk(3)

    chunk_shapes = [
        shape_of((quarter, model), BF16),
        shape_of((quarter, model), BF16),
        shape_of((quarter // 2, model), BF16),
        shape_of((quarter // 2, model), BF16),
        shape_of((quarter, model), BF16),
    ]

    def fc_out_kernel(info_ref, ha, hb, g, *outs):
        acc = outs[-1]
        pair_rows = 2 * rows
        acc[...] = tn(ha[...].reshape(pair_rows, hidden_width), g[0:2].reshape(pair_rows, model))
        acc[...] += tn(hb[...].reshape(pair_rows, hidden_width), g[2:4].reshape(pair_rows, model))
        chunks_out(acc, info_ref, outs[:-1])

    fc_out_chunks = run(
        fc_out_kernel, info, [hid01, hid23, g_slots], chunk_shapes,
        [pltpu.VMEM((hidden_width, model), F32)],
        flops=2 * half * rows * model * hidden_width,
    )

    def fc_in_kernel(info_ref, pa, pb, l0, l1, l2, l3, m0, m1, m2t, m2b, m3, bias_o, acc):
        acc[...] = tn(pa[0], l0[...])
        acc[...] += tn(pa[1], l1[...])
        acc[...] += tn(pb[0], l2[...])
        acc[...] += tn(pb[1], l3[...])
        chunks_out(acc, info_ref, (m0, m1, m2t, m2b, m3))
        total = row_sum(pa[0].astype(F32)) + row_sum(pa[1].astype(F32))
        bias_o[...] = total + row_sum(pb[0].astype(F32)) + row_sum(pb[1].astype(F32))

    def fc_in_natural_kernel(info_ref, pa, pb, l0, l1, l2, l3, m0, m1, m2t, m2b, m3, bias_o, acc):
        acc[...] = tn(l0[...], pa[0])
        acc[...] += tn(l1[...], pa[1])
        acc[...] += tn(l2[...], pb[0])
        acc[...] += tn(l3[...], pb[1])
        chunks_out(acc, info_ref, (m0, m1, m2t, m2b, m3))
        total = row_sum(pa[0].astype(F32)) + row_sum(pa[1].astype(F32))
        bias_o[...] = total + row_sum(pb[0].astype(F32)) + row_sum(pb[1].astype(F32))

    *fc_in_chunks, fc_in_bias_part = run(
        fc_in_natural_kernel, info, [pre01, pre23, *low_two],
        [*chunk_shapes, shape_of((1, hidden_width), F32)],
        [pltpu.VMEM((model, hidden_width), F32)],
        flops=2 * half * rows * model * hidden_width,
    )

    def column_out(values_in, slot, info_ref, keep_o, send_o):
        ten = info_ref[1]
        place = (ten ^ slot) & 1
        for i in range(4):
            block = values_in[:, i * width : (i + 1) * width]
            apart = ten ^ i

            @pl.when((apart & 1) == 0)
            def _():
                keep_o[apart >> 1, place] = block

            @pl.when((apart & 1) == 1)
            def _():
                send_o[apart >> 1, place] = block

    column_shapes = [shape_of((2, 2, rows, width), BF16)] * 2

    def mlp_kernel(info_ref, ha, hb, w, resid, bias, keep01, send01, keep23, send23):
        for s in range(half):
            out = nn((ha, hb)[s // 2][s % 2], w[...])
            if s == 0:
                out = out + resid[...] + bias[...]
            keep_o, send_o = ((keep01, send01), (keep23, send23))[s // 2]
            column_out(out.astype(BF16), s, info_ref, keep_o, send_o)

    block_columns = run(
        mlp_kernel, info, [hid01, hid23, fc_out, resid_own, fc_out_bias_row], column_shapes * 2,
        flops=2 * half * rows * model * hidden_width,
    )

    def column_sum(keep01, send01, keep23, send23):
        got01 = core_swap(send01)
        got23 = core_swap(send23)
        far23 = x_swap(keep01[1] + got01[1])
        far01 = x_swap(keep23[1] + got23[1])
        return keep01, got01, far01, keep23, got23, far23

    def frames_of(refs, info_ref):
        keep01, got01, far01, keep23, got23, far23 = refs
        low_pair = info_ref[1] >> 1
        for i in range(2):
            for pair, keep, got, far in (
                (low_pair, keep01, got01, far01),
                (low_pair ^ 1, keep23, got23, far23),
            ):
                total = keep[0, i].astype(F32) + got[0, i].astype(F32) + far[i].astype(F32)
                yield pair * 2 + i, total[:patch]

    def column_ins(arrays):
        keep01, got01, far01, keep23, got23, far23 = arrays
        first_of = (1, 2, rows, width), (0, 0, 0, 0)
        return [
            (keep01, *first_of), (got01, *first_of), far01,
            (keep23, *first_of), (got23, *first_of), far23,
        ]

    def block_out_kernel(info_ref, *refs):
        out = refs[-1]
        for place, total in frames_of(refs[:-1], info_ref):
            out[place] = total.astype(BF16)

    (block_out,) = run(
        block_out_kernel, info, column_ins(column_sum(*block_columns)),
        [shape_of((half, patch, width), BF16)],
    )

    def attend_back_kernel(
        base, info_ref, ba, bb, q, k, v, probs, x, msg, w, vrow, wo, extra,
        keep_o, send_o, grads_o, low_o, small_o,
    ):
        ten = info_ref[1]
        masks = head_masks(rows)
        here = lax.broadcasted_iota(jnp.int32, (rows, model), 0) == patch
        gain, shift = vrow[0:1], vrow[1:2]
        small_o[...] = jnp.zeros_like(small_o)
        for j in range(2):
            grad_mixed = nt((ba, bb)[j][...], wo[...]).astype(BF16)
            dq = jnp.zeros((rows, width), F32)
            dk = jnp.zeros((rows, width), F32)
            dv = jnp.zeros((rows, width), F32)
            for h in range(heads):
                grad_head = only(masks[h], grad_mixed)
                low_probs = probs[j, h]
                wide = low_probs.astype(F32)
                dv = dv + tn(low_probs, grad_head)
                grad_probs = nt(grad_head, v[j])
                inner = jnp.sum(wide * grad_probs, axis=-1, keepdims=True)
                grad_scores = (wide * (grad_probs - inner)).astype(BF16)
                dq = dq + only(masks[h], nn(grad_scores, k[j]))
                dk = dk + tn(grad_scores, only(masks[h], q[j]))
            dq = (dq * scale).astype(BF16)
            dk = (dk * scale).astype(BF16)
            dv = dv.astype(BF16)
            grads_o[0, j] = dq
            grads_o[1, j] = dk
            grads_o[2, j] = dv
            grad_low = nn(dq, w[0]) + nn(dk, w[1]) + nn(dv, w[2])
            token = jnp.where(here, msg[j : j + 1], x[j].astype(F32))
            normed, inverse = norm_parts(token)
            low_o[j] = (normed * gain + shift).astype(BF16)
            back = norm_back(grad_low, normed, inverse, gain)
            small_o[pl.ds(ten ^ (base + j), 1), :] = row_sum(only(here, back))
            small_o[4:5, :] += row_sum(grad_low * normed)
            small_o[5:6, :] += row_sum(grad_low)
            small_o[6:7, 0:width] += row_sum(dq.astype(F32))
            small_o[6:7, 256 : 256 + width] += row_sum(dv.astype(F32))
            if base + j == 0:
                back = back + extra[...]
            column_out(back.astype(BF16), base + j, info_ref, keep_o, send_o)

    def attend_back(pair, k, v, probs, msg):
        return run(
            functools.partial(attend_back_kernel, 2 * pair),
            info,
            [
                branch[2 * pair], branch[2 * pair + 1],
                (q_one, (2, rows, width), (pair, 0, 0)),
                k, v, probs,
                (x_slots, (2, rows, model), (pair, 0, 0)),
                msg, w_in, vec, w_out, grad_resid,
            ],
            [
                *column_shapes,
                shape_of((3, 2, rows, width), BF16),
                shape_of((2, rows, model), BF16),
                shape_of((8, model), F32),
            ],
            flops=2 * 2 * rows * (4 * width * model + 4 * heads * rows * HEAD_DIM),
        )

    keep01, send01, grads01, low01, small01 = attend_back(0, k01, v01, probs01, msg01)
    keep23, send23, grads23, low23, small23 = attend_back(1, k23, v23, probs23, msg23)
    grad_columns = column_sum(keep01, send01, keep23, send23)

    def attend_weight_kernel(info_ref, ga, gb, la, lb, ma, mb, b0, b1, b2, b3, *outs):
        acc = outs[-1]
        pair_rows = 2 * rows
        low_a = la[...].reshape(pair_rows, model)
        low_b = lb[...].reshape(pair_rows, model)
        for c in range(3):
            acc[c * width : (c + 1) * width, :] = tn(
                ga[c].reshape(pair_rows, width), low_a
            ) + tn(gb[c].reshape(pair_rows, width), low_b)
        acc[3 * width :, :] = (
            tn(ma[0], b0[...]) + tn(ma[1], b1[...]) + tn(mb[0], b2[...]) + tn(mb[1], b3[...])
        )
        chunks_out(acc, info_ref, outs[:-1])

    attend_chunks = run(
        attend_weight_kernel, info,
        [grads01, grads23, low01, low23, mixed01, mixed23, *branch], chunk_shapes,
        [pltpu.VMEM((4 * width, model), F32)],
        flops=2 * half * rows * model * 4 * width,
    )

    def add(*terms):
        return sum(term.astype(F32) for term in terms).astype(BF16)

    def reduce_chunks(m0, m1, m2t, m2b, m3):
        if not ring:
            sizes = [m.shape[0] for m in (m0, m1, m2t, m2b, m3)]
            total = lax.psum(jnp.concatenate([m0, m1, m2t, m2b, m3]), ("pipe", "dp"))
            places = [sum(sizes[:i]) for i in range(6)]
            return [total[a:b] for a, b in zip(places[:-1], places[1:])]
        part = quarter // 2
        up, down = z_up(m2t), z_down(m2b)
        m1 = jnp.concatenate([add(m1[:part], up), m1[part:]])
        m3 = jnp.concatenate([m3[:part], add(m3[part:], down)])
        mine = add(m0, z_up(m1), z_down(m3))
        total = add(mine, y_swap(mine))
        before, after = z_up(total), z_down(total)
        return [total, after, z_up(before[:part]), z_down(after[part:]), before]

    def whole_kernel(info_ref, c0, c1, c2t, c2b, c3, out):
        def put(r, block, shift=0):
            start = pl.multiple_of(((info_ref[2] + r) & 3) * quarter + shift, quarter // 2)
            out[pl.ds(start, block.shape[0]), :] = block.astype(F32)

        put(0, c0[...])
        put(1, c1[...])
        put(2, c2t[...])
        put(2, c2b[...], quarter // 2)
        put(3, c3[...])

    def whole(chunks):
        return run(whole_kernel, info, chunks, [shape_of((4 * quarter, model), F32)])[0]

    fc_out_grad = whole(reduce_chunks(*fc_out_chunks))
    fc_in_grad = whole(reduce_chunks(*fc_in_chunks))
    attend_grad = reduce_chunks(*attend_chunks)

    def spot(row, at, size):
        return jnp.where(jnp.arange(size)[:, None] == at, row, 0.0)

    small = small01 + small23
    pack = jnp.concatenate(
        [
            small[:6],
            small_two[:4],
            spot(fc_in_bias_part, tensor, 4),
            spot(small[6:7], tensor, 4),
            jnp.zeros((6, model), F32),
        ]
    ).astype(BF16)
    pack = add(pack, core_swap(pack))
    pack = add(pack, x_swap(pack))
    other = y_swap(pack)
    early = jnp.where(first_section, pack[:half], other[:half])
    later = jnp.where(first_section, other[:half], pack[:half])
    pack = jnp.concatenate([early, later, add(pack[half:], other[half:])])
    packs = gather_clips(pack)

    pack_rows = pack.shape[0]

    def gather_sent(packs_ref):
        return jnp.concatenate(
            [packs_ref[c, 0:frame_count, :].astype(F32) for c in range(clips)], axis=0
        )

    def message_back(
        info_ref, packs_ref, first, q, k, v, probs, w, wo, gain,
        sent_o, grads_o, back_o,
    ):
        sent = gather_sent(packs_ref)
        low = sent.astype(BF16)
        sent_o[...] = sent
        grad_mixed = nt(low, wo[...]).astype(BF16)
        dq = jnp.zeros((all_rows, width), F32)
        dk = jnp.zeros((all_rows, width), F32)
        dv = jnp.zeros((all_rows, width), F32)
        for h, mask in enumerate(head_masks(all_rows)):
            grad_head = only(mask, grad_mixed)
            wide = probs[h]
            dv = dv + tn(wide.astype(BF16), grad_head)
            grad_probs = nt(grad_head, v[...])
            inner = jnp.sum(wide * grad_probs, axis=-1, keepdims=True)
            grad_scores = (wide * (grad_probs - inner)).astype(BF16)
            dq = dq + only(mask, nn(grad_scores, k[...]))
            dk = dk + tn(grad_scores, only(mask, q[...]))
        dq = (dq * scale).astype(BF16)
        dk = (dk * scale).astype(BF16)
        dv = dv.astype(BF16)
        grads_o[0] = dq
        grads_o[1] = dk
        grads_o[2] = dv
        grad_low = nn(dq, w[0]) + nn(dk, w[1]) + nn(dv, w[2])
        normed, inverse = norm_parts(first[...])
        back = norm_back(grad_low, normed, inverse, gain[...])
        back_o[0:all_rows, :] = back.astype(BF16)
        tail = jnp.concatenate(
            [
                row_sum(grad_low * normed),
                row_sum(grad_low),
                jnp.zeros((14, model), F32),
            ],
            axis=0,
        )
        back_o[all_rows:, :] = tail.astype(BF16)

    sent_all, grads_zero, back_zero = run(
        message_back, info,
        [packs, first_msg, q_zero, k_zero, v_zero, probs_zero, own_in, own_out, norm_gain],
        [
            shape_of((all_rows, model), F32),
            shape_of((3, all_rows, width), BF16),
            shape_of((all_rows + 16, model), BF16),
        ],
    )
    back_zero = add(back_zero, core_swap(back_zero))
    back_zero = add(back_zero, x_swap(back_zero))
    back_late = y_late(back_zero)

    def message_weight(info_ref, sent, grads, low, mixed, in_o, out_o, qv_o, bias_o):
        for c in range(3):
            in_o[c] = tn(grads[c], low[...])
        out_o[...] = tn(mixed[...], sent[...].astype(BF16))
        qv_o[0:1, :] = row_sum(grads[0].astype(F32))
        qv_o[1:2, :] = row_sum(grads[2].astype(F32))
        bias_o[...] = row_sum(sent[...])

    in_zero, out_zero, qv_zero, bias_zero = run(
        message_weight, info, [sent_all, grads_zero, low_zero, mixed_zero],
        [
            shape_of((3, width, model), F32),
            shape_of((width, model), F32),
            shape_of((2, width), F32),
            shape_of((1, model), F32),
        ],
    )

    def attend_whole_kernel(info_ref, c0, c1, c2t, c2b, c3, in_zero, out_zero, in_o, out_o, acc):
        @pl.when(info_ref[0] == 0)
        def _():
            in_o[...] = in_zero[...]
            out_o[...] = out_zero[...]

        @pl.when(info_ref[0] == 1)
        def _():
            whole_kernel(info_ref, c0, c1, c2t, c2b, c3, acc)
            for c in range(3):
                in_o[c] = acc[c * width : (c + 1) * width, :]
            out_o[...] = acc[3 * width :, :]

    attn_in_grad, attn_out_grad = run(
        attend_whole_kernel, info, [*attend_grad, in_zero, out_zero],
        [shape_of((3, width, model), F32), shape_of((width, model), F32)],
        [pltpu.VMEM((4 * width, model), F32)],
    )

    def message_end(
        info_ref, sent, own, late, cls, mw, packs_ref, qv_in, bias_in,
        w_o, cls_o, vec_o, qv_o, acc, sums,
    ):
        sec, ten = info_ref[0], info_ref[1]
        total = jnp.where(sec == 0, own[...].astype(F32), late[...].astype(F32))
        grad_first = sent[...] + total[:all_rows]
        high = grad_first.astype(BF16)
        rest = (grad_first - high.astype(F32)).astype(BF16)
        at = pl.multiple_of(ten * width, width)
        acc[...] = tn(high, cls[...]) + tn(rest, cls[...])
        w_o[...] = acc[pl.ds(at, width), :]
        mw_rows = mw[pl.ds(at, width), :]
        cls_o[...] = nt(high[:16], mw_rows) + nt(rest[:16], mw_rows)
        small = packs_ref[0, frame_count:, :].astype(F32)
        for c in range(1, clips):
            small = small + packs_ref[c, frame_count:, :].astype(F32)
        sums[...] = small
        first_one = sec == 0
        vec_o[...] = jnp.zeros_like(vec_o)
        vec_o[0:1, :] = jnp.where(first_one, total[all_rows : all_rows + 1], sums[0:1])
        vec_o[1:2, :] = jnp.where(first_one, total[all_rows + 1 : all_rows + 2], sums[1:2])
        vec_o[2:3, :] = jnp.where(first_one, bias_in[...], sums[4:5])
        vec_o[3:4, :] = sums[2:3]
        vec_o[4:5, :] = sums[3:4]
        vec_o[5:6, :] = sums[5:6]
        vec_o[6:7, :] = sums[pl.ds(6 + ten, 1), :]
        vec_o[7:8, :] = row_sum(grad_first)
        qv_row = sums[pl.ds(10 + ten, 1), :]
        qv_o[0:1, :] = jnp.where(first_one, qv_in[0:1], qv_row[:, :width])
        qv_o[1:2, :] = jnp.where(first_one, qv_in[1:2], qv_row[:, 256 : 256 + width])

    small_rows = pack_rows - frame_count
    msg_w_grad, cls_part, vec_grads, qv_grad = run(
        message_end, info,
        [sent_all, back_zero, back_late, cls_all, msg_w, packs, qv_zero, bias_zero],
        [
            shape_of((width, model), F32),
            shape_of((16, width), F32),
            shape_of((8, model), F32),
            shape_of((2, width), F32),
        ],
        [pltpu.VMEM((model, model), F32), pltpu.VMEM((small_rows, model), F32)],
    )

    def frames_grad_kernel(info_ref, *refs):
        cls, out = refs[-2:]
        top = lax.broadcasted_iota(jnp.int32, (patch, width), 0) == 0
        for place, total in frames_of(refs[:-2], info_ref):
            row = cls[pl.ds(info_ref[0] * half + place, 1), :]
            out[place] = (total + jnp.where(top, row, 0.0)).astype(BF16)

    (frames_grad,) = run(
        frames_grad_kernel, info, [*column_ins(grad_columns), cls_part],
        [shape_of((half, patch, width), BF16)],
    )

    return (
        block_out[None],
        frames_grad[None],
        msg_w_grad.T,
        vec_grads[7],
        vec_grads[0:1],
        vec_grads[1:2],
        jnp.transpose(attn_in_grad, (2, 0, 1))[None],
        qv_grad[None],
        attn_out_grad[None],
        vec_grads[2:3],
        vec_grads[3],
        vec_grads[4],
        fc_in_grad,
        vec_grads[6],
        fc_out_grad,
        vec_grads[5],
    )


def solution(mesh):
    return jax.shard_map(
        body,
        mesh=mesh,
        in_specs=(
            P("dp", None, None, None),
            P(),
            P(),
            P(),
            P("pipe", None),
            P("pipe", None),
            P("pipe", None, None, "tensor"),
            P("pipe", None, "tensor"),
            P("pipe", "tensor", None),
            P("pipe", None),
            P(),
            P(),
            P(None, "tensor"),
            P("tensor"),
            P("tensor", None),
            P(),
            P("dp", None, None, None),
        ),
        out_specs=(
            P("dp", "pipe", None, "tensor"),
            P("dp", "pipe", None, "tensor"),
            P(None, "tensor"),
            P(),
            P("pipe", None),
            P("pipe", None),
            P("pipe", None, None, "tensor"),
            P("pipe", None, "tensor"),
            P("pipe", "tensor", None),
            P("pipe", None),
            P(),
            P(),
            P(None, "tensor"),
            P("tensor"),
            P("tensor", None),
            P(),
        ),
        check_vma=False,
    )
```

```python
import functools

import jax
import jax.numpy as jnp
from jax import lax
from jax.experimental import pallas as pl
from jax.experimental.pallas import tpu as pltpu
from jax.sharding import PartitionSpec as P

HEAD_DIM = 64
EPSILON = 1e-05
QUICK_GELU = 1.702
F32 = jnp.float32
BF16 = jnp.bfloat16
VMEM_BYTES = 16 * 1024 * 1024


def nn(left, right):
    return lax.dot_general(left, right, (((1,), (0,)), ((), ())), preferred_element_type=F32)


def nt(left, right):
    return lax.dot_general(left, right, (((1,), (1,)), ((), ())), preferred_element_type=F32)


def tn(left, right):
    return lax.dot_general(left, right, (((0,), (0,)), ((), ())), preferred_element_type=F32)


def norm_parts(values_in):
    centred = values_in - jnp.mean(values_in, axis=-1, keepdims=True)
    inverse = lax.rsqrt(jnp.mean(centred * centred, axis=-1, keepdims=True) + EPSILON)
    return centred * inverse, inverse


def norm_back(incoming, normed, inverse, gain):
    weighted = incoming * gain
    centred = weighted - jnp.mean(weighted, axis=-1, keepdims=True)
    return inverse * (centred - normed * jnp.mean(weighted * normed, axis=-1, keepdims=True))


def row_sum(values_in):
    return jnp.sum(values_in, axis=0, keepdims=True)


def shape_of(shape, kind):
    return jax.ShapeDtypeStruct(shape, kind)


def near(shape, kind):
    return pltpu.VMEM(shape, kind)


class Chain:
    def __init__(self):
        self.token = None
        self.near, self.kept = set(), []

    def __call__(self, kernel, ins, outs, scratch=(), flops=0, scalars=()):
        lead, tokens = len(scalars), 0 if self.token is None else 1
        count, given = len(ins), len(outs)

        def stage(*refs):
            rest = refs[lead + tokens :]
            kernel(*refs[:lead], *rest[:count], *rest[count : count + given], *rest[count + given + 1 :])

        vmem = pl.BlockSpec(memory_space=pltpu.VMEM)
        moved = sum(a.size * a.dtype.itemsize for a in ins)
        held = [] if self.token is None else [self.token]
        ins = [
            pltpu.with_memory_space_constraint(a, pltpu.VMEM) if id(a) in self.near else a for a in ins
        ]
        results = pl.pallas_call(
            stage,
            out_shape=[*outs, near((8, 128), F32)],
            in_specs=[pl.BlockSpec(memory_space=pltpu.SMEM)] * lead
            + [pl.BlockSpec(memory_space=pl.ANY)] * tokens
            + [vmem] * count,
            out_specs=[vmem] * (given + 1),
            scratch_shapes=list(scratch),
            compiler_params=pltpu.CompilerParams(vmem_limit_bytes=VMEM_BYTES),
            cost_estimate=pl.CostEstimate(flops=flops, bytes_accessed=moved, transcendentals=0),
        )(*scalars, *held, *ins)
        self.token = results[-1]
        self.kept += results
        for out, result in zip(outs, results):
            if not isinstance(out, jax.ShapeDtypeStruct):
                self.near.add(id(result))
        return results[:-1]


def body(
    frames,
    video_group,
    msg_w,
    msg_bias,
    norm_gain,
    norm_shift,
    attn_in,
    qv_bias,
    attn_out,
    out_bias,
    norm2_gain,
    norm2_shift,
    fc_in,
    fc_in_bias,
    fc_out,
    fc_out_bias,
    cotangent,
):
    _, frame_count, patch, model = frames.shape
    width = attn_in.shape[-1]
    hidden_width = fc_in.shape[-1]
    heads = width // HEAD_DIM
    clips = lax.axis_size("dp")
    half = frame_count // 2
    rows = -(-(patch + 1) // 16) * 16
    all_rows = clips * frame_count
    scale = HEAD_DIM ** (-0.5)
    pipe = lax.axis_index("pipe")
    tensor = lax.axis_index("tensor")
    clip = lax.axis_index("dp")
    ring = clips == 4
    stage = Chain()
    quarter = hidden_width // 4
    assert quarter == width and hidden_width == model and half == 4

    def tensor_swap(v, bit):
        return lax.ppermute(v, "tensor", [(i, i ^ bit) for i in range(4)])

    def core_swap(v):
        return tensor_swap(v, 1)

    def x_swap(v):
        return tensor_swap(v, 2)

    def y_swap(v):
        return lax.ppermute(v, "pipe", [(0, 1), (1, 0)])

    def y_late(v):
        return lax.ppermute(v, "pipe", [(0, 1)])

    def y_early(v):
        return lax.ppermute(v, "pipe", [(1, 0)])

    def z_swap(v, bit):
        return lax.ppermute(v, "dp", [(i, i ^ bit) for i in range(clips)])

    def gather_clips(v):
        if ring:
            return [v] + [z_swap(v, apart) for apart in range(1, clips)]
        every = lax.all_gather(v, "dp")
        every = lax.dynamic_slice_in_dim(jnp.concatenate([every, every]), clip, clips, 0)
        return [every.reshape(clips * v.shape[0], v.shape[1])]

    def clip_block(refs, c, size):
        if len(refs) == clips:
            return refs[c][...]
        return refs[0][c * size : (c + 1) * size, :]

    blocks = clips if ring else 1

    def head_masks(n):
        lane = lax.broadcasted_iota(jnp.int32, (n, width), 1)
        return [(lane >= h * HEAD_DIM) & (lane < (h + 1) * HEAD_DIM) for h in range(heads)]

    def only(mask, v):
        return jnp.where(mask, v, jnp.zeros_like(v))

    def add(*terms):
        total = terms[0].astype(F32)
        for term in terms[1:]:
            total = total + term.astype(F32)
        return total

    def adds(*groups):
        sizes = [len(group) for group in groups]

        def kernel(*refs):
            at = 0
            for size, out in zip(sizes, refs[sum(sizes) :]):
                out[...] = add(*[ref[...] for ref in refs[at : at + size]]).astype(out.dtype)
                at += size

        return stage(
            kernel,
            [array for group in groups for array in group],
            [near(group[0].shape, group[0].dtype) for group in groups],
        )

    own_in = jnp.transpose(attn_in[0], (1, 2, 0))
    own_out = attn_out[0]
    sent_in = y_early(own_in)
    cls_rows = frames[0, :, 0, :]
    cls_all = gather_clips(cls_rows)

    def vector_kernel(mb, g2, s2, fi, fo, gain, shift, ob, qv, vecs_o, own_o):
        for i, ref in enumerate((mb, g2, s2, fi, fo)):
            vecs_o[i : i + 1, :] = ref[...].reshape(1, model)
        for i, ref in enumerate((gain, shift, ob)):
            own_o[i : i + 1, :] = ref[...]
        own_o[3:8, :] = jnp.zeros((5, model), F32)
        own_o[3:5, 0:width] = qv[...]

    vectors, own_vec = stage(
        vector_kernel,
        [
            msg_bias, norm2_gain, norm2_shift, fc_in_bias, fc_out_bias,
            norm_gain, norm_shift, out_bias, qv_bias[0],
        ],
        [near((8, model), F32)] * 2,
    )
    sent_vec = y_early(own_vec)
    sent_out = y_early(own_out)

    tokens_all = rows * frame_count
    lanes = 128

    def slot_kernel(v, *refs):
        wide = refs[-1]
        flat = v[...].astype(F32).reshape(patch * frame_count, model)
        for c in range(model // lanes):
            at = c * tokens_all
            wide[at : at + patch * frame_count, :] = flat[:, c * lanes : (c + 1) * lanes]
            wide[at + patch * frame_count : at + tokens_all, :] = jnp.zeros(
                ((rows - patch) * frame_count, lanes), F32
            )
            for s in range(half):
                frame = at + lax.axis_index("pipe") * half + (lax.axis_index("tensor") ^ s)
                refs[s][:, c * lanes : (c + 1) * lanes] = wide[
                    pl.ds(frame, rows, stride=frame_count), :
                ].astype(BF16)

    def slots(v):
        return stage(
            slot_kernel,
            [jnp.transpose(v[0], (1, 0, 2))],
            [near((rows, model), BF16)] * half,
            [pltpu.VMEM((model // lanes * tokens_all, lanes), F32)],
        )

    x_slots = slots(frames)

    def message_forward(ids, *refs):
        cls_refs, refs = refs[:blocks], refs[blocks:]
        (mw, vecs, vrow, w, wo, first_o, low_o, q_o, k_o, v_o, probs_o, mixed_o, part_o) = refs
        cls = jnp.concatenate([clip_block(cls_refs, c, frame_count).astype(F32) for c in range(clips)])
        first = nn(cls.astype(BF16), mw[...]) + vecs[0:1]
        first_o[...] = first
        normed, _ = norm_parts(first)
        low = (normed * vrow[0:1] + vrow[1:2]).astype(BF16)
        low_o[...] = low
        q = (nt(low, w[0]) + vrow[3:4, :width]).astype(BF16)
        k = nt(low, w[1]).astype(BF16)
        v = (nt(low, w[2]) + vrow[4:5, :width]).astype(BF16)
        q_o[...] = q
        k_o[...] = k
        v_o[...] = v
        of_row = lax.broadcasted_iota(jnp.int32, (all_rows, all_rows), 0) // frame_count
        of_col = lax.broadcasted_iota(jnp.int32, (all_rows, all_rows), 1) // frame_count
        mine = lax.axis_index("dp")
        row_id = jnp.zeros((all_rows, all_rows), jnp.int32)
        col_id = jnp.zeros((all_rows, all_rows), jnp.int32)
        for c in range(clips):
            mark = ids[mine ^ c if ring else lax.rem(mine + c, clips)]
            row_id = jnp.where(of_row == c, mark, row_id)
            col_id = jnp.where(of_col == c, mark, col_id)
        allowed = row_id == col_id
        mixed = jnp.zeros((all_rows, width), F32)
        for h, mask in enumerate(head_masks(all_rows)):
            scores = jnp.where(allowed, nt(only(mask, q), k) * scale, -jnp.inf)
            exponent = jnp.exp(scores - jnp.max(scores, axis=-1, keepdims=True))
            probs = exponent / jnp.sum(exponent, axis=-1, keepdims=True)
            probs_o[h] = probs
            mixed = mixed + only(mask, nn(probs.astype(BF16), v))
        mixed = mixed.astype(BF16)
        mixed_o[...] = mixed
        part = nn(mixed, wo[...]) + jnp.where(lax.axis_index("tensor") == 0, vrow[2:3], 0.0)
        part_o[...] = part[:frame_count]

    (first_msg, low_zero, q_zero, k_zero, v_zero, probs_zero, mixed_zero, part_zero) = stage(
        message_forward,
        [*cls_all, msg_w, vectors, own_vec, own_in, own_out],
        [
            near((all_rows, model), F32),
            near((all_rows, model), BF16),
            near((all_rows, width), BF16),
            near((all_rows, width), BF16),
            near((all_rows, width), BF16),
            near((heads, all_rows, all_rows), F32),
            near((all_rows, width), BF16),
            near((frame_count, model), F32),
        ],
        scalars=[video_group],
    )
    (part_zero,) = adds((part_zero, core_swap(part_zero)))
    from_x = x_swap(part_zero)

    def project_kernel(x0, x1, x2, x3, wa, wb, va, vb, w, vrow, *outs):
        early = lax.axis_index("pipe") == 0
        for c in range(3):
            w[c] = jnp.where(early, wb[c], wa[c])
        vrow[...] = jnp.where(early, vb[...], va[...])
        gain, shift = vrow[0:1], vrow[1:2]
        for s, x in enumerate((x0, x1, x2, x3)):
            normed, _ = norm_parts(x[...].astype(F32))
            low = (normed * gain + shift).astype(BF16)
            outs[s][...] = (nt(low, w[0]) + vrow[3:4, :width]).astype(BF16)
            outs[half + s][...] = nt(low, w[1]).astype(BF16)
            outs[2 * half + s][...] = (nt(low, w[2]) + vrow[4:5, :width]).astype(BF16)

    w_in, vec, *projected = stage(
        project_kernel, [*x_slots, own_in, sent_in, own_vec, sent_vec],
        [near(own_in.shape, BF16), near(own_vec.shape, F32)] + [near((rows, width), BF16)] * 12,
        flops=2 * half * rows * model * 3 * width,
    )
    q_one, k_patch, v_patch = projected[:4], projected[4:8], projected[8:]
    (part_zero,) = adds((part_zero, from_x))
    part_late = y_late(part_zero)

    def message_rows_kernel(first, part, late, w, vrow, wa, wb, msg_o, k_o, v_o, w_o):
        sec, ten = lax.axis_index("pipe"), lax.axis_index("tensor")
        w_o[...] = jnp.where(sec == 0, wb[...], wa[...])
        msg_o[...] = jnp.zeros_like(msg_o)
        for s in range(half):
            at = pl.ds(sec * half + (ten ^ s), 1)
            summed = jnp.where(sec == 0, part[at, :], late[at, :])
            msg_o[s : s + 1, :] = (first[at, :] + summed).astype(BF16).astype(F32)
        normed, _ = norm_parts(msg_o[...])
        low = (normed * vrow[0:1] + vrow[1:2]).astype(BF16)
        k_o[...] = nt(low, w[1])
        v_o[...] = nt(low, w[2]) + vrow[4:5, :width]

    msg_rows, k_msg, v_msg, w_out = stage(
        message_rows_kernel,
        [first_msg, part_zero, part_late, w_in, vec, own_out, sent_out],
        [
            near((16, model), F32), near((16, width), F32), near((16, width), F32),
            near(own_out.shape, BF16),
        ],
    )

    def attend_kernel(
        s, q, k, v, km, vm, wo, part_o, mixed_o, probs_o, k_o, v_o,
    ):
        here = lax.broadcasted_iota(jnp.int32, (rows, width), 0) == patch
        key_here = lax.broadcasted_iota(jnp.int32, (rows, rows), 1) <= patch
        kk = jnp.where(here, km[s : s + 1], k[...].astype(F32)).astype(BF16)
        vv = jnp.where(here, vm[s : s + 1], v[...].astype(F32)).astype(BF16)
        k_o[...] = kk
        v_o[...] = vv
        mixed = jnp.zeros((rows, width), F32)
        for h, mask in enumerate(head_masks(rows)):
            scores = nt(only(mask, q[...]), kk) * scale
            scores = jnp.where(key_here, scores, -jnp.inf)
            exponent = jnp.exp(scores - jnp.max(scores, axis=-1, keepdims=True))
            probs = exponent * (1.0 / jnp.sum(exponent, axis=-1, keepdims=True))
            probs = probs.astype(BF16)
            probs_o[h] = probs
            mixed = mixed + only(mask, nn(probs, vv))
        mixed = mixed.astype(BF16)
        mixed_o[...] = mixed
        part_o[...] = nn(mixed, wo[...]).astype(BF16)

    def attend(s):
        return stage(
            functools.partial(attend_kernel, s),
            [q_one[s], k_patch[s], v_patch[s], k_msg, v_msg, w_out],
            [
                near((rows, model), BF16),
                near((rows, width), BF16),
                near((heads, rows, rows), BF16),
                near((rows, width), BF16),
                near((rows, width), BF16),
            ],
            flops=2 * rows * (width * model + 2 * heads * rows * HEAD_DIM),
        )

    attended = [None] * half
    attended[3] = attend(3)
    from_core = core_swap(attended[3][0])
    attended[2] = attend(2)
    (two,) = adds((attended[2][0], from_core))
    from_x = x_swap(two)
    attended[1] = attend(1)
    from_core = core_swap(attended[1][0])
    attended[0] = attend(0)
    g_slots = slots(cotangent)

    def residual_kernel(a, b, c, x, vrow, vecs, resid_o, low_o):
        resid = x[...].astype(F32) + add(a[...], b[...], c[...]) + vrow[2:3]
        resid_o[...] = resid
        normed, _ = norm_parts(resid)
        low_o[...] = (normed * vecs[1:2] + vecs[2:3]).astype(BF16)

    resid_own, low_own = stage(
        residual_kernel, [attended[0][0], from_core, from_x, x_slots[0], vec, vectors],
        [near((rows, model), F32), near((rows, model), BF16)],
    )

    def relay_kernel(v, out):
        out[...] = v[...]

    def relay(v):
        return stage(relay_kernel, [v], [near(v.shape, v.dtype)])[0]

    from_x = x_swap(low_own)
    low_two = [low_own, core_swap(low_own)]

    def grad_hidden_kernel(g0, g1, g2, g3, w, *outs):
        for g, out in zip((g0, g1, g2, g3), outs):
            out[...] = nt(g[...], w[...]).astype(BF16)

    g_hidden = stage(
        grad_hidden_kernel, [*g_slots, fc_out], [near((rows, hidden_width), BF16)] * half,
        flops=2 * half * rows * model * hidden_width,
    )
    def feed_kernel(low, gh, w, vecs, hid_o, pre_o, grad_o, bias_o):
        hidden_in = nn(low[...], w[...]) + vecs[3:4]
        sig = 1.0 / (1.0 + jnp.exp(-QUICK_GELU * hidden_in))
        hid_o[...] = (hidden_in * sig).astype(BF16)
        slope = sig + QUICK_GELU * hidden_in * sig * (1.0 - sig)
        pre = (gh[...].astype(F32) * slope).astype(BF16)
        pre_o[...] = pre
        grad_o[...] = nt(pre, w[...]).astype(BF16)
        bias_o[...] = row_sum(pre.astype(F32))

    def feed(s):
        return stage(
            feed_kernel, [low_two[s], g_hidden[s], fc_in, vectors],
            [
                near((rows, hidden_width), BF16),
                near((rows, hidden_width), BF16),
                near((rows, model), BF16),
                near((1, hidden_width), F32),
            ],
            flops=2 * 2 * rows * model * hidden_width,
        )

    half_rows, eighth = model // 2, model // 8

    def halves_of(acc, keep, send):
        sec = lax.axis_index("pipe")
        for out, at in ((keep, sec), (send, 1 - sec)):
            start = pl.multiple_of(at * half_rows, half_rows)
            out[...] = acc[pl.ds(start, half_rows), :].astype(BF16)

    half_shapes = [near((half_rows, model), BF16)] * 2

    def weight_half_kernel(a0, a1, b0, b1, out):
        out[...] = tn(a0[...], b0[...])
        out[...] += tn(a1[...], b1[...])

    def weight_half(a0, a1, b0, b1):
        return stage(
            weight_half_kernel, [a0, a1, b0, b1], [near((a0.shape[1], b0.shape[1]), F32)],
            flops=4 * rows * model * hidden_width,
        )[0]

    def weight_kernel(half_sum, a0, a1, b0, b1, keep, send, acc):
        acc[...] = half_sum[...] + tn(a0[...], b0[...])
        acc[...] += tn(a1[...], b1[...])
        halves_of(acc, keep, send)

    def weight(half_sum, a0, a1, b0, b1):
        return stage(
            weight_kernel, [half_sum, a0, a1, b0, b1], half_shapes,
            [pltpu.VMEM((model, model), F32)], flops=4 * rows * model * hidden_width,
        )

    def over_sections(keep, send):
        return keep, y_swap(send) if ring else send

    def over_clips(keep, got):
        if not ring:
            return keep, got

        def kernel(a, b, *refs):
            acc = refs[-1]
            acc[...] = add(a[...], b[...])
            for apart in range(clips):
                start = pl.multiple_of((lax.axis_index("dp") ^ apart) * eighth, eighth)
                refs[apart][...] = acc[pl.ds(start, eighth), :].astype(BF16)

        parts = stage(
            kernel, [keep, got], [near((eighth, model), BF16)] * clips,
            [pltpu.VMEM((half_rows, model), F32)],
        )
        return [parts[0]] + [z_swap(parts[apart], apart) for apart in range(1, clips)]

    def to_clips(parts):
        if not ring:
            return parts
        (own,) = adds(parts)
        return [own] + [z_swap(own, apart) for apart in range(1, clips)]

    def to_sections(parts):
        if not ring:
            keep, send = parts
            sec = lax.axis_index("pipe")
            early = jnp.where(sec == 0, keep, send)
            later = jnp.where(sec == 0, send, keep)
            early, later = lax.psum((early, later), ("pipe", "dp"))
            return jnp.where(sec == 0, early, later), jnp.where(sec == 0, later, early)

        def kernel(*refs):
            for apart in range(clips):
                start = pl.multiple_of((lax.axis_index("dp") ^ apart) * eighth, eighth)
                refs[-1][pl.ds(start, eighth), :] = refs[apart][...]

        (summed,) = stage(kernel, parts, [near((half_rows, model), BF16)])
        return summed, y_swap(summed)

    def put_halves(keep, other, out):
        sec = lax.axis_index("pipe")
        for ref, at in ((keep, sec), (other, 1 - sec)):
            start = pl.multiple_of(at * half_rows, half_rows)
            out[pl.ds(start, half_rows), :] = ref[...].astype(F32)

    def whole(keep, other):
        return stage(put_halves, [keep, other], [shape_of((model, model), F32)])[0]

    hid, pre, grad_parts, bias_rows = [None] * half, [None] * half, [None] * half, [None] * half
    hid[0], pre[0], grad_parts[0], bias_rows[0] = feed(0)
    hid[1], pre[1], grad_parts[1], bias_rows[1] = feed(1)
    from_core1 = core_swap(grad_parts[1])
    fc_out_half = weight_half(hid[0], hid[1], g_slots[0], g_slots[1])
    low_two.append(relay(from_x))
    low_two.append(core_swap(low_two[2]))
    hid[2], pre[2], grad_parts[2], bias_rows[2] = feed(2)
    hid[3], pre[3], grad_parts[3], bias_rows[3] = feed(3)
    from_core3 = core_swap(grad_parts[3])
    fc_out_pair = over_sections(*weight(fc_out_half, hid[2], hid[3], g_slots[2], g_slots[3]))
    (two,) = adds((grad_parts[2], from_core3))
    from_x = x_swap(two)
    fc_in_half = weight_half(low_two[0], low_two[1], pre[0], pre[1])
    fc_in_pair = over_sections(*weight(fc_in_half, low_two[2], low_two[3], pre[2], pre[3]))

    def residual_back_kernel(a, b, c, resid, g, vecs, grad_o, low_o, small_o):
        incoming = add(a[...], b[...], c[...])
        normed, inverse = norm_parts(resid[...])
        real = lax.broadcasted_iota(jnp.int32, (rows, model), 0) < patch
        incoming = jnp.where(real, incoming, 0.0)
        grad = g[...].astype(F32) + norm_back(incoming, normed, inverse, vecs[1:2])
        grad = jnp.where(real, grad, 0.0)
        grad_o[...] = grad
        low = grad.astype(BF16)
        low_o[...] = low
        small_o[...] = jnp.zeros_like(small_o)
        small_o[0:1, :] = row_sum(incoming * normed)
        small_o[1:2, :] = row_sum(incoming)
        small_o[2:3, :] = row_sum(low.astype(F32))
        small_o[3:4, :] = row_sum(g[...].astype(F32))

    grad_resid, grad_low, small_two = stage(
        residual_back_kernel,
        [grad_parts[0], from_core1, from_x, resid_own, g_slots[0], vectors],
        [near((rows, model), F32), near((rows, model), BF16), near((8, model), F32)],
    )
    from_x = x_swap(grad_low)
    branch = [grad_low, core_swap(grad_low)]

    def column_out(values_in, slot, keep_o, send_o):
        ten = lax.axis_index("tensor")
        spot = (ten ^ slot) & 1
        for i in range(4):
            block = values_in[:, i * width : (i + 1) * width]
            apart = ten ^ i

            @pl.when((apart & 1) == 0)
            def _():
                keep_o[apart >> 1, spot] = block

            @pl.when((apart & 1) == 1)
            def _():
                send_o[apart >> 1, spot] = block

    def attend_back_kernel(
        s, branch_in, q, k, v, probs, x, msg, w, vrow, wo, *refs
    ):
        extra = refs[0] if s == 0 else None
        back_o, grads_o, low_o, small_o = refs[-4:]
        gain, shift = vrow[0:1], vrow[1:2]
        here = lax.broadcasted_iota(jnp.int32, (rows, model), 0) == patch
        grad_mixed = nt(branch_in[...], wo[...]).astype(BF16)
        dq = jnp.zeros((rows, width), F32)
        dk = jnp.zeros((rows, width), F32)
        dv = jnp.zeros((rows, width), F32)
        for h, mask in enumerate(head_masks(rows)):
            grad_head = only(mask, grad_mixed)
            low_probs = probs[h]
            wide = low_probs.astype(F32)
            dv = dv + tn(low_probs, grad_head)
            grad_probs = nt(grad_head, v[...])
            inner = jnp.sum(wide * grad_probs, axis=-1, keepdims=True)
            grad_scores = (wide * (grad_probs - inner)).astype(BF16)
            dq = dq + only(mask, nn(grad_scores, k[...]))
            dk = dk + tn(grad_scores, only(mask, q[...]))
        dq = (dq * scale).astype(BF16)
        dk = (dk * scale).astype(BF16)
        dv = dv.astype(BF16)
        grads_o[0] = dq
        grads_o[1] = dk
        grads_o[2] = dv
        grad_low = nn(dq, w[0]) + nn(dk, w[1]) + nn(dv, w[2])
        token = jnp.where(here, msg[s : s + 1], x[...].astype(F32))
        normed, inverse = norm_parts(token)
        low_o[...] = (normed * gain + shift).astype(BF16)
        back = norm_back(grad_low, normed, inverse, gain)
        small_o[...] = jnp.zeros_like(small_o)
        small_o[0:1, :] = row_sum(only(here, back))
        small_o[1:2, :] = row_sum(grad_low * normed)
        small_o[2:3, :] = row_sum(grad_low)
        small_o[3:4, 0:width] = row_sum(dq.astype(F32))
        small_o[3:4, 256 : 256 + width] = row_sum(dv.astype(F32))
        if s == 0:
            back = back + extra[...]
        back_o[...] = back.astype(BF16)

    def attend_back(s):
        _, _, probs, k, v = attended[s]
        ins = [branch[s], q_one[s], k, v, probs, x_slots[s], msg_rows, w_in, vec, w_out]
        return stage(
            functools.partial(attend_back_kernel, s),
            ins + ([grad_resid] if s == 0 else []),
            [
                near((rows, model), BF16),
                near((3, rows, width), BF16),
                near((rows, model), BF16),
                near((8, model), F32),
            ],
            flops=2 * rows * (4 * width * model + 4 * heads * rows * HEAD_DIM),
        )

    column_shapes = [near((2, 2, rows, width), BF16)] * 2

    def column_kernel(*refs):
        for s in range(half):
            keep_o, send_o = refs[half + 2 * (s // 2) : half + 2 * (s // 2) + 2]
            column_out(refs[s][...], s, keep_o, send_o)

    def mlp_kernel(h0, h1, h2, h3, w, resid, vecs, *outs):
        for s, h in enumerate((h0, h1, h2, h3)):
            out = nn(h[...], w[...])
            if s == 0:
                out = out + resid[...] + vecs[4:5]
            keep_o, send_o = outs[2 * (s // 2) : 2 * (s // 2) + 2]
            column_out(out.astype(BF16), s, keep_o, send_o)

    def far_adds(keep01, got01, keep23, got23):
        def kernel(ka, ga, kb, gb, out):
            out[0] = add(kb[1], gb[1]).astype(BF16)
            out[1] = add(ka[1], ga[1]).astype(BF16)

        return x_swap(
            stage(kernel, [keep01, got01, keep23, got23], [near((2, 2, rows, width), BF16)])[0]
        )

    def frames_of(refs):
        keep01, got01, keep23, got23, far = refs
        low_pair = lax.axis_index("tensor") >> 1
        for i in range(2):
            for pair, keep, got, n in (
                (low_pair, keep01, got01, 0),
                (low_pair ^ 1, keep23, got23, 1),
            ):
                yield pair * 2 + i, add(keep[0, i], got[0, i], far[n, i])

    back, grads, low_one, small = [None] * half, [None] * half, [None] * half, [None] * half
    back[0], grads[0], low_one[0], small[0] = attend_back(0)
    back[1], grads[1], low_one[1], small[1] = attend_back(1)
    fc_out_parts = over_clips(*fc_out_pair)

    def attend_weight_half_kernel(ga, gb, la, lb, ma, mb, ba, bb, out):
        for c in range(3):
            at = slice(c * width, (c + 1) * width)
            out[at, :] = tn(ga[c], la[...])
            out[at, :] += tn(gb[c], lb[...])
        out[3 * width :, :] = tn(ma[...], ba[...])
        out[3 * width :, :] += tn(mb[...], bb[...])

    def weight_ins(*picked):
        return [
            array
            for arrays in (grads, low_one, [one[1] for one in attended], branch)
            for array in [arrays[s] for s in picked]
        ]

    (attend_half,) = stage(
        attend_weight_half_kernel, weight_ins(0, 1), [near((4 * width, model), F32)],
        flops=4 * rows * model * 4 * width,
    )
    branch.append(relay(from_x))
    branch.append(core_swap(branch[2]))
    back[2], grads[2], low_one[2], small[2] = attend_back(2)
    fc_in_parts = over_clips(*fc_in_pair)
    back[3], grads[3], low_one[3], small[3] = attend_back(3)

    def pack_kernel(s0, s1, s2, s3, two, p0, p1, p2, p3, out, acc):
        ten = lax.axis_index("tensor")
        acc[...] = jnp.zeros_like(acc)
        for s, ref in enumerate((s0, s1, s2, s3)):
            acc[pl.ds(ten ^ s, 1), :] = ref[0:1, :]
        acc[4:6, :] = s0[1:3, :] + s1[1:3, :] + s2[1:3, :] + s3[1:3, :]
        acc[6:10, :] = two[0:4, :]
        acc[pl.ds(10 + ten, 1), :] = p0[...] + p1[...] + p2[...] + p3[...]
        acc[pl.ds(14 + ten, 1), :] = s0[3:4, :] + s1[3:4, :] + s2[3:4, :] + s3[3:4, :]
        out[...] = acc[...].astype(BF16)

    (pack,) = stage(
        pack_kernel, [*small, small_two, *bias_rows], [near((32, model), BF16)],
        [pltpu.VMEM((32, model), F32)],
    )
    from_core = core_swap(pack)

    def attend_weight_kernel(so_far, ga, gb, la, lb, ma, mb, ba, bb, keep, send, acc):
        for c in range(3):
            at = slice(c * width, (c + 1) * width)
            acc[at, :] = so_far[at, :] + tn(ga[c], la[...])
            acc[at, :] += tn(gb[c], lb[...])
        acc[3 * width :, :] = so_far[3 * width :, :] + tn(ma[...], ba[...])
        acc[3 * width :, :] += tn(mb[...], bb[...])
        halves_of(acc, keep, send)

    attend_pair = over_sections(
        *stage(
            attend_weight_kernel, [attend_half, *weight_ins(2, 3)], half_shapes,
            [pltpu.VMEM((4 * width, model), F32)], flops=4 * rows * model * 4 * width,
        )
    )
    (pack,) = adds((pack, from_core))
    from_x = x_swap(pack)
    keep01, send01, keep23, send23 = stage(column_kernel, back, column_shapes * 2)
    got01, got23 = core_swap(send01), core_swap(send23)
    (pack,) = adds((pack, from_x))
    other_pack = y_swap(pack)
    fc_out_parts = to_clips(fc_out_parts)
    far = far_adds(keep01, got01, keep23, got23)

    def merge_kernel(mine, other, out):
        a, b = mine[...].astype(F32), other[...].astype(F32)
        early = lax.axis_index("pipe") == 0
        out[...] = jnp.concatenate(
            [
                jnp.where(early, a[:half], b[:half]),
                jnp.where(early, b[:half], a[:half]),
                a[half : half + 24] + b[half : half + 24],
            ],
            axis=0,
        ).astype(BF16)

    (pack,) = stage(merge_kernel, [pack, other_pack], [near((32, model), BF16)])
    packs = gather_clips(pack)
    pack_rows = pack.shape[0]
    fc_in_parts = to_clips(fc_in_parts)
    attend_parts = over_clips(*attend_pair)
    block_keep01, block_send01, block_keep23, block_send23 = stage(
        mlp_kernel, [*hid, fc_out, resid_own, vectors], column_shapes * 2,
        flops=2 * half * rows * model * hidden_width,
    )
    block_got01, block_got23 = core_swap(block_send01), core_swap(block_send23)

    def message_back(*refs):
        pack_refs, refs = refs[:blocks], refs[blocks:]
        (first, q, k, v, probs, w, wo, vrow, sent_o, grads_o, back_o) = refs
        sent = jnp.concatenate(
            [clip_block(pack_refs, c, pack_rows).astype(F32)[:frame_count] for c in range(clips)],
            axis=0,
        )
        low = sent.astype(BF16)
        sent_o[...] = sent
        grad_mixed = nt(low, wo[...]).astype(BF16)
        dq = jnp.zeros((all_rows, width), F32)
        dk = jnp.zeros((all_rows, width), F32)
        dv = jnp.zeros((all_rows, width), F32)
        for h, mask in enumerate(head_masks(all_rows)):
            grad_head = only(mask, grad_mixed)
            wide = probs[h]
            dv = dv + tn(wide.astype(BF16), grad_head)
            grad_probs = nt(grad_head, v[...])
            inner = jnp.sum(wide * grad_probs, axis=-1, keepdims=True)
            grad_scores = (wide * (grad_probs - inner)).astype(BF16)
            dq = dq + only(mask, nn(grad_scores, k[...]))
            dk = dk + tn(grad_scores, only(mask, q[...]))
        dq = (dq * scale).astype(BF16)
        dk = (dk * scale).astype(BF16)
        dv = dv.astype(BF16)
        grads_o[0] = dq
        grads_o[1] = dk
        grads_o[2] = dv
        grad_low = nn(dq, w[0]) + nn(dk, w[1]) + nn(dv, w[2])
        normed, inverse = norm_parts(first[...])
        back_msg = norm_back(grad_low, normed, inverse, vrow[0:1])
        back_o[0:all_rows, :] = back_msg.astype(BF16)
        tail = jnp.concatenate(
            [row_sum(grad_low * normed), row_sum(grad_low), jnp.zeros((14, model), F32)], axis=0
        )
        back_o[all_rows:, :] = tail.astype(BF16)

    sent_all, grads_zero, back_zero = stage(
        message_back,
        [*packs, first_msg, q_zero, k_zero, v_zero, probs_zero, own_in, own_out, own_vec],
        [
            near((all_rows, model), F32),
            near((3, all_rows, width), BF16),
            near((all_rows + 16, model), BF16),
        ],
    )
    from_core = core_swap(back_zero)
    fc_out_halves = to_sections(fc_out_parts)
    (back_zero,) = adds((back_zero, from_core))
    from_x = x_swap(back_zero)
    block_far = far_adds(block_keep01, block_got01, block_keep23, block_got23)

    def message_weight(sent, grads_in, low, mixed, in_o, out_o, qv_o, bias_o):
        for c in range(3):
            in_o[c] = tn(grads_in[c], low[...])
        out_o[...] = tn(mixed[...], sent[...].astype(BF16))
        qv_o[0:1, :] = row_sum(grads_in[0].astype(F32))
        qv_o[1:2, :] = row_sum(grads_in[2].astype(F32))
        bias_o[...] = row_sum(sent[...])

    in_zero, out_zero, qv_zero, bias_zero = stage(
        message_weight, [sent_all, grads_zero, low_zero, mixed_zero],
        [
            near((3, width, model), F32),
            near((width, model), F32),
            near((2, width), F32),
            near((1, model), F32),
        ],
    )
    attend_parts = to_clips(attend_parts)
    (back_zero,) = adds((back_zero, from_x))
    back_late = y_late(back_zero)

    def block_out_kernel(*refs):
        for at, total in frames_of(refs[:-1]):
            refs[-1][at] = total.T[:, :patch].astype(BF16)

    (block_out,) = stage(
        block_out_kernel, [block_keep01, block_got01, block_keep23, block_got23, block_far],
        [shape_of((half, width, patch), BF16)],
    )
    fc_in_halves = to_sections(fc_in_parts)
    fc_out_grad = whole(*fc_out_halves)

    def message_end(*refs):
        pack_refs, refs = refs[:blocks], refs[blocks:]
        cls_refs, refs = refs[:blocks], refs[blocks:]
        (sent, own, late, mw, qv_in, bias_in, w_o, cls_o, vec_o, qv_o, turned, sums) = refs
        sec, ten = lax.axis_index("pipe"), lax.axis_index("tensor")
        total = jnp.where(sec == 0, own[...].astype(F32), late[...].astype(F32))
        grad_first = sent[...] + total[:all_rows]
        at = pl.ds(pl.multiple_of(ten * width, width), width)
        mine = grad_first[:16]
        high = mine.astype(BF16)
        rest = (mine - high.astype(F32)).astype(BF16)
        mw_rows = mw[at, :]
        cls_o[...] = nt(high, mw_rows) + nt(rest, mw_rows)
        turned[...] = grad_first.T
        mine = turned[at, :]
        high = mine.astype(BF16)
        rest = (mine - high.astype(F32)).astype(BF16)
        cls = jnp.concatenate([clip_block(cls_refs, c, frame_count).astype(F32) for c in range(clips)])
        cls = cls.astype(BF16)
        w_o[...] = nn(high, cls) + nn(rest, cls)
        summed = clip_block(pack_refs, 0, pack_rows).astype(F32)
        for c in range(1, clips):
            summed = summed + clip_block(pack_refs, c, pack_rows).astype(F32)
        sums[...] = summed[frame_count:]
        first_one = sec == 0
        vec_o[0:1, :] = jnp.where(first_one, total[all_rows : all_rows + 1], sums[0:1])
        vec_o[1:2, :] = jnp.where(first_one, total[all_rows + 1 : all_rows + 2], sums[1:2])
        vec_o[2:3, :] = jnp.where(first_one, bias_in[...], sums[4:5])
        vec_o[3:4, :] = sums[2:3]
        vec_o[4:5, :] = sums[3:4]
        vec_o[5:6, :] = sums[5:6]
        vec_o[6:7, :] = sums[pl.ds(6 + ten, 1), :]
        vec_o[7:8, :] = row_sum(grad_first)
        qv_row = sums[pl.ds(10 + ten, 1), :]
        qv_o[0:1, :] = jnp.where(first_one, qv_in[0:1], qv_row[:, :width])
        qv_o[1:2, :] = jnp.where(first_one, qv_in[1:2], qv_row[:, 256 : 256 + width])

    msg_w_grad, cls_part, vec_grads, qv_grad = stage(
        message_end,
        [*packs, *cls_all, sent_all, back_zero, back_late, msg_w, qv_zero, bias_zero],
        [
            shape_of((width, model), F32),
            near((16, width), F32),
            near((8, model), F32),
            near((2, width), F32),
        ],
        [pltpu.VMEM((model, all_rows), F32), pltpu.VMEM((24, model), F32)],
    )

    def frames_grad_kernel(*refs):
        cls, out = refs[-2:]
        top = lax.broadcasted_iota(jnp.int32, (rows, width), 0) == 0
        for at, total in frames_of(refs[:-2]):
            row = cls[pl.ds(lax.axis_index("pipe") * half + at, 1), :]
            out[at] = (total + jnp.where(top, row, 0.0)).T[:, :patch].astype(BF16)

    (frames_grad,) = stage(
        frames_grad_kernel, [keep01, got01, keep23, got23, far, cls_part],
        [shape_of((half, width, patch), BF16)],
    )
    attend_halves = to_sections(attend_parts)
    fc_in_grad = whole(*fc_in_halves)

    def attend_whole_kernel(keep, other, in_zero_ref, out_zero_ref, in_o, out_o, acc):
        @pl.when(lax.axis_index("pipe") == 0)
        def _():
            in_o[...] = in_zero_ref[...]
            out_o[...] = out_zero_ref[...]

        @pl.when(lax.axis_index("pipe") == 1)
        def _():
            put_halves(keep, other, acc)
            for c in range(3):
                in_o[c] = acc[c * width : (c + 1) * width, :]
            out_o[...] = acc[3 * width :, :]

    attn_in_grad, attn_out_grad = stage(
        attend_whole_kernel, [*attend_halves, in_zero, out_zero],
        [shape_of((3, width, model), F32), shape_of((width, model), F32)],
        [pltpu.VMEM((4 * width, model), F32)],
    )

    return (
        jnp.swapaxes(block_out, 1, 2)[None],
        jnp.swapaxes(frames_grad, 1, 2)[None],
        msg_w_grad.T,
        vec_grads[7],
        vec_grads[0:1],
        vec_grads[1:2],
        jnp.transpose(attn_in_grad, (2, 0, 1))[None],
        qv_grad[None],
        attn_out_grad[None],
        vec_grads[2:3],
        vec_grads[3],
        vec_grads[4],
        fc_in_grad,
        vec_grads[6],
        fc_out_grad,
        vec_grads[5],
    )


def solution(mesh):
    return jax.shard_map(
        body,
        mesh=mesh,
        in_specs=(
            P("dp", None, None, None),
            P(),
            P(),
            P(),
            P("pipe", None),
            P("pipe", None),
            P("pipe", None, None, "tensor"),
            P("pipe", None, "tensor"),
            P("pipe", "tensor", None),
            P("pipe", None),
            P(),
            P(),
            P(None, "tensor"),
            P("tensor"),
            P("tensor", None),
            P(),
            P("dp", None, None, None),
        ),
        out_specs=(
            P("dp", "pipe", None, "tensor"),
            P("dp", "pipe", None, "tensor"),
            P(None, "tensor"),
            P(),
            P("pipe", None),
            P("pipe", None),
            P("pipe", None, None, "tensor"),
            P("pipe", None, "tensor"),
            P("pipe", "tensor", None),
            P("pipe", None),
            P(),
            P(),
            P(None, "tensor"),
            P("tensor"),
            P("tensor", None),
            P(),
        ),
        check_vma=False,
    )
```

```python
import functools

import jax
import jax.numpy as jnp
from jax import lax
from jax.experimental import pallas as pl
from jax.experimental.pallas import tpu as pltpu
from jax.sharding import PartitionSpec as P

HEAD_DIM = 64
EPSILON = 1e-05
QUICK_GELU = 1.702
F32 = jnp.float32
BF16 = jnp.bfloat16
VMEM_BYTES = 16 * 1024 * 1024


def nn(left, right):
    return lax.dot_general(left, right, (((1,), (0,)), ((), ())), preferred_element_type=F32)


def nt(left, right):
    return lax.dot_general(left, right, (((1,), (1,)), ((), ())), preferred_element_type=F32)


def tn(left, right):
    return lax.dot_general(left, right, (((0,), (0,)), ((), ())), preferred_element_type=F32)


def norm_parts(values_in):
    centred = values_in - jnp.mean(values_in, axis=-1, keepdims=True)
    inverse = lax.rsqrt(jnp.mean(centred * centred, axis=-1, keepdims=True) + EPSILON)
    return centred * inverse, inverse


def norm_back(incoming, normed, inverse, gain):
    weighted = incoming * gain
    centred = weighted - jnp.mean(weighted, axis=-1, keepdims=True)
    return inverse * (centred - normed * jnp.mean(weighted * normed, axis=-1, keepdims=True))


def row_sum(values_in):
    return jnp.sum(values_in, axis=0, keepdims=True)


def shape_of(shape, kind):
    return jax.ShapeDtypeStruct(shape, kind)


def near(shape, kind):
    return pltpu.VMEM(shape, kind)


class Chain:
    def __init__(self):
        self.token = None
        self.near, self.kept = set(), []
        self.cost = 4 * 10**9

    def __call__(self, kernel, ins, outs, scratch=(), flops=0, far=0):
        tokens = 0 if self.token is None else 1
        count, given = len(ins), len(outs)

        def stage(*refs):
            rest = refs[tokens:]
            kernel(*rest[:count], *rest[count : count + given], *rest[count + given + 1 :])

        vmem = pl.BlockSpec(memory_space=pltpu.VMEM)
        held = [] if self.token is None else [self.token]
        ins = [
            pltpu.with_memory_space_constraint(a, pltpu.HBM)
            if i < far
            else pltpu.with_memory_space_constraint(a, pltpu.VMEM)
            if id(a) in self.near
            else a
            for i, a in enumerate(ins)
        ]
        results = pl.pallas_call(
            stage,
            out_shape=[*outs, near((8, 128), F32)],
            in_specs=[pl.BlockSpec(memory_space=pl.ANY)] * tokens
            + [pl.BlockSpec(memory_space=pltpu.HBM)] * far
            + [vmem] * (count - far),
            out_specs=[vmem] * (given + 1),
            scratch_shapes=list(scratch),
            compiler_params=pltpu.CompilerParams(vmem_limit_bytes=VMEM_BYTES),
            cost_estimate=pl.CostEstimate(flops=self.cost, bytes_accessed=0, transcendentals=0),
        )(*held, *ins)
        self.token = results[-1]
        self.kept += results
        for out, result in zip(outs, results):
            if not isinstance(out, jax.ShapeDtypeStruct):
                self.near.add(id(result))
        return results[:-1]


def body(
    frames,
    video_group,
    msg_w,
    msg_bias,
    norm_gain,
    norm_shift,
    attn_in,
    qv_bias,
    attn_out,
    out_bias,
    norm2_gain,
    norm2_shift,
    fc_in,
    fc_in_bias,
    fc_out,
    fc_out_bias,
    cotangent,
):
    _, frame_count, patch, model = frames.shape

    width = attn_in.shape[-1]

    hidden_width = fc_in.shape[-1]

    heads = width // HEAD_DIM

    clips = lax.axis_size("dp")

    half = frame_count // 2

    rows = -(-(patch + 1) // 16) * 16

    all_rows = clips * frame_count

    scale = HEAD_DIM ** (-0.5)

    pipe = lax.axis_index("pipe")

    tensor = lax.axis_index("tensor")

    clip = lax.axis_index("dp")

    ring = clips == 4

    stage = Chain()

    quarter = hidden_width // 4

    assert quarter == width and hidden_width == model and half == 4

    def tensor_swap(v, bit):
        return lax.ppermute(v, "tensor", [(i, i ^ bit) for i in range(4)])

    def core_swap(v):
        return tensor_swap(v, 1)

    def x_swap(v):
        return tensor_swap(v, 2)

    def y_swap(v):
        return lax.ppermute(v, "pipe", [(0, 1), (1, 0)])

    def y_late(v):
        return lax.ppermute(v, "pipe", [(0, 1)])

    def y_early(v):
        return lax.ppermute(v, "pipe", [(1, 0)])

    def z_swap(v, bit):
        return lax.ppermute(v, "dp", [(i, i ^ bit) for i in range(clips)])

    def gather_clips(v):
        if ring:
            return [v] + [z_swap(v, apart) for apart in range(1, clips)]
        every = lax.all_gather(v, "dp")
        every = lax.dynamic_slice_in_dim(jnp.concatenate([every, every]), clip, clips, 0)
        return [every.reshape(clips * v.shape[0], v.shape[1])]

    def clip_block(refs, c, size):
        each = clips // len(refs)
        at = c % each * size
        return refs[c // each][at : at + size, :]

    blocks = clips if ring else 1

    pack_blocks = 2 if ring else 1

    def head_masks(n):
        lane = lax.broadcasted_iota(jnp.int32, (n, width), 1)
        return [(lane >= h * HEAD_DIM) & (lane < (h + 1) * HEAD_DIM) for h in range(heads)]

    def only(mask, v):
        return jnp.where(mask, v, jnp.zeros_like(v))

    def add(*terms):
        total = terms[0].astype(F32)
        for term in terms[1:]:
            total = total + term.astype(F32)
        return total

    def adds(*groups):
        sizes = [len(group) for group in groups]

        def kernel(*refs):
            at = 0
            for size, out in zip(sizes, refs[sum(sizes) :]):
                out[...] = add(*[ref[...] for ref in refs[at : at + size]]).astype(out.dtype)
                at += size

        return stage(
            kernel,
            [array for group in groups for array in group],
            [near(group[0].shape, group[0].dtype) for group in groups],
        )

    own_in = jnp.transpose(attn_in[0], (1, 2, 0))

    own_out = attn_out[0]

    tokens = jnp.transpose(frames[0], (1, 0, 2))

    grads_in = jnp.transpose(cotangent[0], (1, 0, 2))

    def small_kernel(*refs):
        ins, vecs_o, own_o, in_o, both_o = refs[:10], *refs[10:14]
        lines, rest, sem = refs[14:19], refs[19:23], refs[23]
        pairs = [(ins[0], in_o)] + list(zip(ins[1:], (*lines, *rest)))
        pairs += [(ins[0].at[c], both_o.at[c * width : (c + 1) * width]) for c in range(3)]
        copies = [pltpu.make_async_copy(a, b, sem.at[i]) for i, (a, b) in enumerate(pairs)]
        for copy in copies:
            copy.start()
        for copy in copies:
            copy.wait()
        for i, line in enumerate(lines):
            vecs_o[i : i + 1, :] = line[...].reshape(1, model)
        for i, line in enumerate(rest[:3]):
            own_o[i : i + 1, :] = line[...]
        own_o[3:8, :] = jnp.zeros((5, model), F32)
        own_o[3:5, 0:width] = rest[3][0]
        high = own_o[...].astype(BF16).astype(F32)
        both_o[3 * width :, :] = jnp.concatenate([high, own_o[...] - high], axis=0).astype(BF16)

    def load_kernel(*refs):
        sem = refs[4]
        copies = [
            pltpu.make_async_copy(a, b, sem.at[i]) for i, (a, b) in enumerate(zip(refs[:2], refs[2:4]))
        ]
        for copy in copies:
            copy.start()
        for copy in copies:
            copy.wait()

    tokens_all = rows * frame_count

    lanes = 128

    def slot_kernel(v, *refs):
        outs, (wide, held, sem) = refs[:-3], refs[-3:]
        copy = pltpu.make_async_copy(v, held, sem)
        copy.start()
        copy.wait()
        flat = held[...].astype(F32).reshape(patch * frame_count, model)
        sec, ten = lax.axis_index("pipe"), lax.axis_index("tensor")
        for c in range(model // lanes):
            at = c * tokens_all
            wide[at : at + patch * frame_count, :] = flat[:, c * lanes : (c + 1) * lanes]
            wide[at + patch * frame_count : at + tokens_all, :] = jnp.zeros(
                ((rows - patch) * frame_count, lanes), F32
            )
            for s, out in enumerate(outs):
                frame = at + (sec if s < half else 1 - sec) * half + (ten ^ (s % half))
                out[:, c * lanes : (c + 1) * lanes] = wide[
                    pl.ds(frame, rows, stride=frame_count), :
                ].astype(BF16)

    def slots(v, count):
        return stage(
            slot_kernel,
            [v],
            [near((rows, model), BF16)] * count,
            [
                pltpu.VMEM((model // lanes * tokens_all, lanes), F32),
                pltpu.VMEM((patch, frame_count, model), BF16),
                pltpu.SemaphoreType.DMA,
            ],
            far=1,
        )

    def message_forward(groups, *refs):
        cls_refs, refs = refs[:blocks], refs[blocks:]
        (mw, vecs, vrow, w, wo, first_o, low_o, q_o, k_o, v_o, probs_o, mixed_o, part_o, ids, sem) = refs
        copy = pltpu.make_async_copy(groups, ids, sem)
        copy.start()
        cls = jnp.concatenate([clip_block(cls_refs, c, frame_count).astype(F32) for c in range(clips)])
        first = nn(cls.astype(BF16), mw[...]) + vecs[0:1]
        first_o[...] = first
        normed, _ = norm_parts(first)
        low = (normed * vrow[0:1] + vrow[1:2]).astype(BF16)
        low_o[...] = low
        q = (nt(low, w[0]) + vrow[3:4, :width]).astype(BF16)
        k = nt(low, w[1]).astype(BF16)
        v = (nt(low, w[2]) + vrow[4:5, :width]).astype(BF16)
        q_o[...] = q
        k_o[...] = k
        v_o[...] = v
        of_row = lax.broadcasted_iota(jnp.int32, (all_rows, all_rows), 0) // frame_count
        of_col = lax.broadcasted_iota(jnp.int32, (all_rows, all_rows), 1) // frame_count
        mine = lax.axis_index("dp")
        copy.wait()
        row_id = jnp.zeros((all_rows, all_rows), jnp.int32)
        col_id = jnp.zeros((all_rows, all_rows), jnp.int32)
        for c in range(clips):
            mark = ids[mine ^ c if ring else lax.rem(mine + c, clips)]
            row_id = jnp.where(of_row == c, mark, row_id)
            col_id = jnp.where(of_col == c, mark, col_id)
        allowed = row_id == col_id
        mixed = jnp.zeros((all_rows, width), F32)
        for h, mask in enumerate(head_masks(all_rows)):
            scores = jnp.where(allowed, nt(only(mask, q), k) * scale, -jnp.inf)
            exponent = jnp.exp(scores - jnp.max(scores, axis=-1, keepdims=True))
            probs = exponent / jnp.sum(exponent, axis=-1, keepdims=True)
            probs_o[h] = probs
            mixed = mixed + only(mask, nn(probs.astype(BF16), v))
        mixed = mixed.astype(BF16)
        mixed_o[...] = mixed
        part = nn(mixed, wo[...]) + jnp.where(lax.axis_index("tensor") == 0, vrow[2:3], 0.0)
        part_o[...] = part[:frame_count]

    def project_kernel(x0, x1, x2, x3, wa, wb, va, w, vrow, *outs):
        early = lax.axis_index("pipe") == 0
        for c in range(3):
            w[c] = jnp.where(early, wb[c * width : (c + 1) * width, :], wa[c])
        sent = wb[3 * width :, :].astype(F32)
        vrow[...] = jnp.where(early, sent[0:8] + sent[8:16], va[...])
        gain, shift = vrow[0:1], vrow[1:2]
        for s, x in enumerate((x0, x1, x2, x3)):
            normed, _ = norm_parts(x[...].astype(F32))
            low = (normed * gain + shift).astype(BF16)
            outs[s][...] = (nt(low, w[0]) + vrow[3:4, :width]).astype(BF16)
            outs[half + s][...] = nt(low, w[1]).astype(BF16)
            outs[2 * half + s][...] = (nt(low, w[2]) + vrow[4:5, :width]).astype(BF16)

    def message_rows_kernel(first, part, late, w, vrow, wa, wb, msg_o, k_o, v_o, w_o):
        sec, ten = lax.axis_index("pipe"), lax.axis_index("tensor")
        w_o[...] = jnp.where(sec == 0, wb[...], wa[...])
        msg_o[...] = jnp.zeros_like(msg_o)
        for s in range(half):
            at = pl.ds(sec * half + (ten ^ s), 1)
            summed = jnp.where(sec == 0, part[at, :], late[at, :])
            msg_o[s : s + 1, :] = (first[at, :] + summed).astype(BF16).astype(F32)
        normed, _ = norm_parts(msg_o[...])
        low = (normed * vrow[0:1] + vrow[1:2]).astype(BF16)
        k_o[...] = nt(low, w[1])
        v_o[...] = nt(low, w[2]) + vrow[4:5, :width]

    def attend_kernel(
        s, q, k, v, km, vm, wo, part_o, mixed_o, probs_o, k_o, v_o,
    ):
        here = lax.broadcasted_iota(jnp.int32, (rows, width), 0) == patch
        key_here = lax.broadcasted_iota(jnp.int32, (rows, rows), 1) <= patch
        kk = jnp.where(here, km[s : s + 1], k[...].astype(F32)).astype(BF16)
        vv = jnp.where(here, vm[s : s + 1], v[...].astype(F32)).astype(BF16)
        k_o[...] = kk
        v_o[...] = vv
        mixed = jnp.zeros((rows, width), F32)
        for h, mask in enumerate(head_masks(rows)):
            scores = nt(only(mask, q[...]), kk) * scale
            scores = jnp.where(key_here, scores, -jnp.inf)
            exponent = jnp.exp(scores - jnp.max(scores, axis=-1, keepdims=True))
            probs = exponent * (1.0 / jnp.sum(exponent, axis=-1, keepdims=True))
            probs = probs.astype(BF16)
            probs_o[h] = probs
            mixed = mixed + only(mask, nn(probs, vv))
        mixed = mixed.astype(BF16)
        mixed_o[...] = mixed
        part_o[...] = nn(mixed, wo[...]).astype(BF16)

    def attend(s):
        return stage(
            functools.partial(attend_kernel, s),
            [q_one[s], k_patch[s], v_patch[s], k_msg, v_msg, w_out],
            [
                near((rows, model), BF16),
                near((rows, width), BF16),
                near((heads, rows, rows), BF16),
                near((rows, width), BF16),
                near((rows, width), BF16),
            ],
            flops=2 * rows * (width * model + 2 * heads * rows * HEAD_DIM),
        )

    def residual_kernel(a, b, x, vrow, vecs, resid_o, low_o):
        resid = x[...].astype(F32) + add(a[...], b[...]) + vrow[2:3]
        resid_o[...] = resid
        normed, _ = norm_parts(resid)
        low_o[...] = (normed * vecs[1:2] + vecs[2:3]).astype(BF16)

    def relay_kernel(v, out):
        out[...] = v[...]

    def relay(v):
        return stage(relay_kernel, [v], [near(v.shape, v.dtype)])[0]

    def grad_hidden_kernel(g0, g1, g2, g3, w, *outs):
        for g, out in zip((g0, g1, g2, g3), outs):
            out[...] = nt(g[...], w[...]).astype(BF16)

    def feed_kernel(low, gh, w, vecs, hid_o, pre_o, grad_o, bias_o):
        hidden_in = nn(low[...], w[...]) + vecs[3:4]
        sig = 1.0 / (1.0 + jnp.exp(-QUICK_GELU * hidden_in))
        hid_o[...] = (hidden_in * sig).astype(BF16)
        slope = sig + QUICK_GELU * hidden_in * sig * (1.0 - sig)
        pre = (gh[...].astype(F32) * slope).astype(BF16)
        pre_o[...] = pre
        grad_o[...] = nt(pre, w[...]).astype(BF16)
        bias_o[...] = row_sum(pre.astype(F32))

    def feed(low, gh):
        return stage(
            feed_kernel, [low, gh, fc_in, vectors],
            [
                near((rows, hidden_width), BF16),
                near((rows, hidden_width), BF16),
                near((rows, model), BF16),
                near((1, hidden_width), F32),
            ],
            flops=2 * 2 * rows * model * hidden_width,
        )

    half_rows, eighth = model // 2, model // 8

    def halves_of(acc, keep, send):
        sec = lax.axis_index("pipe")
        for out, at in ((keep, sec), (send, 1 - sec)):
            start = pl.multiple_of(at * half_rows, half_rows)
            out[...] = acc[pl.ds(start, half_rows), :].astype(BF16)

    half_shapes = [near((half_rows, model), BF16)] * 2

    def section_columns():
        return pl.ds(pl.multiple_of(lax.axis_index("pipe") * half_rows, half_rows), half_rows)

    def feed_other_kernel(low, g, w, w_out, vecs, hid_o, pre_o):
        columns = section_columns()
        hidden_in = nn(low[...], w[:, columns]) + vecs[3:4, columns]
        sig = 1.0 / (1.0 + jnp.exp(-QUICK_GELU * hidden_in))
        hid_o[...] = (hidden_in * sig).astype(BF16)
        slope = sig + QUICK_GELU * hidden_in * sig * (1.0 - sig)
        pre_o[...] = (nt(g[...], w_out[columns, :]).astype(BF16).astype(F32) * slope).astype(BF16)

    def feed_other(low, g):
        return stage(
            feed_other_kernel, [low, g, fc_in, fc_out, vectors],
            [near((rows, half_rows), BF16)] * 2,
        )

    def own_out_kernel(h0, h1, g0, g1, out):
        out[...] = tn(h0[:, section_columns()], g0[...])
        out[...] += tn(h1[:, section_columns()], g1[...])

    def own_in_kernel(l0, l1, p0, p1, out):
        out[...] = tn(l0[...], p0[:, section_columns()])
        out[...] += tn(l1[...], p1[:, section_columns()])

    def own_part(kernel, shape, *ins):
        return stage(kernel, list(ins), [near(shape, F32)])[0]

    def clip_parts(acc, mine, send):
        size = mine.shape[0] // 2
        for out, first in ((mine, 0), (send, 1)):
            for at, apart in ((0, first), (size, first ^ 2)):
                out[at : at + size, :] = acc[clip_rows(apart, size), :].astype(BF16)

    def sum_out_kernel(part, h2, h3, g2, g3, o0, o1, o2, o3, q0, q1, q2, q3, mine, send, acc):
        acc[...] = part[...] + tn(h2[:, section_columns()], g2[...])
        acc[...] += tn(h3[:, section_columns()], g3[...])
        for o, q in ((o0, q0), (o1, q1), (o2, q2), (o3, q3)):
            acc[...] += tn(o[...], q[...])
        clip_parts(acc, mine, send)

    def sum_in_kernel(part, l2, l3, p2, p3, m0, m1, m2, m3, q0, q1, q2, q3, mine, send, acc):
        acc[...] = part[...] + tn(l2[...], p2[:, section_columns()])
        acc[...] += tn(l3[...], p3[:, section_columns()])
        for m, q in ((m0, q0), (m1, q1), (m2, q2), (m3, q3)):
            acc[...] += tn(m[...], q[...])
        clip_parts(acc, mine, send)

    def whole_part(kernel, part, *ins):
        rows_in, columns = part.shape
        mine, send = stage(
            kernel, [part, *ins], [near((rows_in // 2, columns), BF16)] * 2,
            [pltpu.VMEM((rows_in, columns), F32)],
        )
        return mine, z_swap(send, 1) if ring else send

    def over_sections(keep, send):
        return keep, y_swap(send) if ring else send

    def clip_rows(apart, size=eighth):
        here = lax.axis_index("dp") if ring else 0
        return pl.ds(pl.multiple_of((here ^ apart) * size, size), size)

    def over_near_clip(keep, got):
        if not ring:
            return keep, got

        def kernel(a, b, mine, send, acc):
            acc[...] = add(a[...], b[...])
            for out, first in ((mine, 0), (send, 1)):
                out[0:eighth, :] = acc[clip_rows(first), :].astype(BF16)
                out[eighth:, :] = acc[clip_rows(first ^ 2), :].astype(BF16)

        mine, send = stage(
            kernel, [keep, got], [near((2 * eighth, model), BF16)] * 2,
            [pltpu.VMEM((half_rows, model), F32)],
        )
        return mine, z_swap(send, 1)

    def over_far_clip(mine, got):
        if not ring:
            return mine, got
        size = mine.shape[0] // 2

        def kernel(a, b, own, send):
            own[...] = add(a[0:size, :], b[0:size, :]).astype(BF16)
            send[...] = add(a[size:, :], b[size:, :]).astype(BF16)

        own, send = stage(kernel, [mine, got], [near((size, mine.shape[1]), BF16)] * 2)
        return own, z_swap(send, 2)

    def to_far_clip(own, got):
        if not ring:
            return own, got
        (own,) = adds((own, got))
        return own, z_swap(own, 2)

    def to_near_clip(own, got):
        if not ring:
            return own, got

        size = own.shape[0]

        def kernel(a, b, out):
            out[0:size, :] = a[...]
            out[size:, :] = b[...]

        (both,) = stage(kernel, [own, got], [near((2 * size, own.shape[1]), BF16)])
        return both, z_swap(both, 1)

    def join_kernel(a, b, out):
        size = a.shape[0] // 2
        for apart, ref, at in ((0, a, 0), (2, a, size), (1, b, 0), (3, b, size)):
            out[clip_rows(apart, size), :] = ref[at : at + size, :]

    def to_sections(both, got, move=y_swap):
        if not ring:
            sec = lax.axis_index("pipe")
            early = jnp.where(sec == 0, both, got)
            later = jnp.where(sec == 0, got, both)
            early, later = lax.psum((early, later), ("pipe", "dp"))
            return jnp.where(sec == 0, early, later), jnp.where(sec == 0, later, early)
        (summed,) = stage(join_kernel, [both, got], [near((half_rows, model), BF16)])
        return summed, move(summed)

    def to_other_section(both, got):
        if not ring:
            both, got = lax.psum((both, got), "dp")
        (summed,) = stage(join_kernel, [both, got], [near((2 * both.shape[0], both.shape[1]), BF16)])
        return summed, y_swap(summed)

    def put_halves(keep, other, out):
        sec = lax.axis_index("pipe")
        for ref, at in ((keep, sec), (other, 1 - sec)):
            start = pl.multiple_of(at * half_rows, half_rows)
            out[pl.ds(start, half_rows), :] = ref[...].astype(F32)

    def whole(keep, other):
        return stage(put_halves, [keep, other], [shape_of((model, model), F32)])[0]

    def put_columns(keep, other, out):
        sec = lax.axis_index("pipe")
        for ref, at in ((keep, sec), (other, 1 - sec)):
            start = pl.multiple_of(at * half_rows, half_rows)
            out[:, pl.ds(start, half_rows)] = ref[...].astype(F32)

    def whole_of_columns(keep, other):
        return stage(put_columns, [keep, other], [shape_of((model, model), F32)])[0]

    def residual_back_kernel(a, b, resid, g, vecs, grad_o, low_o, small_o):
        incoming = add(a[...], b[...])
        normed, inverse = norm_parts(resid[...])
        real = lax.broadcasted_iota(jnp.int32, (rows, model), 0) < patch
        incoming = jnp.where(real, incoming, 0.0)
        grad = g[...].astype(F32) + norm_back(incoming, normed, inverse, vecs[1:2])
        grad = jnp.where(real, grad, 0.0)
        grad_o[...] = grad
        low = grad.astype(BF16)
        low_o[...] = low
        small_o[...] = jnp.zeros_like(small_o)
        small_o[0:1, :] = row_sum(incoming * normed)
        small_o[1:2, :] = row_sum(incoming)
        small_o[2:3, :] = row_sum(low.astype(F32))
        small_o[3:4, :] = row_sum(g[...].astype(F32))

    def column_out(values_in, slot, keep_o, send_o):
        ten = lax.axis_index("tensor")
        spot = (ten ^ slot) & 1
        for i in range(4):
            block = values_in[:, i * width : (i + 1) * width]
            apart = ten ^ i
            for out, odd in ((keep_o, 0), (send_o, 1)):
                for side in range(2):

                    @pl.when(((apart & 1) == odd) & (spot == side))
                    def _():
                        out[apart >> 1, slot >> 1, :, side * width : (side + 1) * width] = block

    def attend_back_kernel(
        s, branch_in, q, k, v, probs, x, msg, w, vrow, wo, *refs
    ):
        extra = refs[0] if s == 0 else None
        back_o, grads_o, low_o, small_o = refs[-4:]
        gain, shift = vrow[0:1], vrow[1:2]
        here = lax.broadcasted_iota(jnp.int32, (rows, model), 0) == patch
        grad_mixed = nt(branch_in[...], wo[...]).astype(BF16)
        dq = jnp.zeros((rows, width), F32)
        dk = jnp.zeros((rows, width), F32)
        dv = jnp.zeros((rows, width), F32)
        for h, mask in enumerate(head_masks(rows)):
            grad_head = only(mask, grad_mixed)
            low_probs = probs[h]
            wide = low_probs.astype(F32)
            dv = dv + tn(low_probs, grad_head)
            grad_probs = nt(grad_head, v[...])
            inner = jnp.sum(wide * grad_probs, axis=-1, keepdims=True)
            grad_scores = (wide * (grad_probs - inner)).astype(BF16)
            dq = dq + only(mask, nn(grad_scores, k[...]))
            dk = dk + tn(grad_scores, only(mask, q[...]))
        dq = (dq * scale).astype(BF16)
        dk = (dk * scale).astype(BF16)
        dv = dv.astype(BF16)
        grads_o[0] = dq
        grads_o[1] = dk
        grads_o[2] = dv
        grad_low = nn(dq, w[0]) + nn(dk, w[1]) + nn(dv, w[2])
        token = jnp.where(here, msg[s : s + 1], x[...].astype(F32))
        normed, inverse = norm_parts(token)
        low_o[...] = (normed * gain + shift).astype(BF16)
        back = norm_back(grad_low, normed, inverse, gain)
        small_o[...] = jnp.zeros_like(small_o)
        small_o[0:1, :] = row_sum(only(here, back))
        small_o[1:2, :] = row_sum(grad_low * normed)
        small_o[2:3, :] = row_sum(grad_low)
        small_o[3:4, 0:width] = row_sum(dq.astype(F32))
        small_o[3:4, 256 : 256 + width] = row_sum(dv.astype(F32))
        if s == 0:
            back = back + extra[...]
        back_o[...] = back.astype(BF16)

    def attend_back(s, low_grad, kept):
        _, mixed, probs, k, v = kept
        ins = [low_grad, q_one[s], k, v, probs, x_slots[s], msg_rows, w_in, vec, w_out]
        return stage(
            functools.partial(attend_back_kernel, s),
            ins + ([grad_resid] if s == 0 else []),
            [
                near((rows, model), BF16),
                near((3, rows, width), BF16),
                near((rows, model), BF16),
                near((8, model), F32),
            ],
            flops=2 * rows * (4 * width * model + 4 * heads * rows * HEAD_DIM),
        )

    column_shapes = [near((2, 2, rows, 2 * width), BF16)] * 2

    def column_kernel(b0, b1, b2, b3, keep_o, send_o):
        for s, ref in enumerate((b0, b1, b2, b3)):
            column_out(ref[...], s, keep_o, send_o)

    def mlp_kernel(h0, h1, h2, h3, w, resid, vecs, *outs):
        for s, h in enumerate((h0, h1, h2, h3)):
            out = nn(h[...], w[...])
            if s == 0:
                out = out + resid[...] + vecs[4:5]
            outs[s][...] = out.astype(BF16)

    def far_columns(keep, got):
        def kernel(a, b, near_o, far_o):
            for i in range(2):
                near_o[i] = add(a[0, i], b[0, i]).astype(BF16)
                far_o[i ^ 1] = add(a[1, i], b[1, i]).astype(BF16)

        kept, send = stage(kernel, [keep, got], [near((2, rows, 2 * width), BF16)] * 2)
        return kept, x_swap(send)

    def frames_of(kept, far):
        low_pair = lax.axis_index("tensor") >> 1
        for i in range(2):
            total = add(kept[i], far[i])
            for side in range(2):
                yield (low_pair ^ i) * 2 + side, total[:, side * width : (side + 1) * width]

    def attend_weight_half_kernel(ga, gb, la, lb, ma, mb, ba, bb, out):
        for c in range(3):
            at = slice(c * width, (c + 1) * width)
            out[at, :] = tn(ga[c], la[...])
            out[at, :] += tn(gb[c], lb[...])
        out[3 * width :, :] = tn(ma[...], ba[...])
        out[3 * width :, :] += tn(mb[...], bb[...])

    def pack_kernel(s0, s1, s2, s3, two, p0, p1, p2, p3, out, acc):
        ten = lax.axis_index("tensor")
        acc[...] = jnp.zeros_like(acc)
        for s, ref in enumerate((s0, s1, s2, s3)):
            acc[pl.ds(ten ^ s, 1), :] = ref[0:1, :]
        acc[4:6, :] = s0[1:3, :] + s1[1:3, :] + s2[1:3, :] + s3[1:3, :]
        acc[6:10, :] = two[0:4, :]
        acc[pl.ds(10 + ten, 1), :] = p0[...] + p1[...] + p2[...] + p3[...]
        acc[pl.ds(14 + ten, 1), :] = s0[3:4, :] + s1[3:4, :] + s2[3:4, :] + s3[3:4, :]
        out[...] = acc[...].astype(BF16)

    def attend_weight_kernel(so_far, ga, gb, la, lb, ma, mb, ba, bb, keep, send, acc):
        for c in range(3):
            at = slice(c * width, (c + 1) * width)
            acc[at, :] = so_far[at, :] + tn(ga[c], la[...])
            acc[at, :] += tn(gb[c], lb[...])
        acc[3 * width :, :] = so_far[3 * width :, :] + tn(ma[...], ba[...])
        acc[3 * width :, :] += tn(mb[...], bb[...])
        halves_of(acc, keep, send)

    def merge_kernel(mine, other, out):
        a, b = mine[...].astype(F32), other[...].astype(F32)
        early = lax.axis_index("pipe") == 0
        out[...] = jnp.concatenate(
            [
                jnp.where(early, a[:half], b[:half]),
                jnp.where(early, b[:half], a[:half]),
                a[half : half + 24] + b[half : half + 24],
            ],
            axis=0,
        ).astype(BF16)

    def message_back(*refs):
        pack_refs, refs = refs[:pack_blocks], refs[pack_blocks:]
        (first, q, k, v, probs, w, wo, vrow, sent_o, grads_o, back_o) = refs
        sent = jnp.concatenate(
            [clip_block(pack_refs, c, pack_rows).astype(F32)[:frame_count] for c in range(clips)],
            axis=0,
        )
        low = sent.astype(BF16)
        sent_o[...] = sent
        grad_mixed = nt(low, wo[...]).astype(BF16)
        dq = jnp.zeros((all_rows, width), F32)
        dk = jnp.zeros((all_rows, width), F32)
        dv = jnp.zeros((all_rows, width), F32)
        for h, mask in enumerate(head_masks(all_rows)):
            grad_head = only(mask, grad_mixed)
            wide = probs[h]
            dv = dv + tn(wide.astype(BF16), grad_head)
            grad_probs = nt(grad_head, v[...])
            inner = jnp.sum(wide * grad_probs, axis=-1, keepdims=True)
            grad_scores = (wide * (grad_probs - inner)).astype(BF16)
            dq = dq + only(mask, nn(grad_scores, k[...]))
            dk = dk + tn(grad_scores, only(mask, q[...]))
        dq = (dq * scale).astype(BF16)
        dk = (dk * scale).astype(BF16)
        dv = dv.astype(BF16)
        grads_o[0] = dq
        grads_o[1] = dk
        grads_o[2] = dv
        grad_low = nn(dq, w[0]) + nn(dk, w[1]) + nn(dv, w[2])
        normed, inverse = norm_parts(first[...])
        back_msg = norm_back(grad_low, normed, inverse, vrow[0:1])
        back_o[0:all_rows, :] = back_msg.astype(BF16)
        tail = jnp.concatenate(
            [row_sum(grad_low * normed), row_sum(grad_low), jnp.zeros((14, model), F32)], axis=0
        )
        back_o[all_rows:, :] = tail.astype(BF16)

    def message_weight(sent, grads_in, low, mixed, in_o, out_o, qv_o, bias_o):
        for c in range(3):
            in_o[c] = tn(grads_in[c], low[...])
        out_o[...] = tn(mixed[...], sent[...].astype(BF16))
        qv_o[0:1, :] = row_sum(grads_in[0].astype(F32))
        qv_o[1:2, :] = row_sum(grads_in[2].astype(F32))
        bias_o[...] = row_sum(sent[...])

    def block_out_kernel(*refs):
        for at, total in frames_of(*refs[:-1]):
            refs[-1][at] = total.T[:, :patch].astype(BF16)

    def message_end(*refs):
        pack_refs, refs = refs[:pack_blocks], refs[pack_blocks:]
        cls_refs, refs = refs[:blocks], refs[blocks:]
        (sent, own, late, mw, qv_in, bias_in, w_o, cls_o, vec_o, qv_o, turned, sums) = refs
        sec, ten = lax.axis_index("pipe"), lax.axis_index("tensor")
        total = jnp.where(sec == 0, own[...].astype(F32), late[...].astype(F32))
        grad_first = sent[...] + total[:all_rows]
        at = pl.ds(pl.multiple_of(ten * width, width), width)
        mine = grad_first[:16]
        high = mine.astype(BF16)
        rest = (mine - high.astype(F32)).astype(BF16)
        mw_rows = mw[at, :]
        cls_o[...] = nt(high, mw_rows) + nt(rest, mw_rows)
        turned[...] = grad_first.T
        mine = turned[at, :]
        high = mine.astype(BF16)
        rest = (mine - high.astype(F32)).astype(BF16)
        cls = jnp.concatenate([clip_block(cls_refs, c, frame_count).astype(F32) for c in range(clips)])
        cls = cls.astype(BF16)
        w_o[...] = nn(high, cls) + nn(rest, cls)
        summed = clip_block(pack_refs, 0, pack_rows).astype(F32)
        for c in range(1, clips):
            summed = summed + clip_block(pack_refs, c, pack_rows).astype(F32)
        sums[...] = summed[frame_count:]
        first_one = sec == 0
        vec_o[0:1, :] = jnp.where(first_one, total[all_rows : all_rows + 1], sums[0:1])
        vec_o[1:2, :] = jnp.where(first_one, total[all_rows + 1 : all_rows + 2], sums[1:2])
        vec_o[2:3, :] = jnp.where(first_one, bias_in[...], sums[4:5])
        vec_o[3:4, :] = sums[2:3]
        vec_o[4:5, :] = sums[3:4]
        vec_o[5:6, :] = sums[5:6]
        vec_o[6:7, :] = sums[pl.ds(6 + ten, 1), :]
        vec_o[7:8, :] = row_sum(grad_first)
        qv_row = sums[pl.ds(10 + ten, 1), :]
        qv_o[0:1, :] = jnp.where(first_one, qv_in[0:1], qv_row[:, :width])
        qv_o[1:2, :] = jnp.where(first_one, qv_in[1:2], qv_row[:, 256 : 256 + width])

    def frames_grad_kernel(*refs):
        cls, out = refs[-2:]
        top = lax.broadcasted_iota(jnp.int32, (rows, width), 0) == 0
        for at, total in frames_of(*refs[:-2]):
            row = cls[pl.ds(lax.axis_index("pipe") * half + at, 1), :]
            out[at] = (total + jnp.where(top, row, 0.0)).T[:, :patch].astype(BF16)

    def attend_whole_kernel(keep, other, in_zero_ref, out_zero_ref, in_o, out_o, acc):
        @pl.when(lax.axis_index("pipe") == 0)
        def _():
            in_o[...] = in_zero_ref[...]
            out_o[...] = out_zero_ref[...]

        @pl.when(lax.axis_index("pipe") == 1)
        def _():
            put_halves(keep, other, acc)
            for c in range(3):
                in_o[c] = acc[c * width : (c + 1) * width, :]
            out_o[...] = acc[3 * width :, :]

    def pack_join_kernel(a, b, out):
        size = a.shape[0]
        out[0:size, :] = a[...]
        out[size:, :] = b[...]

    stage.cost = 0
    cls_all = gather_clips(frames[0, :, 0, :])
    vectors, own_vec, near_in, in_and_vec = stage(
        small_kernel,
        [
            own_in, msg_bias, norm2_gain, norm2_shift, fc_in_bias, fc_out_bias,
            norm_gain, norm_shift, out_bias, qv_bias,
        ],
        [near((8, model), F32)] * 2 + [near(own_in.shape, BF16), near((3 * width + 16, model), BF16)],
        [pltpu.VMEM((model,), F32)] * 5
        + [pltpu.VMEM((1, model), F32)] * 3
        + [pltpu.VMEM((1, 2, width), F32), pltpu.SemaphoreType.DMA((13,))],
        far=10,
    )
    sent_in = y_early(in_and_vec)
    near_msg_w, near_out = stage(
        load_kernel, [msg_w, own_out], [near(msg_w.shape, BF16), near(own_out.shape, BF16)],
        [pltpu.SemaphoreType.DMA((2,))],
        far=2,
    )
    x_slots = slots(tokens, half)
    (first_msg, low_zero, q_zero, k_zero, v_zero, probs_zero, mixed_zero, part_zero) = stage(
        message_forward,
        [video_group, *cls_all, near_msg_w, vectors, own_vec, near_in, near_out],
        [
            near((all_rows, model), F32),
            near((all_rows, model), BF16),
            near((all_rows, width), BF16),
            near((all_rows, width), BF16),
            near((all_rows, width), BF16),
            near((heads, all_rows, all_rows), F32),
            near((all_rows, width), BF16),
            near((frame_count, model), F32),
        ],
        [pltpu.SMEM(video_group.shape, jnp.int32), pltpu.SemaphoreType.DMA],
        far=1,
    )
    from_core = core_swap(part_zero)
    sent_out = y_early(relay(near_out))
    (part_zero,) = adds((part_zero, from_core))
    from_x = x_swap(part_zero)
    (part_zero,) = adds((part_zero, from_x))
    part_late = y_late(part_zero)
    w_in, vec, *projected = stage(
        project_kernel, [*x_slots, near_in, sent_in, own_vec],
        [near(own_in.shape, BF16), near(own_vec.shape, F32)] + [near((rows, width), BF16)] * 12,
    )
    stage.cost = 4 * 10**9
    q_one, k_patch, v_patch = projected[:4], projected[4:8], projected[8:]
    msg_rows, k_msg, v_msg, w_out = stage(
        message_rows_kernel,
        [first_msg, part_zero, part_late, w_in, vec, near_out, sent_out],
        [
            near((16, model), F32), near((16, width), F32), near((16, width), F32),
            near(own_out.shape, BF16),
        ],
    )

    at3 = attend(3)
    ac3 = core_swap(at3[0])
    at2 = attend(2)
    (two,) = adds((at2[0], ac3))
    ax = x_swap(two)
    at1 = attend(1)
    ac1 = core_swap(at1[0])
    at0 = attend(0)
    g_slots = slots(grads_in, 2 * half)
    (aown,) = adds((at0[0], ac1))
    resid_own, low_own = stage(
        residual_kernel, [aown, ax, x_slots[0], vec, vectors],
        [near((rows, model), F32), near((rows, model), BF16)],
    )
    lx = x_swap(low_own)
    l1 = core_swap(low_own)
    ly = y_swap(low_own)
    g_hidden = stage(
        grad_hidden_kernel, [*g_slots[:half], fc_out], [near((rows, hidden_width), BF16)] * half,
    )
    hid0, pre0, gp0, bs0 = feed(low_own, g_hidden[0])
    hid1, pre1, gp1, bs1 = feed(l1, g_hidden[1])
    fc1 = core_swap(gp1)
    fc_out_half = own_part(own_out_kernel, (half_rows, model), hid0, hid1, g_slots[0], g_slots[1])
    (fown,) = adds((gp0, fc1))
    l2 = relay(lx)
    l3 = core_swap(l2)
    ly2 = y_swap(l2)
    hid2, pre2, gp2, bs2 = feed(l2, g_hidden[2])
    hid3, pre3, gp3, bs3 = feed(l3, g_hidden[3])
    fc3 = core_swap(gp3)
    m0 = relay(ly)
    m1 = core_swap(m0)
    (two,) = adds((gp2, fc3))
    fx = x_swap(two)
    ho0, po0 = feed_other(m0, g_slots[4])
    ho1, po1 = feed_other(m1, g_slots[5])
    fc_in_half = own_part(own_in_kernel, (model, half_rows), low_own, l1, pre0, pre1)
    block_parts = stage(
        mlp_kernel, [hid0, hid1, hid2, hid3, fc_out, resid_own, vectors],
        [near((rows, model), BF16)] * half,
    )
    grad_resid, grad_low, small_two = stage(
        residual_back_kernel, [fown, fx, resid_own, g_slots[0], vectors],
        [near((rows, model), F32), near((rows, model), BF16), near((8, model), F32)],
    )
    bx = x_swap(grad_low)
    b1 = core_swap(grad_low)
    m2 = relay(ly2)
    m3 = core_swap(m2)
    ho2, po2 = feed_other(m2, g_slots[6])
    ho3, po3 = feed_other(m3, g_slots[7])
    p0 = whole_part(
        sum_out_kernel, fc_out_half, hid2, hid3, g_slots[2], g_slots[3], ho0, ho1, ho2, ho3, *g_slots[half:],
    )
    q0 = whole_part(
        sum_in_kernel, fc_in_half, l2, l3, pre2, pre3, m0, m1, m2, m3, po0, po1, po2, po3,
    )
    ba0, gr0, lo0, sm0 = attend_back(0, grad_low, at0)
    ba1, gr1, lo1, sm1 = attend_back(1, b1, at1)
    (attend_half,) = stage(
        attend_weight_half_kernel, [gr0, gr1, lo0, lo1, at0[1], at1[1], grad_low, b1],
        [near((4 * width, model), F32)],
    )
    b2 = relay(bx)
    b3 = core_swap(b2)
    ba2, gr2, lo2, sm2 = attend_back(2, b2, at2)
    p1 = over_far_clip(*p0)
    ba3, gr3, lo3, sm3 = attend_back(3, b3, at3)
    (pk0,) = stage(
        pack_kernel, [sm0, sm1, sm2, sm3, small_two, bs0, bs1, bs2, bs3], [near((32, model), BF16)],
        [pltpu.VMEM((32, model), F32)],
    )
    pkc = core_swap(pk0)
    r0 = over_sections(
        *stage(
            attend_weight_kernel,
            [attend_half, gr2, gr3, lo2, lo3, at2[1], at3[1], b2, b3],
            half_shapes,
            [pltpu.VMEM((4 * width, model), F32)],
        )
    )
    (pk1,) = adds((pk0, pkc))
    pkx = x_swap(pk1)
    q1 = over_far_clip(*q0)
    p2 = to_far_clip(*p1)
    (pk2,) = adds((pk1, pkx))
    pky = y_swap(pk2)
    r1 = over_near_clip(*r0)
    q2 = to_far_clip(*q1)
    (pk3,) = stage(merge_kernel, [pk2, pky], [near((32, model), BF16)])
    pack_rows = pk3.shape[0]
    pkz = z_swap(pk3, 1) if ring else None
    p3 = to_near_clip(*p2)
    r2 = over_far_clip(*r1)
    if ring:
        (pk4,) = stage(pack_join_kernel, [pk3, pkz], [near((2 * pack_rows, model), BF16)])
        packs = [pk4, z_swap(pk4, 2)]
    else:
        packs = gather_clips(pk3)
    q3 = to_near_clip(*q2)
    p4 = to_other_section(*p3)
    sent_all, grads_zero, bz0 = stage(
        message_back,
        [*packs, first_msg, q_zero, k_zero, v_zero, probs_zero, near_in, near_out, own_vec],
        [
            near((all_rows, model), F32),
            near((3, all_rows, width), BF16),
            near((all_rows + 16, model), BF16),
        ],
    )
    bzc = core_swap(bz0)
    in_zero, out_zero, qv_zero, bias_zero = stage(
        message_weight, [sent_all, grads_zero, low_zero, mixed_zero],
        [
            near((3, width, model), F32),
            near((width, model), F32),
            near((2, width), F32),
            near((1, model), F32),
        ],
    )
    (bz1,) = adds((bz0, bzc))
    bzx = x_swap(bz1)
    r3 = to_far_clip(*r2)
    q4 = to_other_section(*q3)
    (bz2,) = adds((bz1, bzx))
    bzy = y_late(bz2)
    ck, send = stage(column_kernel, [ba0, ba1, ba2, ba3], column_shapes)
    cs = core_swap(send)
    fc_out_grad = whole(*p4)
    msg_w_grad, cls_part, vec_grads, qv_grad = stage(
        message_end,
        [*packs, *cls_all, sent_all, bz2, bzy, near_msg_w, qv_zero, bias_zero],
        [
            shape_of((width, model), F32),
            near((16, width), F32),
            near((8, model), F32),
            near((2, width), F32),
        ],
        [pltpu.VMEM((model, all_rows), F32), pltpu.VMEM((24, model), F32)],
    )
    kept, far = far_columns(ck, cs)
    r4 = to_near_clip(*r3)
    (frames_grad,) = stage(
        frames_grad_kernel, [kept, far, cls_part], [shape_of((half, width, patch), BF16)],
    )
    bk, send = stage(column_kernel, block_parts, column_shapes)
    bcs = core_swap(send)
    r5 = to_sections(*r4, move=y_late)
    fc_in_grad = whole_of_columns(*q4)
    bkept, bfar = far_columns(bk, bcs)
    (block_out,) = stage(
        block_out_kernel, [bkept, bfar], [shape_of((half, width, patch), BF16)],
    )
    attn_in_grad, attn_out_grad = stage(
        attend_whole_kernel, [*r5, in_zero, out_zero],
        [shape_of((3, width, model), F32), shape_of((width, model), F32)],
        [pltpu.VMEM((4 * width, model), F32)],
    )

    return (
        jnp.swapaxes(block_out, 1, 2)[None],
        jnp.swapaxes(frames_grad, 1, 2)[None],
        msg_w_grad.T,
        vec_grads[7],
        vec_grads[0:1],
        vec_grads[1:2],
        jnp.transpose(attn_in_grad, (2, 0, 1))[None],
        qv_grad[None],
        attn_out_grad[None],
        vec_grads[2:3],
        vec_grads[3],
        vec_grads[4],
        fc_in_grad,
        vec_grads[6],
        fc_out_grad,
        vec_grads[5],
    )


def solution(mesh):
    return jax.shard_map(
        body,
        mesh=mesh,
        in_specs=(
            P("dp", None, None, None),
            P(),
            P(),
            P(),
            P("pipe", None),
            P("pipe", None),
            P("pipe", None, None, "tensor"),
            P("pipe", None, "tensor"),
            P("pipe", "tensor", None),
            P("pipe", None),
            P(),
            P(),
            P(None, "tensor"),
            P("tensor"),
            P("tensor", None),
            P(),
            P("dp", None, None, None),
        ),
        out_specs=(
            P("dp", "pipe", None, "tensor"),
            P("dp", "pipe", None, "tensor"),
            P(None, "tensor"),
            P(),
            P("pipe", None),
            P("pipe", None),
            P("pipe", None, None, "tensor"),
            P("pipe", None, "tensor"),
            P("pipe", "tensor", None),
            P("pipe", None),
            P(),
            P(),
            P(None, "tensor"),
            P("tensor"),
            P("tensor", None),
            P(),
        ),
        check_vma=False,
    )
```

```python
import functools

import jax
import jax.numpy as jnp
from jax import lax
from jax.experimental import pallas as pl
from jax.experimental.pallas import tpu as pltpu
from jax.sharding import PartitionSpec as P

HEAD_DIM = 64
EPSILON = 1e-05
QUICK_GELU = 1.702
F32 = jnp.float32
BF16 = jnp.bfloat16
VMEM_BYTES = 16 * 1024 * 1024


def nn(left, right):
    return lax.dot_general(left, right, (((1,), (0,)), ((), ())), preferred_element_type=F32)


def nt(left, right):
    return lax.dot_general(left, right, (((1,), (1,)), ((), ())), preferred_element_type=F32)


def tn(left, right):
    return lax.dot_general(left, right, (((0,), (0,)), ((), ())), preferred_element_type=F32)


def norm_parts(values_in):
    centred = values_in - jnp.mean(values_in, axis=-1, keepdims=True)
    inverse = lax.rsqrt(jnp.mean(centred * centred, axis=-1, keepdims=True) + EPSILON)
    return centred * inverse, inverse


def norm_back(incoming, normed, inverse, gain):
    weighted = incoming * gain
    centred = weighted - jnp.mean(weighted, axis=-1, keepdims=True)
    return inverse * (centred - normed * jnp.mean(weighted * normed, axis=-1, keepdims=True))


def row_sum(values_in):
    return jnp.sum(values_in, axis=0, keepdims=True)


def shape_of(shape, kind):
    return jax.ShapeDtypeStruct(shape, kind)


def near(shape, kind):
    return pltpu.VMEM(shape, kind)


class Chain:
    def __init__(self):
        self.token = None
        self.near, self.kept = set(), []
        self.cost = 4 * 10**9

    def __call__(self, kernel, ins, outs, scratch=(), flops=0, far=0):
        tokens = 0 if self.token is None else 1
        count, given = len(ins), len(outs)

        def stage(*refs):
            rest = refs[tokens:]
            kernel(*rest[:count], *rest[count : count + given], *rest[count + given + 1 :])

        vmem = pl.BlockSpec(memory_space=pltpu.VMEM)
        held = [] if self.token is None else [self.token]
        ins = [
            pltpu.with_memory_space_constraint(a, pltpu.HBM)
            if i < far
            else pltpu.with_memory_space_constraint(a, pltpu.VMEM)
            if id(a) in self.near
            else a
            for i, a in enumerate(ins)
        ]
        results = pl.pallas_call(
            stage,
            out_shape=[*outs, near((8, 128), F32)],
            in_specs=[pl.BlockSpec(memory_space=pl.ANY)] * tokens
            + [pl.BlockSpec(memory_space=pltpu.HBM)] * far
            + [vmem] * (count - far),
            out_specs=[vmem] * (given + 1),
            scratch_shapes=list(scratch),
            compiler_params=pltpu.CompilerParams(vmem_limit_bytes=VMEM_BYTES),
            cost_estimate=pl.CostEstimate(flops=self.cost, bytes_accessed=0, transcendentals=0),
        )(*held, *ins)
        self.token = results[-1]
        self.kept += results
        for out, result in zip(outs, results):
            if not isinstance(out, jax.ShapeDtypeStruct):
                self.near.add(id(result))
        return results[:-1]


def body(
    frames,
    video_group,
    msg_w,
    msg_bias,
    norm_gain,
    norm_shift,
    attn_in,
    qv_bias,
    attn_out,
    out_bias,
    norm2_gain,
    norm2_shift,
    fc_in,
    fc_in_bias,
    fc_out,
    fc_out_bias,
    cotangent,
):
    _, frame_count, patch, model = frames.shape

    width = attn_in.shape[-1]

    hidden_width = fc_in.shape[-1]

    heads = width // HEAD_DIM

    clips = lax.axis_size("dp")

    half = frame_count // 2

    rows = -(-(patch + 1) // 16) * 16

    all_rows = clips * frame_count

    scale = HEAD_DIM ** (-0.5)

    pipe = lax.axis_index("pipe")

    tensor = lax.axis_index("tensor")

    clip = lax.axis_index("dp")

    ring = clips == 4

    stage = Chain()

    quarter = hidden_width // 4

    assert quarter == width and hidden_width == model and half == 4

    def tensor_swap(v, bit):
        return lax.ppermute(v, "tensor", [(i, i ^ bit) for i in range(4)])

    def core_swap(v):
        return tensor_swap(v, 1)

    def x_swap(v):
        return tensor_swap(v, 2)

    def y_swap(v):
        return lax.ppermute(v, "pipe", [(0, 1), (1, 0)])

    def y_late(v):
        return lax.ppermute(v, "pipe", [(0, 1)])

    def y_early(v):
        return lax.ppermute(v, "pipe", [(1, 0)])

    def z_swap(v, bit):
        return lax.ppermute(v, "dp", [(i, i ^ bit) for i in range(clips)])

    def gather_clips(v):
        if ring:
            return [v] + [z_swap(v, apart) for apart in range(1, clips)]
        every = lax.all_gather(v, "dp")
        every = lax.dynamic_slice_in_dim(jnp.concatenate([every, every]), clip, clips, 0)
        return [every.reshape(clips * v.shape[0], v.shape[1])]

    def clip_block(refs, c, size):
        each = clips // len(refs)
        at = c % each * size
        return refs[c // each][at : at + size, :]

    blocks = clips if ring else 1

    pack_blocks = 2 if ring else 1

    def head_masks(n):
        lane = lax.broadcasted_iota(jnp.int32, (n, width), 1)
        return [(lane >= h * HEAD_DIM) & (lane < (h + 1) * HEAD_DIM) for h in range(heads)]

    def only(mask, v):
        return jnp.where(mask, v, jnp.zeros_like(v))

    def add(*terms):
        total = terms[0].astype(F32)
        for term in terms[1:]:
            total = total + term.astype(F32)
        return total

    def adds(*groups):
        sizes = [len(group) for group in groups]

        def kernel(*refs):
            at = 0
            for size, out in zip(sizes, refs[sum(sizes) :]):
                out[...] = add(*[ref[...] for ref in refs[at : at + size]]).astype(out.dtype)
                at += size

        return stage(
            kernel,
            [array for group in groups for array in group],
            [near(group[0].shape, group[0].dtype) for group in groups],
        )

    own_in = jnp.transpose(attn_in[0], (1, 2, 0))

    own_out = attn_out[0]

    tokens = jnp.transpose(frames[0], (1, 0, 2))

    grads_in = jnp.transpose(cotangent[0], (1, 0, 2))

    def small_kernel(*refs):
        ins, vecs_o, own_o, in_o, both_o = refs[:10], *refs[10:14]
        lines, rest, sem = refs[14:19], refs[19:23], refs[23]
        pairs = [(ins[0], in_o)] + list(zip(ins[1:], (*lines, *rest)))
        pairs += [(ins[0].at[c], both_o.at[c * width : (c + 1) * width]) for c in range(3)]
        copies = [pltpu.make_async_copy(a, b, sem.at[i]) for i, (a, b) in enumerate(pairs)]
        for copy in copies:
            copy.start()
        for copy in copies:
            copy.wait()
        for i, line in enumerate(lines):
            vecs_o[i : i + 1, :] = line[...].reshape(1, model)
        for i, line in enumerate(rest[:3]):
            own_o[i : i + 1, :] = line[...]
        own_o[3:8, :] = jnp.zeros((5, model), F32)
        own_o[3:5, 0:width] = rest[3][0]
        high = own_o[...].astype(BF16).astype(F32)
        both_o[3 * width :, :] = jnp.concatenate([high, own_o[...] - high], axis=0).astype(BF16)

    def load_kernel(*refs):
        sem = refs[4]
        copies = [
            pltpu.make_async_copy(a, b, sem.at[i]) for i, (a, b) in enumerate(zip(refs[:2], refs[2:4]))
        ]
        for copy in copies:
            copy.start()
        for copy in copies:
            copy.wait()

    tokens_all = rows * frame_count

    lanes = 128

    def slot_kernel(v, *refs):
        outs, (wide, held, sem) = refs[:-3], refs[-3:]
        copy = pltpu.make_async_copy(v, held, sem)
        copy.start()
        copy.wait()
        flat = held[...].astype(F32).reshape(patch * frame_count, model)
        sec, ten = lax.axis_index("pipe"), lax.axis_index("tensor")
        for c in range(model // lanes):
            at = c * tokens_all
            wide[at : at + patch * frame_count, :] = flat[:, c * lanes : (c + 1) * lanes]
            wide[at + patch * frame_count : at + tokens_all, :] = jnp.zeros(
                ((rows - patch) * frame_count, lanes), F32
            )
            for s, out in enumerate(outs):
                frame = at + (sec if s < half else 1 - sec) * half + (ten ^ (s % half))
                out[:, c * lanes : (c + 1) * lanes] = wide[
                    pl.ds(frame, rows, stride=frame_count), :
                ].astype(BF16)

    def slots(v, count):
        return stage(
            slot_kernel,
            [v],
            [near((rows, model), BF16)] * count,
            [
                pltpu.VMEM((model // lanes * tokens_all, lanes), F32),
                pltpu.VMEM((patch, frame_count, model), BF16),
                pltpu.SemaphoreType.DMA,
            ],
            far=1,
        )

    def message_forward(groups, *refs):
        cls_refs, refs = refs[:blocks], refs[blocks:]
        (mw, vecs, vrow, w, wo, first_o, low_o, q_o, k_o, v_o, probs_o, mixed_o, part_o, ids, sem) = refs
        copy = pltpu.make_async_copy(groups, ids, sem)
        copy.start()
        cls = jnp.concatenate([clip_block(cls_refs, c, frame_count).astype(F32) for c in range(clips)])
        first = nn(cls.astype(BF16), mw[...]) + vecs[0:1]
        first_o[...] = first
        normed, _ = norm_parts(first)
        low = (normed * vrow[0:1] + vrow[1:2]).astype(BF16)
        low_o[...] = low
        q = (nt(low, w[0]) + vrow[3:4, :width]).astype(BF16)
        k = nt(low, w[1]).astype(BF16)
        v = (nt(low, w[2]) + vrow[4:5, :width]).astype(BF16)
        q_o[...] = q
        k_o[...] = k
        v_o[...] = v
        of_row = lax.broadcasted_iota(jnp.int32, (all_rows, all_rows), 0) // frame_count
        of_col = lax.broadcasted_iota(jnp.int32, (all_rows, all_rows), 1) // frame_count
        mine = lax.axis_index("dp")
        copy.wait()
        row_id = jnp.zeros((all_rows, all_rows), jnp.int32)
        col_id = jnp.zeros((all_rows, all_rows), jnp.int32)
        for c in range(clips):
            mark = ids[mine ^ c if ring else lax.rem(mine + c, clips)]
            row_id = jnp.where(of_row == c, mark, row_id)
            col_id = jnp.where(of_col == c, mark, col_id)
        allowed = row_id == col_id
        mixed = jnp.zeros((all_rows, width), F32)
        for h, mask in enumerate(head_masks(all_rows)):
            scores = jnp.where(allowed, nt(only(mask, q), k) * scale, -jnp.inf)
            exponent = jnp.exp(scores - jnp.max(scores, axis=-1, keepdims=True))
            probs = exponent / jnp.sum(exponent, axis=-1, keepdims=True)
            probs_o[h] = probs
            mixed = mixed + only(mask, nn(probs.astype(BF16), v))
        mixed = mixed.astype(BF16)
        mixed_o[...] = mixed
        part = nn(mixed, wo[...]) + jnp.where(lax.axis_index("tensor") == 0, vrow[2:3], 0.0)
        part_o[...] = part[:frame_count]

    def project_kernel(x0, x1, x2, x3, wa, wb, va, w, vrow, *outs):
        early = lax.axis_index("pipe") == 0
        for c in range(3):
            w[c] = jnp.where(early, wb[c * width : (c + 1) * width, :], wa[c])
        sent = wb[3 * width :, :].astype(F32)
        vrow[...] = jnp.where(early, sent[0:8] + sent[8:16], va[...])
        gain, shift = vrow[0:1], vrow[1:2]
        for s, x in enumerate((x0, x1, x2, x3)):
            normed, _ = norm_parts(x[...].astype(F32))
            low = (normed * gain + shift).astype(BF16)
            outs[s][...] = (nt(low, w[0]) + vrow[3:4, :width]).astype(BF16)
            outs[half + s][...] = nt(low, w[1]).astype(BF16)
            outs[2 * half + s][...] = (nt(low, w[2]) + vrow[4:5, :width]).astype(BF16)

    def message_rows_kernel(first, part, late, w, vrow, wa, wb, msg_o, k_o, v_o, w_o):
        sec, ten = lax.axis_index("pipe"), lax.axis_index("tensor")
        w_o[...] = jnp.where(sec == 0, wb[...], wa[...])
        msg_o[...] = jnp.zeros_like(msg_o)
        for s in range(half):
            at = pl.ds(sec * half + (ten ^ s), 1)
            summed = jnp.where(sec == 0, part[at, :], late[at, :])
            msg_o[s : s + 1, :] = (first[at, :] + summed).astype(BF16).astype(F32)
        normed, _ = norm_parts(msg_o[...])
        low = (normed * vrow[0:1] + vrow[1:2]).astype(BF16)
        k_o[...] = nt(low, w[1])
        v_o[...] = nt(low, w[2]) + vrow[4:5, :width]

    def attend_kernel(
        s, q, k, v, km, vm, wo, part_o, mixed_o, probs_o, k_o, v_o,
    ):
        here = lax.broadcasted_iota(jnp.int32, (rows, width), 0) == patch
        key_here = lax.broadcasted_iota(jnp.int32, (rows, rows), 1) <= patch
        kk = jnp.where(here, km[s : s + 1], k[...].astype(F32)).astype(BF16)
        vv = jnp.where(here, vm[s : s + 1], v[...].astype(F32)).astype(BF16)
        k_o[...] = kk
        v_o[...] = vv
        mixed = jnp.zeros((rows, width), F32)
        for h, mask in enumerate(head_masks(rows)):
            scores = nt(only(mask, q[...]), kk) * scale
            scores = jnp.where(key_here, scores, -jnp.inf)
            exponent = jnp.exp(scores - jnp.max(scores, axis=-1, keepdims=True))
            probs = exponent * (1.0 / jnp.sum(exponent, axis=-1, keepdims=True))
            probs = probs.astype(BF16)
            probs_o[h] = probs
            mixed = mixed + only(mask, nn(probs, vv))
        mixed = mixed.astype(BF16)
        mixed_o[...] = mixed
        part_o[...] = nn(mixed, wo[...]).astype(BF16)

    def attend(s):
        return stage(
            functools.partial(attend_kernel, s),
            [q_one[s], k_patch[s], v_patch[s], k_msg, v_msg, w_out],
            [
                near((rows, model), BF16),
                near((rows, width), BF16),
                near((heads, rows, rows), BF16),
                near((rows, width), BF16),
                near((rows, width), BF16),
            ],
            flops=2 * rows * (width * model + 2 * heads * rows * HEAD_DIM),
        )

    first_rows = rows // 32 * 16 + 16

    row_parts = (slice(0, first_rows), slice(first_rows, rows))

    def add_parts(a, b):
        def kernel(a_ref, b_ref, *outs):
            for at, out in zip(row_parts, outs):
                out[...] = add(a_ref[at, :], b_ref[at, :]).astype(BF16)

        return stage(
            kernel, [a, b], [near((at.stop - at.start, model), BF16) for at in row_parts]
        )

    def join_parts(a, b):
        def kernel(a_ref, b_ref, out):
            for at, ref in zip(row_parts, (a_ref, b_ref)):
                out[at, :] = ref[...]

        return stage(kernel, [a, b], [near((rows, model), a.dtype)])[0]

    def residual_of(at, a, b, x, vrow, vecs):
        resid = x[at, :].astype(F32) + add(a[at, :], b[...]) + vrow[2:3]
        normed, _ = norm_parts(resid)
        return resid, (normed * vecs[1:2] + vecs[2:3]).astype(BF16)

    def residual_first_kernel(a, b, x, vrow, vecs, resid_o, low_o):
        resid_o[...], low_o[...] = residual_of(row_parts[0], a, b, x, vrow, vecs)

    def residual_last_kernel(a, b, x, vrow, vecs, resid_in, low_in, resid_o, low_o, part_o):
        resid, low = residual_of(row_parts[1], a, b, x, vrow, vecs)
        for at, one, two in zip(row_parts, (resid_in[...], resid), (low_in[...], low)):
            resid_o[at, :] = one
            low_o[at, :] = two
        part_o[...] = low

    def relay_kernel(v, out):
        out[...] = v[...]

    def relay(v):
        return stage(relay_kernel, [v], [near(v.shape, v.dtype)])[0]

    def grad_hidden_kernel(g0, g1, g2, g3, w, *outs):
        for g, out in zip((g0, g1, g2, g3), outs):
            out[...] = nt(g[...], w[...]).astype(BF16)

    def feed_kernel(low, gh, w, vecs, hid_o, pre_o, grad_o, bias_o):
        hidden_in = nn(low[...], w[...]) + vecs[3:4]
        sig = 1.0 / (1.0 + jnp.exp(-QUICK_GELU * hidden_in))
        hid_o[...] = (hidden_in * sig).astype(BF16)
        slope = sig + QUICK_GELU * hidden_in * sig * (1.0 - sig)
        pre = (gh[...].astype(F32) * slope).astype(BF16)
        pre_o[...] = pre
        grad_o[...] = nt(pre, w[...]).astype(BF16)
        bias_o[...] = row_sum(pre.astype(F32))

    def feed(low, gh):
        return stage(
            feed_kernel, [low, gh, fc_in, vectors],
            [
                near((rows, hidden_width), BF16),
                near((rows, hidden_width), BF16),
                near((rows, model), BF16),
                near((1, hidden_width), F32),
            ],
            flops=2 * 2 * rows * model * hidden_width,
        )

    half_rows, eighth = model // 2, model // 8

    def halves_of(acc, keep, send):
        sec = lax.axis_index("pipe")
        for out, at in ((keep, sec), (send, 1 - sec)):
            start = pl.multiple_of(at * half_rows, half_rows)
            out[...] = acc[pl.ds(start, half_rows), :].astype(BF16)

    half_shapes = [near((half_rows, model), BF16)] * 2

    def section_columns():
        return pl.ds(pl.multiple_of(lax.axis_index("pipe") * half_rows, half_rows), half_rows)

    def feed_other_kernel(low, g, w, w_out, vecs, hid_o, pre_o):
        columns = section_columns()
        hidden_in = nn(low[...], w[:, columns]) + vecs[3:4, columns]
        sig = 1.0 / (1.0 + jnp.exp(-QUICK_GELU * hidden_in))
        hid_o[...] = (hidden_in * sig).astype(BF16)
        slope = sig + QUICK_GELU * hidden_in * sig * (1.0 - sig)
        pre_o[...] = (nt(g[...], w_out[columns, :]).astype(BF16).astype(F32) * slope).astype(BF16)

    def feed_other(low, g):
        return stage(
            feed_other_kernel, [low, g, fc_in, fc_out, vectors],
            [near((rows, half_rows), BF16)] * 2,
        )

    def own_out_kernel(h0, h1, g0, g1, out):
        out[...] = tn(h0[:, section_columns()], g0[...])
        out[...] += tn(h1[:, section_columns()], g1[...])

    def own_in_kernel(l0, l1, p0, p1, out):
        out[...] = tn(l0[...], p0[:, section_columns()])
        out[...] += tn(l1[...], p1[:, section_columns()])

    def own_part(kernel, shape, *ins):
        return stage(kernel, list(ins), [near(shape, F32)])[0]

    def clip_parts(acc, mine, send):
        size = mine.shape[0] // 2
        for out, first in ((mine, 0), (send, 1)):
            for at, apart in ((0, first), (size, first ^ 2)):
                out[at : at + size, :] = acc[clip_rows(apart, size), :].astype(BF16)

    def sum_out_kernel(part, h2, h3, g2, g3, o0, o1, o2, o3, q0, q1, q2, q3, mine, send, acc):
        acc[...] = part[...] + tn(h2[:, section_columns()], g2[...])
        acc[...] += tn(h3[:, section_columns()], g3[...])
        for o, q in ((o0, q0), (o1, q1), (o2, q2), (o3, q3)):
            acc[...] += tn(o[...], q[...])
        clip_parts(acc, mine, send)

    def sum_in_kernel(part, l2, l3, p2, p3, m0, m1, m2, m3, q0, q1, q2, q3, mine, send, acc):
        acc[...] = part[...] + tn(l2[...], p2[:, section_columns()])
        acc[...] += tn(l3[...], p3[:, section_columns()])
        for m, q in ((m0, q0), (m1, q1), (m2, q2), (m3, q3)):
            acc[...] += tn(m[...], q[...])
        clip_parts(acc, mine, send)

    def whole_part(kernel, part, *ins):
        rows_in, columns = part.shape
        mine, send = stage(
            kernel, [part, *ins], [near((rows_in // 2, columns), BF16)] * 2,
            [pltpu.VMEM((rows_in, columns), F32)],
        )
        return mine, z_swap(send, 1) if ring else send

    def over_sections(keep, send):
        return keep, y_swap(send) if ring else send

    def clip_rows(apart, size=eighth):
        here = lax.axis_index("dp") if ring else 0
        return pl.ds(pl.multiple_of((here ^ apart) * size, size), size)

    def over_near_clip(keep, got):
        if not ring:
            return keep, got

        def kernel(a, b, mine, send, acc):
            acc[...] = add(a[...], b[...])
            for out, first in ((mine, 0), (send, 1)):
                out[0:eighth, :] = acc[clip_rows(first), :].astype(BF16)
                out[eighth:, :] = acc[clip_rows(first ^ 2), :].astype(BF16)

        mine, send = stage(
            kernel, [keep, got], [near((2 * eighth, model), BF16)] * 2,
            [pltpu.VMEM((half_rows, model), F32)],
        )
        return mine, z_swap(send, 1)

    def over_far_clip(mine, got):
        if not ring:
            return mine, got
        size = mine.shape[0] // 2

        def kernel(a, b, own, send):
            own[...] = add(a[0:size, :], b[0:size, :]).astype(BF16)
            send[...] = add(a[size:, :], b[size:, :]).astype(BF16)

        own, send = stage(kernel, [mine, got], [near((size, mine.shape[1]), BF16)] * 2)
        return own, z_swap(send, 2)

    def to_far_clip(own, got):
        if not ring:
            return own, got
        (own,) = adds((own, got))
        return own, z_swap(own, 2)

    def to_near_clip(own, got):
        if not ring:
            return own, got

        size = own.shape[0]

        def kernel(a, b, out):
            out[0:size, :] = a[...]
            out[size:, :] = b[...]

        (both,) = stage(kernel, [own, got], [near((2 * size, own.shape[1]), BF16)])
        return both, z_swap(both, 1)

    def join_kernel(a, b, out):
        size = a.shape[0] // 2
        for apart, ref, at in ((0, a, 0), (2, a, size), (1, b, 0), (3, b, size)):
            out[clip_rows(apart, size), :] = ref[at : at + size, :]

    def to_sections(both, got, move=y_swap):
        if not ring:
            sec = lax.axis_index("pipe")
            early = jnp.where(sec == 0, both, got)
            later = jnp.where(sec == 0, got, both)
            early, later = lax.psum((early, later), ("pipe", "dp"))
            return jnp.where(sec == 0, early, later), jnp.where(sec == 0, later, early)
        (summed,) = stage(join_kernel, [both, got], [near((half_rows, model), BF16)])
        return summed, move(summed)

    def to_other_section(both, got):
        if not ring:
            both, got = lax.psum((both, got), "dp")
        (summed,) = stage(join_kernel, [both, got], [near((2 * both.shape[0], both.shape[1]), BF16)])
        return summed, y_swap(summed)

    def put_halves(keep, other, out):
        sec = lax.axis_index("pipe")
        for ref, at in ((keep, sec), (other, 1 - sec)):
            start = pl.multiple_of(at * half_rows, half_rows)
            out[pl.ds(start, half_rows), :] = ref[...].astype(F32)

    def whole(keep, other):
        return stage(put_halves, [keep, other], [shape_of((model, model), F32)])[0]

    def put_columns(keep, other, out):
        sec = lax.axis_index("pipe")
        for ref, at in ((keep, sec), (other, 1 - sec)):
            start = pl.multiple_of(at * half_rows, half_rows)
            out[:, pl.ds(start, half_rows)] = ref[...].astype(F32)

    def whole_of_columns(keep, other):
        return stage(put_columns, [keep, other], [shape_of((model, model), F32)])[0]

    def residual_back_of(at, a, b, resid, g, vecs):
        incoming = add(a[at, :], b[...])
        normed, inverse = norm_parts(resid[at, :])
        real = lax.broadcasted_iota(jnp.int32, incoming.shape, 0) < patch - at.start
        incoming = jnp.where(real, incoming, 0.0)
        from_out = g[at, :].astype(F32)
        grad = from_out + norm_back(incoming, normed, inverse, vecs[1:2])
        grad = jnp.where(real, grad, 0.0)
        low = grad.astype(BF16)
        sums = [row_sum(incoming * normed), row_sum(incoming), row_sum(low.astype(F32)), row_sum(from_out)]
        return grad, low, jnp.concatenate(sums + [jnp.zeros((4, model), F32)], axis=0)

    def residual_back_first_kernel(a, b, resid, g, vecs, grad_o, low_o, small_o):
        grad_o[...], low_o[...], small_o[...] = residual_back_of(row_parts[0], a, b, resid, g, vecs)

    def residual_back_last_kernel(
        a, b, resid, g, vecs, grad_in, low_in, small_in, grad_o, low_o, part_o, small_o
    ):
        grad, low, small = residual_back_of(row_parts[1], a, b, resid, g, vecs)
        for at, one, two in zip(row_parts, (grad_in[...], grad), (low_in[...], low)):
            grad_o[at, :] = one
            low_o[at, :] = two
        part_o[...] = low
        small_o[...] = small_in[...] + small

    def column_out(values_in, slot, keep_o, send_o):
        ten = lax.axis_index("tensor")
        spot = (ten ^ slot) & 1
        for i in range(4):
            block = values_in[:, i * width : (i + 1) * width]
            apart = ten ^ i
            for out, odd in ((keep_o, 0), (send_o, 1)):
                for side in range(2):

                    @pl.when(((apart & 1) == odd) & (spot == side))
                    def _():
                        out[apart >> 1, slot >> 1, :, side * width : (side + 1) * width] = block

    def attend_back_kernel(
        s, branch_in, q, k, v, probs, x, msg, w, vrow, wo, *refs
    ):
        extra = refs[0] if s == 0 else None
        back_o, grads_o, low_o, small_o = refs[-4:]
        gain, shift = vrow[0:1], vrow[1:2]
        here = lax.broadcasted_iota(jnp.int32, (rows, model), 0) == patch
        grad_mixed = nt(branch_in[...], wo[...]).astype(BF16)
        dq = jnp.zeros((rows, width), F32)
        dk = jnp.zeros((rows, width), F32)
        dv = jnp.zeros((rows, width), F32)
        for h, mask in enumerate(head_masks(rows)):
            grad_head = only(mask, grad_mixed)
            low_probs = probs[h]
            wide = low_probs.astype(F32)
            dv = dv + tn(low_probs, grad_head)
            grad_probs = nt(grad_head, v[...])
            inner = jnp.sum(wide * grad_probs, axis=-1, keepdims=True)
            grad_scores = (wide * (grad_probs - inner)).astype(BF16)
            dq = dq + only(mask, nn(grad_scores, k[...]))
            dk = dk + tn(grad_scores, only(mask, q[...]))
        dq = (dq * scale).astype(BF16)
        dk = (dk * scale).astype(BF16)
        dv = dv.astype(BF16)
        grads_o[0] = dq
        grads_o[1] = dk
        grads_o[2] = dv
        grad_low = nn(dq, w[0]) + nn(dk, w[1]) + nn(dv, w[2])
        token = jnp.where(here, msg[s : s + 1], x[...].astype(F32))
        normed, inverse = norm_parts(token)
        low_o[...] = (normed * gain + shift).astype(BF16)
        back = norm_back(grad_low, normed, inverse, gain)
        small_o[...] = jnp.zeros_like(small_o)
        small_o[0:1, :] = row_sum(only(here, back))
        small_o[1:2, :] = row_sum(grad_low * normed)
        small_o[2:3, :] = row_sum(grad_low)
        small_o[3:4, 0:width] = row_sum(dq.astype(F32))
        small_o[3:4, 256 : 256 + width] = row_sum(dv.astype(F32))
        if s == 0:
            back = back + extra[...]
        back_o[...] = back.astype(BF16)

    def attend_back(s, low_grad, kept):
        _, mixed, probs, k, v = kept
        ins = [low_grad, q_one[s], k, v, probs, x_slots[s], msg_rows, w_in, vec, w_out]
        return stage(
            functools.partial(attend_back_kernel, s),
            ins + ([grad_resid] if s == 0 else []),
            [
                near((rows, model), BF16),
                near((3, rows, width), BF16),
                near((rows, model), BF16),
                near((8, model), F32),
            ],
            flops=2 * rows * (4 * width * model + 4 * heads * rows * HEAD_DIM),
        )

    column_shapes = [near((2, 2, rows, 2 * width), BF16)] * 2

    def column_kernel(b0, b1, b2, b3, keep_o, send_o):
        for s, ref in enumerate((b0, b1, b2, b3)):
            column_out(ref[...], s, keep_o, send_o)

    def mlp_kernel(h0, h1, h2, h3, w, resid, vecs, *outs):
        for s, h in enumerate((h0, h1, h2, h3)):
            out = nn(h[...], w[...])
            if s == 0:
                out = out + resid[...] + vecs[4:5]
            outs[s][...] = out.astype(BF16)

    def far_columns(keep, got):
        def kernel(a, b, near_o, far_o):
            for i in range(2):
                near_o[i] = add(a[0, i], b[0, i]).astype(BF16)
                far_o[i ^ 1] = add(a[1, i], b[1, i]).astype(BF16)

        kept, send = stage(kernel, [keep, got], [near((2, rows, 2 * width), BF16)] * 2)
        return kept, x_swap(send)

    def frames_of(kept, far):
        low_pair = lax.axis_index("tensor") >> 1
        for i in range(2):
            total = add(kept[i], far[i])
            for side in range(2):
                yield (low_pair ^ i) * 2 + side, total[:, side * width : (side + 1) * width]

    def attend_weight_half_kernel(ga, gb, la, lb, ma, mb, ba, bb, out):
        for c in range(3):
            at = slice(c * width, (c + 1) * width)
            out[at, :] = tn(ga[c], la[...])
            out[at, :] += tn(gb[c], lb[...])
        out[3 * width :, :] = tn(ma[...], ba[...])
        out[3 * width :, :] += tn(mb[...], bb[...])

    def pack_kernel(s0, s1, s2, s3, two, p0, p1, p2, p3, out, acc):
        ten = lax.axis_index("tensor")
        acc[...] = jnp.zeros_like(acc)
        for s, ref in enumerate((s0, s1, s2, s3)):
            acc[pl.ds(ten ^ s, 1), :] = ref[0:1, :]
        acc[4:6, :] = s0[1:3, :] + s1[1:3, :] + s2[1:3, :] + s3[1:3, :]
        acc[6:10, :] = two[0:4, :]
        acc[pl.ds(10 + ten, 1), :] = p0[...] + p1[...] + p2[...] + p3[...]
        acc[pl.ds(14 + ten, 1), :] = s0[3:4, :] + s1[3:4, :] + s2[3:4, :] + s3[3:4, :]
        out[...] = acc[...].astype(BF16)

    def attend_weight_kernel(so_far, ga, gb, la, lb, ma, mb, ba, bb, keep, send, acc):
        for c in range(3):
            at = slice(c * width, (c + 1) * width)
            acc[at, :] = so_far[at, :] + tn(ga[c], la[...])
            acc[at, :] += tn(gb[c], lb[...])
        acc[3 * width :, :] = so_far[3 * width :, :] + tn(ma[...], ba[...])
        acc[3 * width :, :] += tn(mb[...], bb[...])
        halves_of(acc, keep, send)

    def merge_kernel(mine, other, out):
        a, b = mine[...].astype(F32), other[...].astype(F32)
        early = lax.axis_index("pipe") == 0
        out[...] = jnp.concatenate(
            [
                jnp.where(early, a[:half], b[:half]),
                jnp.where(early, b[:half], a[:half]),
                a[half : half + 24] + b[half : half + 24],
            ],
            axis=0,
        ).astype(BF16)

    def message_back(*refs):
        pack_refs, refs = refs[:pack_blocks], refs[pack_blocks:]
        (first, q, k, v, probs, w, wo, vrow, sent_o, grads_o, back_o) = refs
        sent = jnp.concatenate(
            [clip_block(pack_refs, c, pack_rows).astype(F32)[:frame_count] for c in range(clips)],
            axis=0,
        )
        low = sent.astype(BF16)
        sent_o[...] = sent
        grad_mixed = nt(low, wo[...]).astype(BF16)
        dq = jnp.zeros((all_rows, width), F32)
        dk = jnp.zeros((all_rows, width), F32)
        dv = jnp.zeros((all_rows, width), F32)
        for h, mask in enumerate(head_masks(all_rows)):
            grad_head = only(mask, grad_mixed)
            wide = probs[h]
            dv = dv + tn(wide.astype(BF16), grad_head)
            grad_probs = nt(grad_head, v[...])
            inner = jnp.sum(wide * grad_probs, axis=-1, keepdims=True)
            grad_scores = (wide * (grad_probs - inner)).astype(BF16)
            dq = dq + only(mask, nn(grad_scores, k[...]))
            dk = dk + tn(grad_scores, only(mask, q[...]))
        dq = (dq * scale).astype(BF16)
        dk = (dk * scale).astype(BF16)
        dv = dv.astype(BF16)
        grads_o[0] = dq
        grads_o[1] = dk
        grads_o[2] = dv
        grad_low = nn(dq, w[0]) + nn(dk, w[1]) + nn(dv, w[2])
        normed, inverse = norm_parts(first[...])
        back_msg = norm_back(grad_low, normed, inverse, vrow[0:1])
        back_o[0:all_rows, :] = back_msg.astype(BF16)
        tail = jnp.concatenate(
            [row_sum(grad_low * normed), row_sum(grad_low), jnp.zeros((14, model), F32)], axis=0
        )
        back_o[all_rows:, :] = tail.astype(BF16)

    def message_weight(sent, grads_in, low, mixed, in_o, out_o, qv_o, bias_o):
        for c in range(3):
            in_o[c] = tn(grads_in[c], low[...])
        out_o[...] = tn(mixed[...], sent[...].astype(BF16))
        qv_o[0:1, :] = row_sum(grads_in[0].astype(F32))
        qv_o[1:2, :] = row_sum(grads_in[2].astype(F32))
        bias_o[...] = row_sum(sent[...])

    def block_out_kernel(*refs):
        for at, total in frames_of(*refs[:-1]):
            refs[-1][at] = total.T[:, :patch].astype(BF16)

    def message_end(*refs):
        pack_refs, refs = refs[:pack_blocks], refs[pack_blocks:]
        cls_refs, refs = refs[:blocks], refs[blocks:]
        (sent, own, late, mw, qv_in, bias_in, w_o, cls_o, vec_o, qv_o, turned, sums) = refs
        sec, ten = lax.axis_index("pipe"), lax.axis_index("tensor")
        total = jnp.where(sec == 0, own[...].astype(F32), late[...].astype(F32))
        grad_first = sent[...] + total[:all_rows]
        at = pl.ds(pl.multiple_of(ten * width, width), width)
        mine = grad_first[:16]
        high = mine.astype(BF16)
        rest = (mine - high.astype(F32)).astype(BF16)
        mw_rows = mw[at, :]
        cls_o[...] = nt(high, mw_rows) + nt(rest, mw_rows)
        turned[...] = grad_first.T
        mine = turned[at, :]
        high = mine.astype(BF16)
        rest = (mine - high.astype(F32)).astype(BF16)
        cls = jnp.concatenate([clip_block(cls_refs, c, frame_count).astype(F32) for c in range(clips)])
        cls = cls.astype(BF16)
        w_o[...] = nn(high, cls) + nn(rest, cls)
        summed = clip_block(pack_refs, 0, pack_rows).astype(F32)
        for c in range(1, clips):
            summed = summed + clip_block(pack_refs, c, pack_rows).astype(F32)
        sums[...] = summed[frame_count:]
        first_one = sec == 0
        vec_o[0:1, :] = jnp.where(first_one, total[all_rows : all_rows + 1], sums[0:1])
        vec_o[1:2, :] = jnp.where(first_one, total[all_rows + 1 : all_rows + 2], sums[1:2])
        vec_o[2:3, :] = jnp.where(first_one, bias_in[...], sums[4:5])
        vec_o[3:4, :] = sums[2:3]
        vec_o[4:5, :] = sums[3:4]
        vec_o[5:6, :] = sums[5:6]
        vec_o[6:7, :] = sums[pl.ds(6 + ten, 1), :]
        vec_o[7:8, :] = row_sum(grad_first)
        qv_row = sums[pl.ds(10 + ten, 1), :]
        qv_o[0:1, :] = jnp.where(first_one, qv_in[0:1], qv_row[:, :width])
        qv_o[1:2, :] = jnp.where(first_one, qv_in[1:2], qv_row[:, 256 : 256 + width])

    def frames_grad_kernel(*refs):
        cls, out = refs[-2:]
        top = lax.broadcasted_iota(jnp.int32, (rows, width), 0) == 0
        for at, total in frames_of(*refs[:-2]):
            row = cls[pl.ds(lax.axis_index("pipe") * half + at, 1), :]
            out[at] = (total + jnp.where(top, row, 0.0)).T[:, :patch].astype(BF16)

    def attend_whole_kernel(keep, other, in_zero_ref, out_zero_ref, in_o, out_o, acc):
        @pl.when(lax.axis_index("pipe") == 0)
        def _():
            in_o[...] = in_zero_ref[...]
            out_o[...] = out_zero_ref[...]

        @pl.when(lax.axis_index("pipe") == 1)
        def _():
            put_halves(keep, other, acc)
            for c in range(3):
                in_o[c] = acc[c * width : (c + 1) * width, :]
            out_o[...] = acc[3 * width :, :]

    def pack_join_kernel(a, b, out):
        size = a.shape[0]
        out[0:size, :] = a[...]
        out[size:, :] = b[...]

    stage.cost = 0
    sent_out = y_early(own_out)
    cls_all = gather_clips(frames[0, :, 0, :])
    vectors, own_vec, near_in, in_and_vec = stage(
        small_kernel,
        [
            own_in, msg_bias, norm2_gain, norm2_shift, fc_in_bias, fc_out_bias,
            norm_gain, norm_shift, out_bias, qv_bias,
        ],
        [near((8, model), F32)] * 2 + [near(own_in.shape, BF16), near((3 * width + 16, model), BF16)],
        [pltpu.VMEM((model,), F32)] * 5
        + [pltpu.VMEM((1, model), F32)] * 3
        + [pltpu.VMEM((1, 2, width), F32), pltpu.SemaphoreType.DMA((13,))],
        far=10,
    )
    sent_in = y_early(in_and_vec)
    near_msg_w, near_out = stage(
        load_kernel, [msg_w, own_out], [near(msg_w.shape, BF16), near(own_out.shape, BF16)],
        [pltpu.SemaphoreType.DMA((2,))],
        far=2,
    )
    x_slots = slots(tokens, half)
    (first_msg, low_zero, q_zero, k_zero, v_zero, probs_zero, mixed_zero, part_zero) = stage(
        message_forward,
        [video_group, *cls_all, near_msg_w, vectors, own_vec, near_in, near_out],
        [
            near((all_rows, model), F32),
            near((all_rows, model), BF16),
            near((all_rows, width), BF16),
            near((all_rows, width), BF16),
            near((all_rows, width), BF16),
            near((heads, all_rows, all_rows), F32),
            near((all_rows, width), BF16),
            near((frame_count, model), F32),
        ],
        [pltpu.SMEM(video_group.shape, jnp.int32), pltpu.SemaphoreType.DMA],
        far=1,
    )
    from_core = core_swap(part_zero)
    (part_zero,) = adds((part_zero, from_core))
    from_x = x_swap(part_zero)
    (part_zero,) = adds((part_zero, from_x))
    part_late = y_late(part_zero)
    w_in, vec, *projected = stage(
        project_kernel, [*x_slots, near_in, sent_in, own_vec],
        [near(own_in.shape, BF16), near(own_vec.shape, F32)] + [near((rows, width), BF16)] * 12,
    )
    stage.cost = 4 * 10**9
    q_one, k_patch, v_patch = projected[:4], projected[4:8], projected[8:]
    msg_rows, k_msg, v_msg, w_out = stage(
        message_rows_kernel,
        [first_msg, part_zero, part_late, w_in, vec, near_out, sent_out],
        [
            near((16, model), F32), near((16, width), F32), near((16, width), F32),
            near(own_out.shape, BF16),
        ],
    )

    at3 = attend(3)
    ac3 = core_swap(at3[0])
    at2 = attend(2)
    two0, two1 = add_parts(at2[0], ac3)
    ax0 = x_swap(two0)
    ax1 = x_swap(two1)
    at1 = attend(1)
    ac1 = core_swap(at1[0])
    at0 = attend(0)
    g_slots = slots(grads_in, 2 * half)
    (aown,) = adds((at0[0], ac1))
    resid0, low0 = stage(
        residual_first_kernel, [aown, ax0, x_slots[0], vec, vectors],
        [near((first_rows, model), F32), near((first_rows, model), BF16)],
    )
    lx0 = x_swap(low0)
    resid_own, low_own, low1 = stage(
        residual_last_kernel, [aown, ax1, x_slots[0], vec, vectors, resid0, low0],
        [near((rows, model), F32), near((rows, model), BF16), near((rows - first_rows, model), BF16)],
    )
    lx1 = x_swap(low1)
    l1 = core_swap(low_own)
    ly = y_swap(low_own)
    g_hidden = stage(
        grad_hidden_kernel, [*g_slots[:half], fc_out], [near((rows, hidden_width), BF16)] * half,
    )
    hid0, pre0, gp0, bs0 = feed(low_own, g_hidden[0])
    hid1, pre1, gp1, bs1 = feed(l1, g_hidden[1])
    fc1 = core_swap(gp1)
    fc_out_half = own_part(own_out_kernel, (half_rows, model), hid0, hid1, g_slots[0], g_slots[1])
    (fown,) = adds((gp0, fc1))
    l2 = join_parts(lx0, lx1)
    l3 = core_swap(l2)
    ly2 = y_swap(l2)
    hid2, pre2, gp2, bs2 = feed(l2, g_hidden[2])
    hid3, pre3, gp3, bs3 = feed(l3, g_hidden[3])
    fc3 = core_swap(gp3)
    m0 = relay(ly)
    m1 = core_swap(m0)
    two0, two1 = add_parts(gp2, fc3)
    fx0 = x_swap(two0)
    fx1 = x_swap(two1)
    ho0, po0 = feed_other(m0, g_slots[4])
    ho1, po1 = feed_other(m1, g_slots[5])
    block_parts = stage(
        mlp_kernel, [hid0, hid1, hid2, hid3, fc_out, resid_own, vectors],
        [near((rows, model), BF16)] * half,
    )
    fc_in_half = own_part(own_in_kernel, (model, half_rows), low_own, l1, pre0, pre1)
    grad0, glow0, small0 = stage(
        residual_back_first_kernel, [fown, fx0, resid_own, g_slots[0], vectors],
        [near((first_rows, model), F32), near((first_rows, model), BF16), near((8, model), F32)],
    )
    bx0 = x_swap(glow0)
    m2 = relay(ly2)
    m3 = core_swap(m2)
    grad_resid, grad_low, glow1, small_two = stage(
        residual_back_last_kernel,
        [fown, fx1, resid_own, g_slots[0], vectors, grad0, glow0, small0],
        [
            near((rows, model), F32), near((rows, model), BF16),
            near((rows - first_rows, model), BF16), near((8, model), F32),
        ],
    )
    bx1 = x_swap(glow1)
    b1 = core_swap(grad_low)
    ho2, po2 = feed_other(m2, g_slots[6])
    ho3, po3 = feed_other(m3, g_slots[7])
    p0 = whole_part(
        sum_out_kernel, fc_out_half, hid2, hid3, g_slots[2], g_slots[3], ho0, ho1, ho2, ho3, *g_slots[half:],
    )
    q0 = whole_part(
        sum_in_kernel, fc_in_half, l2, l3, pre2, pre3, m0, m1, m2, m3, po0, po1, po2, po3,
    )
    ba0, gr0, lo0, sm0 = attend_back(0, grad_low, at0)
    ba1, gr1, lo1, sm1 = attend_back(1, b1, at1)
    (attend_half,) = stage(
        attend_weight_half_kernel, [gr0, gr1, lo0, lo1, at0[1], at1[1], grad_low, b1],
        [near((4 * width, model), F32)],
    )
    b2 = join_parts(bx0, bx1)
    b3 = core_swap(b2)
    ba2, gr2, lo2, sm2 = attend_back(2, b2, at2)
    p1 = over_far_clip(*p0)
    ba3, gr3, lo3, sm3 = attend_back(3, b3, at3)
    (pk0,) = stage(
        pack_kernel, [sm0, sm1, sm2, sm3, small_two, bs0, bs1, bs2, bs3], [near((32, model), BF16)],
        [pltpu.VMEM((32, model), F32)],
    )
    pkc = core_swap(pk0)
    r0 = over_sections(
        *stage(
            attend_weight_kernel,
            [attend_half, gr2, gr3, lo2, lo3, at2[1], at3[1], b2, b3],
            half_shapes,
            [pltpu.VMEM((4 * width, model), F32)],
        )
    )
    (pk1,) = adds((pk0, pkc))
    pkx = x_swap(pk1)
    q1 = over_far_clip(*q0)
    p2 = to_far_clip(*p1)
    (pk2,) = adds((pk1, pkx))
    pky = y_swap(pk2)
    r1 = over_near_clip(*r0)
    q2 = to_far_clip(*q1)
    (pk3,) = stage(merge_kernel, [pk2, pky], [near((32, model), BF16)])
    pack_rows = pk3.shape[0]
    pkz = z_swap(pk3, 1) if ring else None
    p3 = to_near_clip(*p2)
    r2 = over_far_clip(*r1)
    if ring:
        (pk4,) = stage(pack_join_kernel, [pk3, pkz], [near((2 * pack_rows, model), BF16)])
        packs = [pk4, z_swap(pk4, 2)]
    else:
        packs = gather_clips(pk3)
    q3 = to_near_clip(*q2)
    p4 = to_other_section(*p3)
    sent_all, grads_zero, bz0 = stage(
        message_back,
        [*packs, first_msg, q_zero, k_zero, v_zero, probs_zero, near_in, near_out, own_vec],
        [
            near((all_rows, model), F32),
            near((3, all_rows, width), BF16),
            near((all_rows + 16, model), BF16),
        ],
    )
    bzc = core_swap(bz0)
    in_zero, out_zero, qv_zero, bias_zero = stage(
        message_weight, [sent_all, grads_zero, low_zero, mixed_zero],
        [
            near((3, width, model), F32),
            near((width, model), F32),
            near((2, width), F32),
            near((1, model), F32),
        ],
    )
    (bz1,) = adds((bz0, bzc))
    bzx = x_swap(bz1)
    r3 = to_far_clip(*r2)
    q4 = to_other_section(*q3)
    (bz2,) = adds((bz1, bzx))
    bzy = y_late(bz2)
    ck, send = stage(column_kernel, [ba0, ba1, ba2, ba3], column_shapes)
    cs = core_swap(send)
    msg_w_grad, cls_part, vec_grads, qv_grad = stage(
        message_end,
        [*packs, *cls_all, sent_all, bz2, bzy, near_msg_w, qv_zero, bias_zero],
        [
            shape_of((width, model), F32),
            near((16, width), F32),
            near((8, model), F32),
            near((2, width), F32),
        ],
        [pltpu.VMEM((model, all_rows), F32), pltpu.VMEM((24, model), F32)],
    )
    fc_out_grad = whole(*p4)
    kept, far = far_columns(ck, cs)
    bk, send = stage(column_kernel, block_parts, column_shapes)
    bcs = core_swap(send)
    r4 = to_near_clip(*r3)
    (frames_grad,) = stage(
        frames_grad_kernel, [kept, far, cls_part], [shape_of((half, width, patch), BF16)],
    )
    bkept, bfar = far_columns(bk, bcs)
    fc_in_grad = whole_of_columns(*q4)
    r5 = to_sections(*r4, move=y_late)
    (block_out,) = stage(
        block_out_kernel, [bkept, bfar], [shape_of((half, width, patch), BF16)],
    )
    attn_in_grad, attn_out_grad = stage(
        attend_whole_kernel, [*r5, in_zero, out_zero],
        [shape_of((3, width, model), F32), shape_of((width, model), F32)],
        [pltpu.VMEM((4 * width, model), F32)],
    )

    return (
        jnp.swapaxes(block_out, 1, 2)[None],
        jnp.swapaxes(frames_grad, 1, 2)[None],
        msg_w_grad.T,
        vec_grads[7],
        vec_grads[0:1],
        vec_grads[1:2],
        jnp.transpose(attn_in_grad, (2, 0, 1))[None],
        qv_grad[None],
        attn_out_grad[None],
        vec_grads[2:3],
        vec_grads[3],
        vec_grads[4],
        fc_in_grad,
        vec_grads[6],
        fc_out_grad,
        vec_grads[5],
    )


def solution(mesh):
    return jax.shard_map(
        body,
        mesh=mesh,
        in_specs=(
            P("dp", None, None, None),
            P(),
            P(),
            P(),
            P("pipe", None),
            P("pipe", None),
            P("pipe", None, None, "tensor"),
            P("pipe", None, "tensor"),
            P("pipe", "tensor", None),
            P("pipe", None),
            P(),
            P(),
            P(None, "tensor"),
            P("tensor"),
            P("tensor", None),
            P(),
            P("dp", None, None, None),
        ),
        out_specs=(
            P("dp", "pipe", None, "tensor"),
            P("dp", "pipe", None, "tensor"),
            P(None, "tensor"),
            P(),
            P("pipe", None),
            P("pipe", None),
            P("pipe", None, None, "tensor"),
            P("pipe", None, "tensor"),
            P("pipe", "tensor", None),
            P("pipe", None),
            P(),
            P(),
            P(None, "tensor"),
            P("tensor"),
            P("tensor", None),
            P(),
        ),
        check_vma=False,
    )
```

```python
import functools

import jax
import jax.numpy as jnp
from jax import lax
from jax.experimental import pallas as pl
from jax.experimental.pallas import tpu as pltpu
from jax.sharding import PartitionSpec as P

HEAD_DIM = 64
EPSILON = 1e-05
QUICK_GELU = 1.702
F32 = jnp.float32
BF16 = jnp.bfloat16
VMEM_BYTES = 16 * 1024 * 1024


def nn(left, right):
    return lax.dot_general(left, right, (((1,), (0,)), ((), ())), preferred_element_type=F32)


def nt(left, right):
    return lax.dot_general(left, right, (((1,), (1,)), ((), ())), preferred_element_type=F32)


def tn(left, right):
    return lax.dot_general(left, right, (((0,), (0,)), ((), ())), preferred_element_type=F32)


def norm_parts(values_in):
    centred = values_in - jnp.mean(values_in, axis=-1, keepdims=True)
    inverse = lax.rsqrt(jnp.mean(centred * centred, axis=-1, keepdims=True) + EPSILON)
    return centred * inverse, inverse


def norm_back(incoming, normed, inverse, gain):
    weighted = incoming * gain
    centred = weighted - jnp.mean(weighted, axis=-1, keepdims=True)
    return inverse * (centred - normed * jnp.mean(weighted * normed, axis=-1, keepdims=True))


def row_sum(values_in):
    return jnp.sum(values_in, axis=0, keepdims=True)


def shape_of(shape, kind):
    return jax.ShapeDtypeStruct(shape, kind)


def near(shape, kind):
    return pltpu.VMEM(shape, kind)


class Chain:
    def __init__(self):
        self.token = None
        self.near, self.kept = set(), []
        self.cost = 4 * 10**9

    def __call__(self, kernel, ins, outs, scratch=(), flops=0, far=0):
        tokens = 0 if self.token is None else 1
        count, given = len(ins), len(outs)

        def stage(*refs):
            rest = refs[tokens:]
            kernel(*rest[:count], *rest[count : count + given], *rest[count + given + 1 :])

        vmem = pl.BlockSpec(memory_space=pltpu.VMEM)
        held = [] if self.token is None else [self.token]
        ins = [
            pltpu.with_memory_space_constraint(a, pltpu.HBM)
            if i < far
            else pltpu.with_memory_space_constraint(a, pltpu.VMEM)
            if id(a) in self.near
            else a
            for i, a in enumerate(ins)
        ]
        results = pl.pallas_call(
            stage,
            out_shape=[*outs, near((8, 128), F32)],
            in_specs=[pl.BlockSpec(memory_space=pl.ANY)] * tokens
            + [pl.BlockSpec(memory_space=pltpu.HBM)] * far
            + [vmem] * (count - far),
            out_specs=[vmem] * (given + 1),
            scratch_shapes=list(scratch),
            compiler_params=pltpu.CompilerParams(vmem_limit_bytes=VMEM_BYTES),
            cost_estimate=pl.CostEstimate(flops=self.cost, bytes_accessed=0, transcendentals=0),
        )(*held, *ins)
        self.token = results[-1]
        self.kept += results
        for out, result in zip(outs, results):
            if not isinstance(out, jax.ShapeDtypeStruct):
                self.near.add(id(result))
        return results[:-1]


def body(
    frames,
    video_group,
    msg_w,
    msg_bias,
    norm_gain,
    norm_shift,
    attn_in,
    qv_bias,
    attn_out,
    out_bias,
    norm2_gain,
    norm2_shift,
    fc_in,
    fc_in_bias,
    fc_out,
    fc_out_bias,
    cotangent,
):
    _, frame_count, patch, model = frames.shape

    width = attn_in.shape[-1]

    hidden_width = fc_in.shape[-1]

    heads = width // HEAD_DIM

    clips = lax.axis_size("dp")

    half = frame_count // 2

    rows = -(-(patch + 1) // 16) * 16

    all_rows = clips * frame_count

    scale = HEAD_DIM ** (-0.5)

    pipe = lax.axis_index("pipe")

    tensor = lax.axis_index("tensor")

    clip = lax.axis_index("dp")

    ring = clips == 4

    stage = Chain()

    quarter = hidden_width // 4

    assert quarter == width and hidden_width == model and half == 4

    def tensor_swap(v, bit):
        return lax.ppermute(v, "tensor", [(i, i ^ bit) for i in range(4)])

    def core_swap(v):
        return tensor_swap(v, 1)

    def x_swap(v):
        return tensor_swap(v, 2)

    def y_swap(v):
        return lax.ppermute(v, "pipe", [(0, 1), (1, 0)])

    def y_late(v):
        return lax.ppermute(v, "pipe", [(0, 1)])

    def y_early(v):
        return lax.ppermute(v, "pipe", [(1, 0)])

    def z_swap(v, bit):
        return lax.ppermute(v, "dp", [(i, i ^ bit) for i in range(clips)])

    def gather_clips(v):
        if ring:
            return [v] + [z_swap(v, apart) for apart in range(1, clips)]
        every = lax.all_gather(v, "dp")
        every = lax.dynamic_slice_in_dim(jnp.concatenate([every, every]), clip, clips, 0)
        return [every.reshape(clips * v.shape[0], v.shape[1])]

    def clip_block(refs, c, size):
        each = clips // len(refs)
        at = c % each * size
        return refs[c // each][at : at + size, :]

    blocks = clips if ring else 1

    pack_blocks = 2 if ring else 1

    def head_masks(n):
        lane = lax.broadcasted_iota(jnp.int32, (n, width), 1)
        return [(lane >= h * HEAD_DIM) & (lane < (h + 1) * HEAD_DIM) for h in range(heads)]

    def only(mask, v):
        return jnp.where(mask, v, jnp.zeros_like(v))

    def add(*terms):
        total = terms[0].astype(F32)
        for term in terms[1:]:
            total = total + term.astype(F32)
        return total

    def adds(*groups):
        sizes = [len(group) for group in groups]

        def kernel(*refs):
            at = 0
            for size, out in zip(sizes, refs[sum(sizes) :]):
                out[...] = add(*[ref[...] for ref in refs[at : at + size]]).astype(out.dtype)
                at += size

        return stage(
            kernel,
            [array for group in groups for array in group],
            [near(group[0].shape, group[0].dtype) for group in groups],
        )

    own_in = jnp.transpose(attn_in[0], (1, 2, 0))

    own_out = attn_out[0]

    tokens = jnp.transpose(frames[0], (1, 0, 2))

    grads_in = jnp.transpose(cotangent[0], (1, 0, 2))

    def small_kernel(*refs):
        ins, vecs_o, own_o, in_o, both_o = refs[:10], *refs[10:14]
        lines, rest, sem = refs[14:19], refs[19:23], refs[23]
        pairs = [(ins[0], in_o)] + list(zip(ins[1:], (*lines, *rest)))
        pairs += [(ins[0].at[c], both_o.at[c * width : (c + 1) * width]) for c in range(3)]
        copies = [pltpu.make_async_copy(a, b, sem.at[i]) for i, (a, b) in enumerate(pairs)]
        for copy in copies:
            copy.start()
        for copy in copies:
            copy.wait()
        for i, line in enumerate(lines):
            vecs_o[i : i + 1, :] = line[...].reshape(1, model)
        for i, line in enumerate(rest[:3]):
            own_o[i : i + 1, :] = line[...]
        own_o[3:8, :] = jnp.zeros((5, model), F32)
        own_o[3:5, 0:width] = rest[3][0]
        high = own_o[...].astype(BF16).astype(F32)
        both_o[3 * width :, :] = jnp.concatenate([high, own_o[...] - high], axis=0).astype(BF16)

    def load_kernel(*refs):
        sem = refs[4]
        copies = [
            pltpu.make_async_copy(a, b, sem.at[i]) for i, (a, b) in enumerate(zip(refs[:2], refs[2:4]))
        ]
        for copy in copies:
            copy.start()
        for copy in copies:
            copy.wait()

    tokens_all = rows * frame_count

    lanes = 128

    def slot_kernel(v, *refs):
        outs, (wide, held, sem) = refs[:-3], refs[-3:]
        copy = pltpu.make_async_copy(v, held, sem)
        copy.start()
        copy.wait()
        flat = held[...].astype(F32).reshape(patch * frame_count, model)
        sec, ten = lax.axis_index("pipe"), lax.axis_index("tensor")
        for c in range(model // lanes):
            at = c * tokens_all
            wide[at : at + patch * frame_count, :] = flat[:, c * lanes : (c + 1) * lanes]
            wide[at + patch * frame_count : at + tokens_all, :] = jnp.zeros(
                ((rows - patch) * frame_count, lanes), F32
            )
            for s, out in enumerate(outs):
                frame = at + (sec if s < half else 1 - sec) * half + (ten ^ (s % half))
                out[:, c * lanes : (c + 1) * lanes] = wide[
                    pl.ds(frame, rows, stride=frame_count), :
                ].astype(BF16)

    def slots(v, count):
        return stage(
            slot_kernel,
            [v],
            [near((rows, model), BF16)] * count,
            [
                pltpu.VMEM((model // lanes * tokens_all, lanes), F32),
                pltpu.VMEM((patch, frame_count, model), BF16),
                pltpu.SemaphoreType.DMA,
            ],
            far=1,
        )

    def message_forward(groups, *refs):
        cls_refs, refs = refs[:blocks], refs[blocks:]
        (mw, vecs, vrow, w, wo, first_o, low_o, q_o, k_o, v_o, probs_o, mixed_o, part_o, ids, sem) = refs
        copy = pltpu.make_async_copy(groups, ids, sem)
        copy.start()
        cls = jnp.concatenate([clip_block(cls_refs, c, frame_count).astype(F32) for c in range(clips)])
        first = nn(cls.astype(BF16), mw[...]) + vecs[0:1]
        first_o[...] = first
        normed, _ = norm_parts(first)
        low = (normed * vrow[0:1] + vrow[1:2]).astype(BF16)
        low_o[...] = low
        q = (nt(low, w[0]) + vrow[3:4, :width]).astype(BF16)
        k = nt(low, w[1]).astype(BF16)
        v = (nt(low, w[2]) + vrow[4:5, :width]).astype(BF16)
        q_o[...] = q
        k_o[...] = k
        v_o[...] = v
        of_row = lax.broadcasted_iota(jnp.int32, (all_rows, all_rows), 0) // frame_count
        of_col = lax.broadcasted_iota(jnp.int32, (all_rows, all_rows), 1) // frame_count
        mine = lax.axis_index("dp")
        copy.wait()
        row_id = jnp.zeros((all_rows, all_rows), jnp.int32)
        col_id = jnp.zeros((all_rows, all_rows), jnp.int32)
        for c in range(clips):
            mark = ids[mine ^ c if ring else lax.rem(mine + c, clips)]
            row_id = jnp.where(of_row == c, mark, row_id)
            col_id = jnp.where(of_col == c, mark, col_id)
        allowed = row_id == col_id
        mixed = jnp.zeros((all_rows, width), F32)
        for h, mask in enumerate(head_masks(all_rows)):
            scores = jnp.where(allowed, nt(only(mask, q), k) * scale, -jnp.inf)
            exponent = jnp.exp(scores - jnp.max(scores, axis=-1, keepdims=True))
            probs = exponent / jnp.sum(exponent, axis=-1, keepdims=True)
            probs_o[h] = probs
            mixed = mixed + only(mask, nn(probs.astype(BF16), v))
        mixed = mixed.astype(BF16)
        mixed_o[...] = mixed
        part = nn(mixed, wo[...]) + jnp.where(lax.axis_index("tensor") == 0, vrow[2:3], 0.0)
        part_o[...] = part[:frame_count]

    def project_kernel(x0, x1, x2, x3, wa, wb, va, w, vrow, *outs):
        early = lax.axis_index("pipe") == 0
        for c in range(3):
            w[c] = jnp.where(early, wb[c * width : (c + 1) * width, :], wa[c])
        sent = wb[3 * width :, :].astype(F32)
        vrow[...] = jnp.where(early, sent[0:8] + sent[8:16], va[...])
        gain, shift = vrow[0:1], vrow[1:2]
        for s, x in enumerate((x0, x1, x2, x3)):
            normed, _ = norm_parts(x[...].astype(F32))
            low = (normed * gain + shift).astype(BF16)
            outs[s][...] = (nt(low, w[0]) + vrow[3:4, :width]).astype(BF16)
            outs[half + s][...] = nt(low, w[1]).astype(BF16)
            outs[2 * half + s][...] = (nt(low, w[2]) + vrow[4:5, :width]).astype(BF16)

    def message_rows_kernel(first, part, late, w, vrow, msg_o, k_o, v_o):
        sec, ten = lax.axis_index("pipe"), lax.axis_index("tensor")
        msg_o[...] = jnp.zeros_like(msg_o)
        for s in range(half):
            at = pl.ds(sec * half + (ten ^ s), 1)
            summed = jnp.where(sec == 0, part[at, :], late[at, :])
            msg_o[s : s + 1, :] = (first[at, :] + summed).astype(BF16).astype(F32)
        normed, _ = norm_parts(msg_o[...])
        low = (normed * vrow[0:1] + vrow[1:2]).astype(BF16)
        k_o[...] = nt(low, w[1])
        v_o[...] = nt(low, w[2]) + vrow[4:5, :width]

    def attend_kernel(
        s, with_out, q, k, v, km, vm, *refs
    ):
        mixed_o, probs_o, k_o, v_o = refs[-4:]
        here = lax.broadcasted_iota(jnp.int32, (rows, width), 0) == patch
        key_here = lax.broadcasted_iota(jnp.int32, (rows, rows), 1) <= patch
        kk = jnp.where(here, km[s : s + 1], k[...].astype(F32)).astype(BF16)
        vv = jnp.where(here, vm[s : s + 1], v[...].astype(F32)).astype(BF16)
        k_o[...] = kk
        v_o[...] = vv
        mixed = jnp.zeros((rows, width), F32)
        for h, mask in enumerate(head_masks(rows)):
            scores = nt(only(mask, q[...]), kk) * scale
            scores = jnp.where(key_here, scores, -jnp.inf)
            exponent = jnp.exp(scores - jnp.max(scores, axis=-1, keepdims=True))
            probs = exponent * (1.0 / jnp.sum(exponent, axis=-1, keepdims=True))
            probs = probs.astype(BF16)
            probs_o[h] = probs
            mixed = mixed + only(mask, nn(probs, vv))
        mixed = mixed.astype(BF16)
        mixed_o[...] = mixed
        if with_out:
            wo, part_o = refs[:2]
            part_o[...] = nn(mixed, wo[...]).astype(BF16)

    def attend(s, *out):
        return stage(
            functools.partial(attend_kernel, s, bool(out)),
            [q_one[s], k_patch[s], v_patch[s], k_msg, v_msg, *out],
            [near((rows, model), BF16)] * len(out)
            + [
                near((rows, width), BF16),
                near((heads, rows, rows), BF16),
                near((rows, width), BF16),
                near((rows, width), BF16),
            ],
            flops=2 * rows * (width * model + 2 * heads * rows * HEAD_DIM),
        )

    def first_out_kernel(mixed, wa, wb, part_o, w_o):
        w_o[...] = jnp.where(lax.axis_index("pipe") == 0, wb[...], wa[...])
        part_o[...] = nn(mixed[...], w_o[...]).astype(BF16)

    def out_kernel(mixed, w, part_o):
        part_o[...] = nn(mixed[...], w[...]).astype(BF16)

    first_rows = rows // 32 * 16 + 16

    row_parts = (slice(0, first_rows), slice(first_rows, rows))

    def add_parts(a, b):
        def kernel(a_ref, b_ref, *outs):
            for at, out in zip(row_parts, outs):
                out[...] = add(a_ref[at, :], b_ref[at, :]).astype(BF16)

        return stage(
            kernel, [a, b], [near((at.stop - at.start, model), BF16) for at in row_parts]
        )

    def join_parts(a, b):
        def kernel(a_ref, b_ref, out):
            for at, ref in zip(row_parts, (a_ref, b_ref)):
                out[at, :] = ref[...]

        return stage(kernel, [a, b], [near((rows, model), a.dtype)])[0]

    def residual_of(at, a, b, x, vrow, vecs):
        resid = x[at, :].astype(F32) + add(a[at, :], b[...]) + vrow[2:3]
        normed, _ = norm_parts(resid)
        return resid, (normed * vecs[1:2] + vecs[2:3]).astype(BF16)

    def residual_first_kernel(a, b, x, vrow, vecs, resid_o, low_o):
        resid_o[...], low_o[...] = residual_of(row_parts[0], a, b, x, vrow, vecs)

    def residual_last_kernel(a, b, x, vrow, vecs, resid_in, low_in, resid_o, low_o, part_o):
        resid, low = residual_of(row_parts[1], a, b, x, vrow, vecs)
        for at, one, two in zip(row_parts, (resid_in[...], resid), (low_in[...], low)):
            resid_o[at, :] = one
            low_o[at, :] = two
        part_o[...] = low

    def relay_kernel(v, out):
        out[...] = v[...]

    def relay(v):
        return stage(relay_kernel, [v], [near(v.shape, v.dtype)])[0]

    def grad_hidden_kernel(g0, g1, g2, g3, w, *outs):
        for g, out in zip((g0, g1, g2, g3), outs):
            out[...] = nt(g[...], w[...]).astype(BF16)

    def feed_kernel(low, gh, w, vecs, hid_o, pre_o, grad_o, bias_o):
        hidden_in = nn(low[...], w[...]) + vecs[3:4]
        sig = 1.0 / (1.0 + jnp.exp(-QUICK_GELU * hidden_in))
        hid_o[...] = (hidden_in * sig).astype(BF16)
        slope = sig + QUICK_GELU * hidden_in * sig * (1.0 - sig)
        pre = (gh[...].astype(F32) * slope).astype(BF16)
        pre_o[...] = pre
        grad_o[...] = nt(pre, w[...]).astype(BF16)
        bias_o[...] = row_sum(pre.astype(F32))

    def feed(low, gh):
        return stage(
            feed_kernel, [low, gh, fc_in, vectors],
            [
                near((rows, hidden_width), BF16),
                near((rows, hidden_width), BF16),
                near((rows, model), BF16),
                near((1, hidden_width), F32),
            ],
            flops=2 * 2 * rows * model * hidden_width,
        )

    half_rows, eighth = model // 2, model // 8

    def halves_of(acc, keep, send):
        sec = lax.axis_index("pipe")
        for out, at in ((keep, sec), (send, 1 - sec)):
            start = pl.multiple_of(at * half_rows, half_rows)
            out[...] = acc[pl.ds(start, half_rows), :].astype(BF16)

    half_shapes = [near((half_rows, model), BF16)] * 2

    def section_columns():
        return pl.ds(pl.multiple_of(lax.axis_index("pipe") * half_rows, half_rows), half_rows)

    def feed_other_kernel(low, g, w, w_out, vecs, hid_o, pre_o):
        columns = section_columns()
        hidden_in = nn(low[...], w[:, columns]) + vecs[3:4, columns]
        sig = 1.0 / (1.0 + jnp.exp(-QUICK_GELU * hidden_in))
        hid_o[...] = (hidden_in * sig).astype(BF16)
        slope = sig + QUICK_GELU * hidden_in * sig * (1.0 - sig)
        pre_o[...] = (nt(g[...], w_out[columns, :]).astype(BF16).astype(F32) * slope).astype(BF16)

    def feed_other(low, g):
        return stage(
            feed_other_kernel, [low, g, fc_in, fc_out, vectors],
            [near((rows, half_rows), BF16)] * 2,
        )

    def own_out_kernel(h0, h1, g0, g1, out):
        out[...] = tn(h0[:, section_columns()], g0[...])
        out[...] += tn(h1[:, section_columns()], g1[...])

    def own_in_kernel(l0, l1, p0, p1, out):
        out[...] = tn(l0[...], p0[:, section_columns()])
        out[...] += tn(l1[...], p1[:, section_columns()])

    def own_part(kernel, shape, *ins):
        return stage(kernel, list(ins), [near(shape, F32)])[0]

    def clip_parts(acc, mine, send):
        size = mine.shape[0] // 2
        for out, first in ((mine, 0), (send, 1)):
            for at, apart in ((0, first), (size, first ^ 2)):
                out[at : at + size, :] = acc[clip_rows(apart, size), :].astype(BF16)

    def sum_out_kernel(part, h2, h3, g2, g3, o0, o1, o2, o3, q0, q1, q2, q3, mine, send, acc):
        acc[...] = part[...] + tn(h2[:, section_columns()], g2[...])
        acc[...] += tn(h3[:, section_columns()], g3[...])
        for o, q in ((o0, q0), (o1, q1), (o2, q2), (o3, q3)):
            acc[...] += tn(o[...], q[...])
        clip_parts(acc, mine, send)

    def sum_in_kernel(part, l2, l3, p2, p3, m0, m1, m2, m3, q0, q1, q2, q3, mine, send, acc):
        acc[...] = part[...] + tn(l2[...], p2[:, section_columns()])
        acc[...] += tn(l3[...], p3[:, section_columns()])
        for m, q in ((m0, q0), (m1, q1), (m2, q2), (m3, q3)):
            acc[...] += tn(m[...], q[...])
        clip_parts(acc, mine, send)

    def whole_part(kernel, part, *ins):
        rows_in, columns = part.shape
        mine, send = stage(
            kernel, [part, *ins], [near((rows_in // 2, columns), BF16)] * 2,
            [pltpu.VMEM((rows_in, columns), F32)],
        )
        return mine, z_swap(send, 1) if ring else send

    def over_sections(keep, send):
        return keep, y_swap(send) if ring else send

    def clip_rows(apart, size=eighth):
        here = lax.axis_index("dp") if ring else 0
        return pl.ds(pl.multiple_of((here ^ apart) * size, size), size)

    def over_near_clip(keep, got):
        if not ring:
            return keep, got

        def kernel(a, b, mine, send, acc):
            acc[...] = add(a[...], b[...])
            for out, first in ((mine, 0), (send, 1)):
                out[0:eighth, :] = acc[clip_rows(first), :].astype(BF16)
                out[eighth:, :] = acc[clip_rows(first ^ 2), :].astype(BF16)

        mine, send = stage(
            kernel, [keep, got], [near((2 * eighth, model), BF16)] * 2,
            [pltpu.VMEM((half_rows, model), F32)],
        )
        return mine, z_swap(send, 1)

    def over_far_clip(mine, got):
        if not ring:
            return mine, got
        size = mine.shape[0] // 2

        def kernel(a, b, own, send):
            own[...] = add(a[0:size, :], b[0:size, :]).astype(BF16)
            send[...] = add(a[size:, :], b[size:, :]).astype(BF16)

        own, send = stage(kernel, [mine, got], [near((size, mine.shape[1]), BF16)] * 2)
        return own, z_swap(send, 2)

    def to_far_clip(own, got):
        if not ring:
            return own, got
        (own,) = adds((own, got))
        return own, z_swap(own, 2)

    def to_near_clip(own, got):
        if not ring:
            return own, got

        size = own.shape[0]

        def kernel(a, b, out):
            out[0:size, :] = a[...]
            out[size:, :] = b[...]

        (both,) = stage(kernel, [own, got], [near((2 * size, own.shape[1]), BF16)])
        return both, z_swap(both, 1)

    def join_kernel(a, b, out):
        size = a.shape[0] // 2
        for apart, ref, at in ((0, a, 0), (2, a, size), (1, b, 0), (3, b, size)):
            out[clip_rows(apart, size), :] = ref[at : at + size, :]

    def to_sections(both, got, move=y_swap):
        if not ring:
            sec = lax.axis_index("pipe")
            early = jnp.where(sec == 0, both, got)
            later = jnp.where(sec == 0, got, both)
            early, later = lax.psum((early, later), ("pipe", "dp"))
            return jnp.where(sec == 0, early, later), jnp.where(sec == 0, later, early)
        (summed,) = stage(join_kernel, [both, got], [near((half_rows, model), BF16)])
        return summed, move(summed)

    def to_other_section(both, got):
        if not ring:
            both, got = lax.psum((both, got), "dp")
        (summed,) = stage(join_kernel, [both, got], [near((2 * both.shape[0], both.shape[1]), BF16)])
        return summed, y_swap(summed)

    def put_halves(keep, other, out):
        sec = lax.axis_index("pipe")
        for ref, at in ((keep, sec), (other, 1 - sec)):
            start = pl.multiple_of(at * half_rows, half_rows)
            out[pl.ds(start, half_rows), :] = ref[...].astype(F32)

    def whole(keep, other):
        return stage(put_halves, [keep, other], [shape_of((model, model), F32)])[0]

    def put_columns(keep, other, out):
        sec = lax.axis_index("pipe")
        for ref, at in ((keep, sec), (other, 1 - sec)):
            start = pl.multiple_of(at * half_rows, half_rows)
            out[:, pl.ds(start, half_rows)] = ref[...].astype(F32)

    def whole_of_columns(keep, other):
        return stage(put_columns, [keep, other], [shape_of((model, model), F32)])[0]

    def residual_back_of(at, a, b, resid, g, vecs):
        incoming = add(a[at, :], b[...])
        normed, inverse = norm_parts(resid[at, :])
        real = lax.broadcasted_iota(jnp.int32, incoming.shape, 0) < patch - at.start
        incoming = jnp.where(real, incoming, 0.0)
        from_out = g[at, :].astype(F32)
        grad = from_out + norm_back(incoming, normed, inverse, vecs[1:2])
        grad = jnp.where(real, grad, 0.0)
        low = grad.astype(BF16)
        sums = [row_sum(incoming * normed), row_sum(incoming), row_sum(low.astype(F32)), row_sum(from_out)]
        return grad, low, jnp.concatenate(sums + [jnp.zeros((4, model), F32)], axis=0)

    def residual_back_first_kernel(a, b, resid, g, vecs, grad_o, low_o, small_o):
        grad_o[...], low_o[...], small_o[...] = residual_back_of(row_parts[0], a, b, resid, g, vecs)

    def residual_back_last_kernel(
        a, b, resid, g, vecs, grad_in, low_in, small_in, grad_o, low_o, part_o, small_o
    ):
        grad, low, small = residual_back_of(row_parts[1], a, b, resid, g, vecs)
        for at, one, two in zip(row_parts, (grad_in[...], grad), (low_in[...], low)):
            grad_o[at, :] = one
            low_o[at, :] = two
        part_o[...] = low
        small_o[...] = small_in[...] + small

    def column_out(values_in, slot, keep_o, send_o):
        ten = lax.axis_index("tensor")
        spot = (ten ^ slot) & 1
        for i in range(4):
            block = values_in[:, i * width : (i + 1) * width]
            apart = ten ^ i
            for out, odd in ((keep_o, 0), (send_o, 1)):
                for side in range(2):

                    @pl.when(((apart & 1) == odd) & (spot == side))
                    def _():
                        out[apart >> 1, slot >> 1, :, side * width : (side + 1) * width] = block

    def attend_back_kernel(
        s, branch_in, q, k, v, probs, x, msg, w, vrow, wo, *refs
    ):
        extra = refs[0] if s == 0 else None
        back_o, grads_o, low_o, small_o = refs[-4:]
        gain, shift = vrow[0:1], vrow[1:2]
        here = lax.broadcasted_iota(jnp.int32, (rows, model), 0) == patch
        grad_mixed = nt(branch_in[...], wo[...]).astype(BF16)
        dq = jnp.zeros((rows, width), F32)
        dk = jnp.zeros((rows, width), F32)
        dv = jnp.zeros((rows, width), F32)
        for h, mask in enumerate(head_masks(rows)):
            grad_head = only(mask, grad_mixed)
            low_probs = probs[h]
            wide = low_probs.astype(F32)
            dv = dv + tn(low_probs, grad_head)
            grad_probs = nt(grad_head, v[...])
            inner = jnp.sum(wide * grad_probs, axis=-1, keepdims=True)
            grad_scores = (wide * (grad_probs - inner)).astype(BF16)
            dq = dq + only(mask, nn(grad_scores, k[...]))
            dk = dk + tn(grad_scores, only(mask, q[...]))
        dq = (dq * scale).astype(BF16)
        dk = (dk * scale).astype(BF16)
        dv = dv.astype(BF16)
        grads_o[0] = dq
        grads_o[1] = dk
        grads_o[2] = dv
        grad_low = nn(dq, w[0]) + nn(dk, w[1]) + nn(dv, w[2])
        token = jnp.where(here, msg[s : s + 1], x[...].astype(F32))
        normed, inverse = norm_parts(token)
        low_o[...] = (normed * gain + shift).astype(BF16)
        back = norm_back(grad_low, normed, inverse, gain)
        small_o[...] = jnp.zeros_like(small_o)
        small_o[0:1, :] = row_sum(only(here, back))
        small_o[1:2, :] = row_sum(grad_low * normed)
        small_o[2:3, :] = row_sum(grad_low)
        small_o[3:4, 0:width] = row_sum(dq.astype(F32))
        small_o[3:4, 256 : 256 + width] = row_sum(dv.astype(F32))
        if s == 0:
            back = back + extra[...]
        back_o[...] = back.astype(BF16)

    def attend_back(s, low_grad, kept):
        _, mixed, probs, k, v = kept
        ins = [low_grad, q_one[s], k, v, probs, x_slots[s], msg_rows, w_in, vec, w_out]
        return stage(
            functools.partial(attend_back_kernel, s),
            ins + ([grad_resid] if s == 0 else []),
            [
                near((rows, model), BF16),
                near((3, rows, width), BF16),
                near((rows, model), BF16),
                near((8, model), F32),
            ],
            flops=2 * rows * (4 * width * model + 4 * heads * rows * HEAD_DIM),
        )

    column_shapes = [near((2, 2, rows, 2 * width), BF16)] * 2

    def column_kernel(b0, b1, b2, b3, keep_o, send_o):
        for s, ref in enumerate((b0, b1, b2, b3)):
            column_out(ref[...], s, keep_o, send_o)

    def mlp_kernel(h0, h1, h2, h3, w, resid, vecs, *outs):
        for s, h in enumerate((h0, h1, h2, h3)):
            out = nn(h[...], w[...])
            if s == 0:
                out = out + resid[...] + vecs[4:5]
            outs[s][...] = out.astype(BF16)

    def far_columns(keep, got):
        def kernel(a, b, near_o, far_o):
            for i in range(2):
                near_o[i] = add(a[0, i], b[0, i]).astype(BF16)
                far_o[i ^ 1] = add(a[1, i], b[1, i]).astype(BF16)

        kept, send = stage(kernel, [keep, got], [near((2, rows, 2 * width), BF16)] * 2)
        return kept, x_swap(send)

    def frames_of(kept, far):
        low_pair = lax.axis_index("tensor") >> 1
        for i in range(2):
            total = add(kept[i], far[i])
            for side in range(2):
                yield (low_pair ^ i) * 2 + side, total[:, side * width : (side + 1) * width]

    def attend_weight_half_kernel(ga, gb, la, lb, ma, mb, ba, bb, out):
        for c in range(3):
            at = slice(c * width, (c + 1) * width)
            out[at, :] = tn(ga[c], la[...])
            out[at, :] += tn(gb[c], lb[...])
        out[3 * width :, :] = tn(ma[...], ba[...])
        out[3 * width :, :] += tn(mb[...], bb[...])

    def pack_kernel(s0, s1, s2, s3, two, p0, p1, p2, p3, out, acc):
        ten = lax.axis_index("tensor")
        acc[...] = jnp.zeros_like(acc)
        for s, ref in enumerate((s0, s1, s2, s3)):
            acc[pl.ds(ten ^ s, 1), :] = ref[0:1, :]
        acc[4:6, :] = s0[1:3, :] + s1[1:3, :] + s2[1:3, :] + s3[1:3, :]
        acc[6:10, :] = two[0:4, :]
        acc[pl.ds(10 + ten, 1), :] = p0[...] + p1[...] + p2[...] + p3[...]
        acc[pl.ds(14 + ten, 1), :] = s0[3:4, :] + s1[3:4, :] + s2[3:4, :] + s3[3:4, :]
        out[...] = acc[...].astype(BF16)

    def attend_weight_kernel(so_far, ga, gb, la, lb, ma, mb, ba, bb, keep, send, acc):
        for c in range(3):
            at = slice(c * width, (c + 1) * width)
            acc[at, :] = so_far[at, :] + tn(ga[c], la[...])
            acc[at, :] += tn(gb[c], lb[...])
        acc[3 * width :, :] = so_far[3 * width :, :] + tn(ma[...], ba[...])
        acc[3 * width :, :] += tn(mb[...], bb[...])
        halves_of(acc, keep, send)

    def merge_kernel(mine, other, out):
        a, b = mine[...].astype(F32), other[...].astype(F32)
        early = lax.axis_index("pipe") == 0
        out[...] = jnp.concatenate(
            [
                jnp.where(early, a[:half], b[:half]),
                jnp.where(early, b[:half], a[:half]),
                a[half : half + 24] + b[half : half + 24],
            ],
            axis=0,
        ).astype(BF16)

    def message_back(*refs):
        pack_refs, refs = refs[:pack_blocks], refs[pack_blocks:]
        (first, q, k, v, probs, w, wo, vrow, sent_o, grads_o, back_o) = refs
        sent = jnp.concatenate(
            [clip_block(pack_refs, c, pack_rows).astype(F32)[:frame_count] for c in range(clips)],
            axis=0,
        )
        low = sent.astype(BF16)
        sent_o[...] = sent
        grad_mixed = nt(low, wo[...]).astype(BF16)
        dq = jnp.zeros((all_rows, width), F32)
        dk = jnp.zeros((all_rows, width), F32)
        dv = jnp.zeros((all_rows, width), F32)
        for h, mask in enumerate(head_masks(all_rows)):
            grad_head = only(mask, grad_mixed)
            wide = probs[h]
            dv = dv + tn(wide.astype(BF16), grad_head)
            grad_probs = nt(grad_head, v[...])
            inner = jnp.sum(wide * grad_probs, axis=-1, keepdims=True)
            grad_scores = (wide * (grad_probs - inner)).astype(BF16)
            dq = dq + only(mask, nn(grad_scores, k[...]))
            dk = dk + tn(grad_scores, only(mask, q[...]))
        dq = (dq * scale).astype(BF16)
        dk = (dk * scale).astype(BF16)
        dv = dv.astype(BF16)
        grads_o[0] = dq
        grads_o[1] = dk
        grads_o[2] = dv
        grad_low = nn(dq, w[0]) + nn(dk, w[1]) + nn(dv, w[2])
        normed, inverse = norm_parts(first[...])
        back_msg = norm_back(grad_low, normed, inverse, vrow[0:1])
        back_o[0:all_rows, :] = back_msg.astype(BF16)
        tail = jnp.concatenate(
            [row_sum(grad_low * normed), row_sum(grad_low), jnp.zeros((14, model), F32)], axis=0
        )
        back_o[all_rows:, :] = tail.astype(BF16)

    def message_weight(sent, grads_in, low, mixed, in_o, out_o, qv_o, bias_o):
        for c in range(3):
            in_o[c] = tn(grads_in[c], low[...])
        out_o[...] = tn(mixed[...], sent[...].astype(BF16))
        qv_o[0:1, :] = row_sum(grads_in[0].astype(F32))
        qv_o[1:2, :] = row_sum(grads_in[2].astype(F32))
        bias_o[...] = row_sum(sent[...])

    def block_out_kernel(*refs):
        for at, total in frames_of(*refs[:-1]):
            refs[-1][at] = total.T[:, :patch].astype(BF16)

    def message_end(*refs):
        pack_refs, refs = refs[:pack_blocks], refs[pack_blocks:]
        cls_refs, refs = refs[:blocks], refs[blocks:]
        (sent, own, late, mw, qv_in, bias_in, w_o, cls_o, vec_o, qv_o, turned, sums) = refs
        sec, ten = lax.axis_index("pipe"), lax.axis_index("tensor")
        total = jnp.where(sec == 0, own[...].astype(F32), late[...].astype(F32))
        grad_first = sent[...] + total[:all_rows]
        at = pl.ds(pl.multiple_of(ten * width, width), width)
        mine = grad_first[:16]
        high = mine.astype(BF16)
        rest = (mine - high.astype(F32)).astype(BF16)
        mw_rows = mw[at, :]
        cls_o[...] = nt(high, mw_rows) + nt(rest, mw_rows)
        turned[...] = grad_first.T
        mine = turned[at, :]
        high = mine.astype(BF16)
        rest = (mine - high.astype(F32)).astype(BF16)
        cls = jnp.concatenate([clip_block(cls_refs, c, frame_count).astype(F32) for c in range(clips)])
        cls = cls.astype(BF16)
        w_o[...] = nn(high, cls) + nn(rest, cls)
        summed = clip_block(pack_refs, 0, pack_rows).astype(F32)
        for c in range(1, clips):
            summed = summed + clip_block(pack_refs, c, pack_rows).astype(F32)
        sums[...] = summed[frame_count:]
        first_one = sec == 0
        vec_o[0:1, :] = jnp.where(first_one, total[all_rows : all_rows + 1], sums[0:1])
        vec_o[1:2, :] = jnp.where(first_one, total[all_rows + 1 : all_rows + 2], sums[1:2])
        vec_o[2:3, :] = jnp.where(first_one, bias_in[...], sums[4:5])
        vec_o[3:4, :] = sums[2:3]
        vec_o[4:5, :] = sums[3:4]
        vec_o[5:6, :] = sums[5:6]
        vec_o[6:7, :] = sums[pl.ds(6 + ten, 1), :]
        vec_o[7:8, :] = row_sum(grad_first)
        qv_row = sums[pl.ds(10 + ten, 1), :]
        qv_o[0:1, :] = jnp.where(first_one, qv_in[0:1], qv_row[:, :width])
        qv_o[1:2, :] = jnp.where(first_one, qv_in[1:2], qv_row[:, 256 : 256 + width])

    def frames_grad_kernel(*refs):
        cls, out = refs[-2:]
        top = lax.broadcasted_iota(jnp.int32, (rows, width), 0) == 0
        for at, total in frames_of(*refs[:-2]):
            row = cls[pl.ds(lax.axis_index("pipe") * half + at, 1), :]
            out[at] = (total + jnp.where(top, row, 0.0)).T[:, :patch].astype(BF16)

    def attend_whole_kernel(keep, other, in_zero_ref, out_zero_ref, in_o, out_o, acc):
        @pl.when(lax.axis_index("pipe") == 0)
        def _():
            in_o[...] = in_zero_ref[...]
            out_o[...] = out_zero_ref[...]

        @pl.when(lax.axis_index("pipe") == 1)
        def _():
            put_halves(keep, other, acc)
            for c in range(3):
                in_o[c] = acc[c * width : (c + 1) * width, :]
            out_o[...] = acc[3 * width :, :]

    def pack_join_kernel(a, b, out):
        size = a.shape[0]
        out[0:size, :] = a[...]
        out[size:, :] = b[...]

    stage.cost = 0
    sent_out = y_early(own_out)
    cls_all = gather_clips(frames[0, :, 0, :])
    vectors, own_vec, near_in, in_and_vec = stage(
        small_kernel,
        [
            own_in, msg_bias, norm2_gain, norm2_shift, fc_in_bias, fc_out_bias,
            norm_gain, norm_shift, out_bias, qv_bias,
        ],
        [near((8, model), F32)] * 2 + [near(own_in.shape, BF16), near((3 * width + 16, model), BF16)],
        [pltpu.VMEM((model,), F32)] * 5
        + [pltpu.VMEM((1, model), F32)] * 3
        + [pltpu.VMEM((1, 2, width), F32), pltpu.SemaphoreType.DMA((13,))],
        far=10,
    )
    sent_in = y_early(in_and_vec)
    near_msg_w, near_out = stage(
        load_kernel, [msg_w, own_out], [near(msg_w.shape, BF16), near(own_out.shape, BF16)],
        [pltpu.SemaphoreType.DMA((2,))],
        far=2,
    )
    x_slots = slots(tokens, half)
    (first_msg, low_zero, q_zero, k_zero, v_zero, probs_zero, mixed_zero, part_zero) = stage(
        message_forward,
        [video_group, *cls_all, near_msg_w, vectors, own_vec, near_in, near_out],
        [
            near((all_rows, model), F32),
            near((all_rows, model), BF16),
            near((all_rows, width), BF16),
            near((all_rows, width), BF16),
            near((all_rows, width), BF16),
            near((heads, all_rows, all_rows), F32),
            near((all_rows, width), BF16),
            near((frame_count, model), F32),
        ],
        [pltpu.SMEM(video_group.shape, jnp.int32), pltpu.SemaphoreType.DMA],
        far=1,
    )
    from_core = core_swap(part_zero)
    (part_zero,) = adds((part_zero, from_core))
    from_x = x_swap(part_zero)
    (part_zero,) = adds((part_zero, from_x))
    part_late = y_late(part_zero)
    w_in, vec, *projected = stage(
        project_kernel, [*x_slots, near_in, sent_in, own_vec],
        [near(own_in.shape, BF16), near(own_vec.shape, F32)] + [near((rows, width), BF16)] * 12,
    )
    stage.cost = 0
    q_one, k_patch, v_patch = projected[:4], projected[4:8], projected[8:]
    msg_rows, k_msg, v_msg = stage(
        message_rows_kernel, [first_msg, part_zero, part_late, w_in, vec],
        [near((16, model), F32), near((16, width), F32), near((16, width), F32)],
    )

    at3 = (None, *attend(3))
    at2 = (None, *attend(2))
    pr3, w_out = stage(
        first_out_kernel, [at3[1], near_out, sent_out],
        [near((rows, model), BF16), near(own_out.shape, BF16)],
    )
    ac3 = core_swap(pr3)
    stage.cost = 4 * 10**9
    (pr2,) = stage(out_kernel, [at2[1], w_out], [near((rows, model), BF16)])
    two0, two1 = add_parts(pr2, ac3)
    ax0 = x_swap(two0)
    ax1 = x_swap(two1)
    at1 = attend(1, w_out)
    ac1 = core_swap(at1[0])
    at0 = attend(0, w_out)
    g_slots = slots(grads_in, 2 * half)
    (aown,) = adds((at0[0], ac1))
    resid0, low0 = stage(
        residual_first_kernel, [aown, ax0, x_slots[0], vec, vectors],
        [near((first_rows, model), F32), near((first_rows, model), BF16)],
    )
    lx0 = x_swap(low0)
    resid_own, low_own, low1 = stage(
        residual_last_kernel, [aown, ax1, x_slots[0], vec, vectors, resid0, low0],
        [near((rows, model), F32), near((rows, model), BF16), near((rows - first_rows, model), BF16)],
    )
    lx1 = x_swap(low1)
    l1 = core_swap(low_own)
    ly = y_swap(low_own)
    g_hidden = stage(
        grad_hidden_kernel, [*g_slots[:half], fc_out], [near((rows, hidden_width), BF16)] * half,
    )
    hid0, pre0, gp0, bs0 = feed(low_own, g_hidden[0])
    hid1, pre1, gp1, bs1 = feed(l1, g_hidden[1])
    fc1 = core_swap(gp1)
    fc_out_half = own_part(own_out_kernel, (half_rows, model), hid0, hid1, g_slots[0], g_slots[1])
    (fown,) = adds((gp0, fc1))
    l2 = join_parts(lx0, lx1)
    l3 = core_swap(l2)
    ly2 = y_swap(l2)
    hid2, pre2, gp2, bs2 = feed(l2, g_hidden[2])
    hid3, pre3, gp3, bs3 = feed(l3, g_hidden[3])
    fc3 = core_swap(gp3)
    m0 = relay(ly)
    m1 = core_swap(m0)
    two0, two1 = add_parts(gp2, fc3)
    fx0 = x_swap(two0)
    fx1 = x_swap(two1)
    ho0, po0 = feed_other(m0, g_slots[4])
    ho1, po1 = feed_other(m1, g_slots[5])
    block_parts = stage(
        mlp_kernel, [hid0, hid1, hid2, hid3, fc_out, resid_own, vectors],
        [near((rows, model), BF16)] * half,
    )
    fc_in_half = own_part(own_in_kernel, (model, half_rows), low_own, l1, pre0, pre1)
    grad0, glow0, small0 = stage(
        residual_back_first_kernel, [fown, fx0, resid_own, g_slots[0], vectors],
        [near((first_rows, model), F32), near((first_rows, model), BF16), near((8, model), F32)],
    )
    bx0 = x_swap(glow0)
    m2 = relay(ly2)
    m3 = core_swap(m2)
    grad_resid, grad_low, glow1, small_two = stage(
        residual_back_last_kernel,
        [fown, fx1, resid_own, g_slots[0], vectors, grad0, glow0, small0],
        [
            near((rows, model), F32), near((rows, model), BF16),
            near((rows - first_rows, model), BF16), near((8, model), F32),
        ],
    )
    bx1 = x_swap(glow1)
    b1 = core_swap(grad_low)
    ho2, po2 = feed_other(m2, g_slots[6])
    ho3, po3 = feed_other(m3, g_slots[7])
    p0 = whole_part(
        sum_out_kernel, fc_out_half, hid2, hid3, g_slots[2], g_slots[3], ho0, ho1, ho2, ho3, *g_slots[half:],
    )
    q0 = whole_part(
        sum_in_kernel, fc_in_half, l2, l3, pre2, pre3, m0, m1, m2, m3, po0, po1, po2, po3,
    )
    ba0, gr0, lo0, sm0 = attend_back(0, grad_low, at0)
    ba1, gr1, lo1, sm1 = attend_back(1, b1, at1)
    (attend_half,) = stage(
        attend_weight_half_kernel, [gr0, gr1, lo0, lo1, at0[1], at1[1], grad_low, b1],
        [near((4 * width, model), F32)],
    )
    b2 = join_parts(bx0, bx1)
    b3 = core_swap(b2)
    ba2, gr2, lo2, sm2 = attend_back(2, b2, at2)
    p1 = over_far_clip(*p0)
    ba3, gr3, lo3, sm3 = attend_back(3, b3, at3)
    (pk0,) = stage(
        pack_kernel, [sm0, sm1, sm2, sm3, small_two, bs0, bs1, bs2, bs3], [near((32, model), BF16)],
        [pltpu.VMEM((32, model), F32)],
    )
    pkc = core_swap(pk0)
    r0 = over_sections(
        *stage(
            attend_weight_kernel,
            [attend_half, gr2, gr3, lo2, lo3, at2[1], at3[1], b2, b3],
            half_shapes,
            [pltpu.VMEM((4 * width, model), F32)],
        )
    )
    (pk1,) = adds((pk0, pkc))
    pkx = x_swap(pk1)
    q1 = over_far_clip(*q0)
    p2 = to_far_clip(*p1)
    (pk2,) = adds((pk1, pkx))
    pky = y_swap(pk2)
    r1 = over_near_clip(*r0)
    q2 = to_far_clip(*q1)
    (pk3,) = stage(merge_kernel, [pk2, pky], [near((32, model), BF16)])
    pack_rows = pk3.shape[0]
    pkz = z_swap(pk3, 1) if ring else None
    p3 = to_near_clip(*p2)
    r2 = over_far_clip(*r1)
    if ring:
        (pk4,) = stage(pack_join_kernel, [pk3, pkz], [near((2 * pack_rows, model), BF16)])
        packs = [pk4, z_swap(pk4, 2)]
    else:
        packs = gather_clips(pk3)
    stage.cost = 0
    q3 = to_near_clip(*q2)
    stage.cost = 4 * 10**9
    p4 = to_other_section(*p3)
    sent_all, grads_zero, bz0 = stage(
        message_back,
        [*packs, first_msg, q_zero, k_zero, v_zero, probs_zero, near_in, near_out, own_vec],
        [
            near((all_rows, model), F32),
            near((3, all_rows, width), BF16),
            near((all_rows + 16, model), BF16),
        ],
    )
    bzc = core_swap(bz0)
    stage.cost = 10**10
    in_zero, out_zero, qv_zero, bias_zero = stage(
        message_weight, [sent_all, grads_zero, low_zero, mixed_zero],
        [
            near((3, width, model), F32),
            near((width, model), F32),
            near((2, width), F32),
            near((1, model), F32),
        ],
    )
    stage.cost = 4 * 10**9
    (bz1,) = adds((bz0, bzc))
    bzx = x_swap(bz1)
    r3 = to_far_clip(*r2)
    q4 = to_other_section(*q3)
    (bz2,) = adds((bz1, bzx))
    bzy = y_late(bz2)
    ck, send = stage(column_kernel, [ba0, ba1, ba2, ba3], column_shapes)
    cs = core_swap(send)
    msg_w_grad, cls_part, vec_grads, qv_grad = stage(
        message_end,
        [*packs, *cls_all, sent_all, bz2, bzy, near_msg_w, qv_zero, bias_zero],
        [
            shape_of((width, model), F32),
            near((16, width), F32),
            near((8, model), F32),
            near((2, width), F32),
        ],
        [pltpu.VMEM((model, all_rows), F32), pltpu.VMEM((24, model), F32)],
    )
    fc_out_grad = whole(*p4)
    kept, far = far_columns(ck, cs)
    bk, send = stage(column_kernel, block_parts, column_shapes)
    bcs = core_swap(send)
    r4 = to_near_clip(*r3)
    (frames_grad,) = stage(
        frames_grad_kernel, [kept, far, cls_part], [shape_of((half, width, patch), BF16)],
    )
    r5 = to_sections(*r4, move=y_late)
    bkept, bfar = far_columns(bk, bcs)
    fc_in_grad = whole_of_columns(*q4)
    (block_out,) = stage(
        block_out_kernel, [bkept, bfar], [shape_of((half, width, patch), BF16)],
    )
    attn_in_grad, attn_out_grad = stage(
        attend_whole_kernel, [*r5, in_zero, out_zero],
        [shape_of((3, width, model), F32), shape_of((width, model), F32)],
        [pltpu.VMEM((4 * width, model), F32)],
    )

    return (
        jnp.swapaxes(block_out, 1, 2)[None],
        jnp.swapaxes(frames_grad, 1, 2)[None],
        msg_w_grad.T,
        vec_grads[7],
        vec_grads[0:1],
        vec_grads[1:2],
        jnp.transpose(attn_in_grad, (2, 0, 1))[None],
        qv_grad[None],
        attn_out_grad[None],
        vec_grads[2:3],
        vec_grads[3],
        vec_grads[4],
        fc_in_grad,
        vec_grads[6],
        fc_out_grad,
        vec_grads[5],
    )


def solution(mesh):
    return jax.shard_map(
        body,
        mesh=mesh,
        in_specs=(
            P("dp", None, None, None),
            P(),
            P(),
            P(),
            P("pipe", None),
            P("pipe", None),
            P("pipe", None, None, "tensor"),
            P("pipe", None, "tensor"),
            P("pipe", "tensor", None),
            P("pipe", None),
            P(),
            P(),
            P(None, "tensor"),
            P("tensor"),
            P("tensor", None),
            P(),
            P("dp", None, None, None),
        ),
        out_specs=(
            P("dp", "pipe", None, "tensor"),
            P("dp", "pipe", None, "tensor"),
            P(None, "tensor"),
            P(),
            P("pipe", None),
            P("pipe", None),
            P("pipe", None, None, "tensor"),
            P("pipe", None, "tensor"),
            P("pipe", "tensor", None),
            P("pipe", None),
            P(),
            P(),
            P(None, "tensor"),
            P("tensor"),
            P("tensor", None),
            P(),
        ),
        check_vma=False,
    )
```

```python
import functools

import jax
import jax.numpy as jnp
from jax import lax
from jax.experimental import pallas as pl
from jax.experimental.pallas import tpu as pltpu
from jax.sharding import PartitionSpec as P

HEAD_DIM = 64
EPSILON = 1e-05
QUICK_GELU = 1.702
F32 = jnp.float32
BF16 = jnp.bfloat16
VMEM_BYTES = 16 * 1024 * 1024


def nn(left, right):
    return lax.dot_general(left, right, (((1,), (0,)), ((), ())), preferred_element_type=F32)


def nt(left, right):
    return lax.dot_general(left, right, (((1,), (1,)), ((), ())), preferred_element_type=F32)


def tn(left, right):
    return lax.dot_general(left, right, (((0,), (0,)), ((), ())), preferred_element_type=F32)


def norm_parts(values_in):
    centred = values_in - jnp.mean(values_in, axis=-1, keepdims=True)
    inverse = lax.rsqrt(jnp.mean(centred * centred, axis=-1, keepdims=True) + EPSILON)
    return centred * inverse, inverse


def norm_back(incoming, normed, inverse, gain):
    weighted = incoming * gain
    centred = weighted - jnp.mean(weighted, axis=-1, keepdims=True)
    return inverse * (centred - normed * jnp.mean(weighted * normed, axis=-1, keepdims=True))


def row_sum(values_in):
    return jnp.sum(values_in, axis=0, keepdims=True)


def shape_of(shape, kind):
    return jax.ShapeDtypeStruct(shape, kind)


def near(shape, kind):
    return pltpu.VMEM(shape, kind)


class Chain:
    def __init__(self):
        self.token = None
        self.near, self.kept = set(), []
        self.cost = 4 * 10**9

    def __call__(self, kernel, ins, outs, scratch=(), flops=0, far=0):
        tokens = 0 if self.token is None else 1
        count, given = len(ins), len(outs)

        def stage(*refs):
            rest = refs[tokens:]
            kernel(*rest[:count], *rest[count : count + given], *rest[count + given + 1 :])

        vmem = pl.BlockSpec(memory_space=pltpu.VMEM)
        held = [] if self.token is None else [self.token]
        ins = [
            pltpu.with_memory_space_constraint(a, pltpu.HBM)
            if i < far
            else pltpu.with_memory_space_constraint(a, pltpu.VMEM)
            if id(a) in self.near
            else a
            for i, a in enumerate(ins)
        ]
        results = pl.pallas_call(
            stage,
            out_shape=[*outs, near((8, 128), F32)],
            in_specs=[pl.BlockSpec(memory_space=pl.ANY)] * tokens
            + [pl.BlockSpec(memory_space=pltpu.HBM)] * far
            + [vmem] * (count - far),
            out_specs=[vmem] * (given + 1),
            scratch_shapes=list(scratch),
            compiler_params=pltpu.CompilerParams(vmem_limit_bytes=VMEM_BYTES),
            cost_estimate=pl.CostEstimate(flops=self.cost, bytes_accessed=0, transcendentals=0),
        )(*held, *ins)
        self.token = results[-1]
        self.kept += results
        for out, result in zip(outs, results):
            if not isinstance(out, jax.ShapeDtypeStruct):
                self.near.add(id(result))
        return results[:-1]


def body(
    frames,
    video_group,
    msg_w,
    msg_bias,
    norm_gain,
    norm_shift,
    attn_in,
    qv_bias,
    attn_out,
    out_bias,
    norm2_gain,
    norm2_shift,
    fc_in,
    fc_in_bias,
    fc_out,
    fc_out_bias,
    cotangent,
):
    _, frame_count, patch, model = frames.shape

    width = attn_in.shape[-1]

    hidden_width = fc_in.shape[-1]

    heads = width // HEAD_DIM

    clips = lax.axis_size("dp")

    half = frame_count // 2

    rows = -(-(patch + 1) // 16) * 16

    all_rows = clips * frame_count

    scale = HEAD_DIM ** (-0.5)

    pipe = lax.axis_index("pipe")

    tensor = lax.axis_index("tensor")

    clip = lax.axis_index("dp")

    ring = clips == 4

    stage = Chain()

    quarter = hidden_width // 4

    assert quarter == width and hidden_width == model and half == 4

    def tensor_swap(v, bit):
        return lax.ppermute(v, "tensor", [(i, i ^ bit) for i in range(4)])

    def core_swap(v):
        return tensor_swap(v, 1)

    def x_swap(v):
        return tensor_swap(v, 2)

    def y_swap(v):
        return lax.ppermute(v, "pipe", [(0, 1), (1, 0)])

    def y_late(v):
        return lax.ppermute(v, "pipe", [(0, 1)])

    def y_early(v):
        return lax.ppermute(v, "pipe", [(1, 0)])

    def z_swap(v, bit):
        return lax.ppermute(v, "dp", [(i, i ^ bit) for i in range(clips)])

    def gather_clips(v):
        if ring:
            return [v] + [z_swap(v, apart) for apart in range(1, clips)]
        every = lax.all_gather(v, "dp")
        every = lax.dynamic_slice_in_dim(jnp.concatenate([every, every]), clip, clips, 0)
        return [every.reshape(clips * v.shape[0], v.shape[1])]

    def clip_block(refs, c, size):
        each = clips // len(refs)
        at = c % each * size
        return refs[c // each][at : at + size, :]

    blocks = clips if ring else 1

    pack_blocks = 2 if ring else 1

    def head_masks(n):
        lane = lax.broadcasted_iota(jnp.int32, (n, width), 1)
        return [(lane >= h * HEAD_DIM) & (lane < (h + 1) * HEAD_DIM) for h in range(heads)]

    def only(mask, v):
        return jnp.where(mask, v, jnp.zeros_like(v))

    def add(*terms):
        total = terms[0].astype(F32)
        for term in terms[1:]:
            total = total + term.astype(F32)
        return total

    def adds(*groups):
        sizes = [len(group) for group in groups]

        def kernel(*refs):
            at = 0
            for size, out in zip(sizes, refs[sum(sizes) :]):
                out[...] = add(*[ref[...] for ref in refs[at : at + size]]).astype(out.dtype)
                at += size

        return stage(
            kernel,
            [array for group in groups for array in group],
            [near(group[0].shape, group[0].dtype) for group in groups],
        )

    own_in = jnp.transpose(attn_in[0], (1, 2, 0))

    own_out = attn_out[0]

    tokens = jnp.transpose(frames[0], (1, 0, 2))

    grads_in = jnp.transpose(cotangent[0], (1, 0, 2))

    def small_kernel(*refs):
        ins, vecs_o, own_o, in_o, both_o = refs[:10], *refs[10:14]
        lines, rest, sem = refs[14:19], refs[19:23], refs[23]
        pairs = [(ins[0], in_o)] + list(zip(ins[1:], (*lines, *rest)))
        pairs += [(ins[0].at[c], both_o.at[c * width : (c + 1) * width]) for c in range(3)]
        copies = [pltpu.make_async_copy(a, b, sem.at[i]) for i, (a, b) in enumerate(pairs)]
        for copy in copies:
            copy.start()
        for copy in copies:
            copy.wait()
        for i, line in enumerate(lines):
            vecs_o[i : i + 1, :] = line[...].reshape(1, model)
        for i, line in enumerate(rest[:3]):
            own_o[i : i + 1, :] = line[...]
        own_o[3:8, :] = jnp.zeros((5, model), F32)
        own_o[3:5, 0:width] = rest[3][0]
        high = own_o[...].astype(BF16).astype(F32)
        both_o[3 * width :, :] = jnp.concatenate([high, own_o[...] - high], axis=0).astype(BF16)

    def load_kernel(*refs):
        sem = refs[4]
        copies = [
            pltpu.make_async_copy(a, b, sem.at[i]) for i, (a, b) in enumerate(zip(refs[:2], refs[2:4]))
        ]
        for copy in copies:
            copy.start()
        for copy in copies:
            copy.wait()

    tokens_all = rows * frame_count

    lanes = 128

    def slot_kernel(v, *refs):
        outs, (wide, held, sem) = refs[:-3], refs[-3:]
        copy = pltpu.make_async_copy(v, held, sem)
        copy.start()
        copy.wait()
        flat = held[...].astype(F32).reshape(patch * frame_count, model)
        sec, ten = lax.axis_index("pipe"), lax.axis_index("tensor")
        for c in range(model // lanes):
            at = c * tokens_all
            wide[at : at + patch * frame_count, :] = flat[:, c * lanes : (c + 1) * lanes]
            wide[at + patch * frame_count : at + tokens_all, :] = jnp.zeros(
                ((rows - patch) * frame_count, lanes), F32
            )
            for s, out in enumerate(outs):
                frame = at + (sec if s < half else 1 - sec) * half + (ten ^ (s % half))
                out[:, c * lanes : (c + 1) * lanes] = wide[
                    pl.ds(frame, rows, stride=frame_count), :
                ].astype(BF16)

    def slots(v, count):
        return stage(
            slot_kernel,
            [v],
            [near((rows, model), BF16)] * count,
            [
                pltpu.VMEM((model // lanes * tokens_all, lanes), F32),
                pltpu.VMEM((patch, frame_count, model), BF16),
                pltpu.SemaphoreType.DMA,
            ],
            far=1,
        )

    def message_forward(groups, *refs):
        cls_refs, refs = refs[:blocks], refs[blocks:]
        (mw, vecs, vrow, w, wo, first_o, low_o, q_o, k_o, v_o, probs_o, mixed_o, part_o, ids, sem) = refs
        copy = pltpu.make_async_copy(groups, ids, sem)
        copy.start()
        cls = jnp.concatenate([clip_block(cls_refs, c, frame_count).astype(F32) for c in range(clips)])
        first = nn(cls.astype(BF16), mw[...]) + vecs[0:1]
        first_o[...] = first
        normed, _ = norm_parts(first)
        low = (normed * vrow[0:1] + vrow[1:2]).astype(BF16)
        low_o[...] = low
        q = (nt(low, w[0]) + vrow[3:4, :width]).astype(BF16)
        k = nt(low, w[1]).astype(BF16)
        v = (nt(low, w[2]) + vrow[4:5, :width]).astype(BF16)
        q_o[...] = q
        k_o[...] = k
        v_o[...] = v
        of_row = lax.broadcasted_iota(jnp.int32, (all_rows, all_rows), 0) // frame_count
        of_col = lax.broadcasted_iota(jnp.int32, (all_rows, all_rows), 1) // frame_count
        mine = lax.axis_index("dp")
        copy.wait()
        row_id = jnp.zeros((all_rows, all_rows), jnp.int32)
        col_id = jnp.zeros((all_rows, all_rows), jnp.int32)
        for c in range(clips):
            mark = ids[mine ^ c if ring else lax.rem(mine + c, clips)]
            row_id = jnp.where(of_row == c, mark, row_id)
            col_id = jnp.where(of_col == c, mark, col_id)
        allowed = row_id == col_id
        mixed = jnp.zeros((all_rows, width), F32)
        for h, mask in enumerate(head_masks(all_rows)):
            scores = jnp.where(allowed, nt(only(mask, q), k) * scale, -jnp.inf)
            exponent = jnp.exp(scores - jnp.max(scores, axis=-1, keepdims=True))
            probs = exponent / jnp.sum(exponent, axis=-1, keepdims=True)
            probs_o[h] = probs
            mixed = mixed + only(mask, nn(probs.astype(BF16), v))
        mixed = mixed.astype(BF16)
        mixed_o[...] = mixed
        part = nn(mixed, wo[...]) + jnp.where(lax.axis_index("tensor") == 0, vrow[2:3], 0.0)
        part_o[...] = part[:frame_count]

    def project_kernel(x0, x1, x2, x3, wa, wb, va, w, vrow, *outs):
        early = lax.axis_index("pipe") == 0
        for c in range(3):
            w[c] = jnp.where(early, wb[c * width : (c + 1) * width, :], wa[c])
        sent = wb[3 * width :, :].astype(F32)
        vrow[...] = jnp.where(early, sent[0:8] + sent[8:16], va[...])
        gain, shift = vrow[0:1], vrow[1:2]
        for s, x in enumerate((x0, x1, x2, x3)):
            normed, _ = norm_parts(x[...].astype(F32))
            low = (normed * gain + shift).astype(BF16)
            outs[s][...] = (nt(low, w[0]) + vrow[3:4, :width]).astype(BF16)
            outs[half + s][...] = nt(low, w[1]).astype(BF16)
            outs[2 * half + s][...] = (nt(low, w[2]) + vrow[4:5, :width]).astype(BF16)

    def message_rows_kernel(first, part, late, w, vrow, msg_o, k_o, v_o):
        sec, ten = lax.axis_index("pipe"), lax.axis_index("tensor")
        msg_o[...] = jnp.zeros_like(msg_o)
        for s in range(half):
            at = pl.ds(sec * half + (ten ^ s), 1)
            summed = jnp.where(sec == 0, part[at, :], late[at, :])
            msg_o[s : s + 1, :] = (first[at, :] + summed).astype(BF16).astype(F32)
        normed, _ = norm_parts(msg_o[...])
        low = (normed * vrow[0:1] + vrow[1:2]).astype(BF16)
        k_o[...] = nt(low, w[1])
        v_o[...] = nt(low, w[2]) + vrow[4:5, :width]

    def attend_kernel(
        s, with_out, q, k, v, km, vm, *refs
    ):
        mixed_o, probs_o, k_o, v_o = refs[-4:]
        here = lax.broadcasted_iota(jnp.int32, (rows, width), 0) == patch
        key_here = lax.broadcasted_iota(jnp.int32, (rows, rows), 1) <= patch
        kk = jnp.where(here, km[s : s + 1], k[...].astype(F32)).astype(BF16)
        vv = jnp.where(here, vm[s : s + 1], v[...].astype(F32)).astype(BF16)
        k_o[...] = kk
        v_o[...] = vv
        mixed = jnp.zeros((rows, width), F32)
        for h, mask in enumerate(head_masks(rows)):
            scores = nt(only(mask, q[...]), kk) * scale
            scores = jnp.where(key_here, scores, -jnp.inf)
            exponent = jnp.exp(scores - jnp.max(scores, axis=-1, keepdims=True))
            probs = exponent * (1.0 / jnp.sum(exponent, axis=-1, keepdims=True))
            probs = probs.astype(BF16)
            probs_o[h] = probs
            mixed = mixed + only(mask, nn(probs, vv))
        mixed = mixed.astype(BF16)
        mixed_o[...] = mixed
        if with_out:
            wo, part_o = refs[:2]
            part_o[...] = nn(mixed, wo[...]).astype(BF16)

    def attend(s, *out):
        return stage(
            functools.partial(attend_kernel, s, bool(out)),
            [q_one[s], k_patch[s], v_patch[s], k_msg, v_msg, *out],
            [near((rows, model), BF16)] * len(out)
            + [
                near((rows, width), BF16),
                near((heads, rows, rows), BF16),
                near((rows, width), BF16),
                near((rows, width), BF16),
            ],
            flops=2 * rows * (width * model + 2 * heads * rows * HEAD_DIM),
        )

    def first_out_kernel(mixed, wa, wb, part_o, w_o):
        w_o[...] = jnp.where(lax.axis_index("pipe") == 0, wb[...], wa[...])
        part_o[...] = nn(mixed[...], w_o[...]).astype(BF16)

    def out_kernel(mixed, w, part_o):
        part_o[...] = nn(mixed[...], w[...]).astype(BF16)

    first_rows = rows // 32 * 16 + 16

    row_parts = (slice(0, first_rows), slice(first_rows, rows))

    def add_parts(a, b):
        def kernel(a_ref, b_ref, *outs):
            for at, out in zip(row_parts, outs):
                out[...] = add(a_ref[at, :], b_ref[at, :]).astype(BF16)

        return stage(
            kernel, [a, b], [near((at.stop - at.start, model), BF16) for at in row_parts]
        )

    def join_parts(a, b):
        def kernel(a_ref, b_ref, out):
            for at, ref in zip(row_parts, (a_ref, b_ref)):
                out[at, :] = ref[...]

        return stage(kernel, [a, b], [near((rows, model), a.dtype)])[0]

    def residual_of(at, a, b, x, vrow, vecs):
        resid = x[at, :].astype(F32) + add(a[at, :], b[...]) + vrow[2:3]
        normed, _ = norm_parts(resid)
        return resid, (normed * vecs[1:2] + vecs[2:3]).astype(BF16)

    def residual_first_kernel(a, b, x, vrow, vecs, resid_o, low_o):
        resid_o[...], low_o[...] = residual_of(row_parts[0], a, b, x, vrow, vecs)

    def residual_last_kernel(a, b, x, vrow, vecs, resid_in, low_in, resid_o, low_o, part_o):
        resid, low = residual_of(row_parts[1], a, b, x, vrow, vecs)
        for at, one, two in zip(row_parts, (resid_in[...], resid), (low_in[...], low)):
            resid_o[at, :] = one
            low_o[at, :] = two
        part_o[...] = low

    def relay_kernel(v, out):
        out[...] = v[...]

    def relay(v):
        return stage(relay_kernel, [v], [near(v.shape, v.dtype)])[0]

    def grad_hidden_kernel(g0, g1, g2, g3, w, *outs):
        for g, out in zip((g0, g1, g2, g3), outs):
            out[...] = nt(g[...], w[...]).astype(BF16)

    def feed_kernel(low, gh, w, vecs, hid_o, pre_o, grad_o, bias_o):
        hidden_in = nn(low[...], w[...]) + vecs[3:4]
        sig = 1.0 / (1.0 + jnp.exp(-QUICK_GELU * hidden_in))
        hid_o[...] = (hidden_in * sig).astype(BF16)
        slope = sig + QUICK_GELU * hidden_in * sig * (1.0 - sig)
        pre = (gh[...].astype(F32) * slope).astype(BF16)
        pre_o[...] = pre
        grad_o[...] = nt(pre, w[...]).astype(BF16)
        bias_o[...] = row_sum(pre.astype(F32))

    def feed(low, gh):
        return stage(
            feed_kernel, [low, gh, fc_in, vectors],
            [
                near((rows, hidden_width), BF16),
                near((rows, hidden_width), BF16),
                near((rows, model), BF16),
                near((1, hidden_width), F32),
            ],
            flops=2 * 2 * rows * model * hidden_width,
        )

    half_rows, eighth = model // 2, model // 8

    def halves_of(acc, keep, send):
        sec = lax.axis_index("pipe")
        for out, at in ((keep, sec), (send, 1 - sec)):
            start = pl.multiple_of(at * half_rows, half_rows)
            out[...] = acc[pl.ds(start, half_rows), :].astype(BF16)

    half_shapes = [near((half_rows, model), BF16)] * 2

    def section_columns():
        return pl.ds(pl.multiple_of(lax.axis_index("pipe") * half_rows, half_rows), half_rows)

    def feed_other_kernel(low, g, w, w_out, vecs, hid_o, pre_o):
        columns = section_columns()
        hidden_in = nn(low[...], w[:, columns]) + vecs[3:4, columns]
        sig = 1.0 / (1.0 + jnp.exp(-QUICK_GELU * hidden_in))
        hid_o[...] = (hidden_in * sig).astype(BF16)
        slope = sig + QUICK_GELU * hidden_in * sig * (1.0 - sig)
        pre_o[...] = (nt(g[...], w_out[columns, :]).astype(BF16).astype(F32) * slope).astype(BF16)

    def feed_other(low, g):
        return stage(
            feed_other_kernel, [low, g, fc_in, fc_out, vectors],
            [near((rows, half_rows), BF16)] * 2,
        )

    def own_out_kernel(h0, h1, g0, g1, out):
        out[...] = tn(h0[:, section_columns()], g0[...])
        out[...] += tn(h1[:, section_columns()], g1[...])

    def own_in_kernel(l0, l1, p0, p1, out):
        out[...] = tn(l0[...], p0[:, section_columns()])
        out[...] += tn(l1[...], p1[:, section_columns()])

    def own_part(kernel, shape, *ins):
        return stage(kernel, list(ins), [near(shape, F32)])[0]

    def clip_parts(acc, mine, send):
        size = mine.shape[0] // 2
        for out, first in ((mine, 0), (send, 1)):
            for at, apart in ((0, first), (size, first ^ 2)):
                out[at : at + size, :] = acc[clip_rows(apart, size), :].astype(BF16)

    def sum_out_kernel(part, h2, h3, g2, g3, o0, o1, o2, o3, q0, q1, q2, q3, mine, send, acc):
        acc[...] = part[...] + tn(h2[:, section_columns()], g2[...])
        acc[...] += tn(h3[:, section_columns()], g3[...])
        for o, q in ((o0, q0), (o1, q1), (o2, q2), (o3, q3)):
            acc[...] += tn(o[...], q[...])
        clip_parts(acc, mine, send)

    def sum_in_kernel(part, l2, l3, p2, p3, m0, m1, m2, m3, q0, q1, q2, q3, mine, send, acc):
        acc[...] = part[...] + tn(l2[...], p2[:, section_columns()])
        acc[...] += tn(l3[...], p3[:, section_columns()])
        for m, q in ((m0, q0), (m1, q1), (m2, q2), (m3, q3)):
            acc[...] += tn(m[...], q[...])
        clip_parts(acc, mine, send)

    def whole_part(kernel, part, *ins):
        rows_in, columns = part.shape
        mine, send = stage(
            kernel, [part, *ins], [near((rows_in // 2, columns), BF16)] * 2,
            [pltpu.VMEM((rows_in, columns), F32)],
        )
        return mine, z_swap(send, 1) if ring else send

    def over_sections(keep, send):
        return keep, y_swap(send) if ring else send

    def clip_rows(apart, size=eighth):
        here = lax.axis_index("dp") if ring else 0
        return pl.ds(pl.multiple_of((here ^ apart) * size, size), size)

    def over_near_clip(keep, got):
        if not ring:
            return keep, got

        def kernel(a, b, mine, send, acc):
            acc[...] = add(a[...], b[...])
            for out, first in ((mine, 0), (send, 1)):
                out[0:eighth, :] = acc[clip_rows(first), :].astype(BF16)
                out[eighth:, :] = acc[clip_rows(first ^ 2), :].astype(BF16)

        mine, send = stage(
            kernel, [keep, got], [near((2 * eighth, model), BF16)] * 2,
            [pltpu.VMEM((half_rows, model), F32)],
        )
        return mine, z_swap(send, 1)

    def over_far_clip(mine, got):
        if not ring:
            return mine, got
        size = mine.shape[0] // 2

        def kernel(a, b, own, send):
            own[...] = add(a[0:size, :], b[0:size, :]).astype(BF16)
            send[...] = add(a[size:, :], b[size:, :]).astype(BF16)

        own, send = stage(kernel, [mine, got], [near((size, mine.shape[1]), BF16)] * 2)
        return own, z_swap(send, 2)

    def to_far_clip(own, got):
        if not ring:
            return own, got
        (own,) = adds((own, got))
        return own, z_swap(own, 2)

    def to_near_clip(own, got):
        if not ring:
            return own, got

        size = own.shape[0]

        def kernel(a, b, out):
            out[0:size, :] = a[...]
            out[size:, :] = b[...]

        (both,) = stage(kernel, [own, got], [near((2 * size, own.shape[1]), BF16)])
        return both, z_swap(both, 1)

    def join_kernel(a, b, out):
        size = a.shape[0] // 2
        for apart, ref, at in ((0, a, 0), (2, a, size), (1, b, 0), (3, b, size)):
            out[clip_rows(apart, size), :] = ref[at : at + size, :]

    def to_sections(both, got, move=y_swap):
        if not ring:
            sec = lax.axis_index("pipe")
            early = jnp.where(sec == 0, both, got)
            later = jnp.where(sec == 0, got, both)
            early, later = lax.psum((early, later), ("pipe", "dp"))
            return jnp.where(sec == 0, early, later), jnp.where(sec == 0, later, early)
        (summed,) = stage(join_kernel, [both, got], [near((half_rows, model), BF16)])
        return summed, move(summed)

    def to_other_section(both, got):
        if not ring:
            both, got = lax.psum((both, got), "dp")
        (summed,) = stage(join_kernel, [both, got], [near((2 * both.shape[0], both.shape[1]), BF16)])
        return summed, y_swap(summed)

    def put_halves(keep, other, out):
        sec = lax.axis_index("pipe")
        for ref, at in ((keep, sec), (other, 1 - sec)):
            start = pl.multiple_of(at * half_rows, half_rows)
            out[pl.ds(start, half_rows), :] = ref[...].astype(F32)

    def whole(keep, other):
        return stage(put_halves, [keep, other], [shape_of((model, model), F32)])[0]

    def put_columns(keep, other, out):
        sec = lax.axis_index("pipe")
        for ref, at in ((keep, sec), (other, 1 - sec)):
            start = pl.multiple_of(at * half_rows, half_rows)
            out[:, pl.ds(start, half_rows)] = ref[...].astype(F32)

    def whole_of_columns(keep, other):
        return stage(put_columns, [keep, other], [shape_of((model, model), F32)])[0]

    def residual_back_of(at, a, b, resid, g, vecs):
        incoming = add(a[at, :], b[...])
        normed, inverse = norm_parts(resid[at, :])
        real = lax.broadcasted_iota(jnp.int32, incoming.shape, 0) < patch - at.start
        incoming = jnp.where(real, incoming, 0.0)
        from_out = g[at, :].astype(F32)
        grad = from_out + norm_back(incoming, normed, inverse, vecs[1:2])
        grad = jnp.where(real, grad, 0.0)
        low = grad.astype(BF16)
        sums = [row_sum(incoming * normed), row_sum(incoming), row_sum(low.astype(F32)), row_sum(from_out)]
        return grad, low, jnp.concatenate(sums + [jnp.zeros((4, model), F32)], axis=0)

    def residual_back_first_kernel(a, b, resid, g, vecs, grad_o, low_o, small_o):
        grad_o[...], low_o[...], small_o[...] = residual_back_of(row_parts[0], a, b, resid, g, vecs)

    def residual_back_last_kernel(
        a, b, resid, g, vecs, grad_in, low_in, small_in, grad_o, low_o, part_o, small_o
    ):
        grad, low, small = residual_back_of(row_parts[1], a, b, resid, g, vecs)
        for at, one, two in zip(row_parts, (grad_in[...], grad), (low_in[...], low)):
            grad_o[at, :] = one
            low_o[at, :] = two
        part_o[...] = low
        small_o[...] = small_in[...] + small

    def column_out(values_in, slot, keep_o, send_o):
        ten = lax.axis_index("tensor")
        spot = (ten ^ slot) & 1
        for i in range(4):
            block = values_in[:, i * width : (i + 1) * width]
            apart = ten ^ i
            for out, odd in ((keep_o, 0), (send_o, 1)):
                for side in range(2):

                    @pl.when(((apart & 1) == odd) & (spot == side))
                    def _():
                        out[apart >> 1, slot >> 1, :, side * width : (side + 1) * width] = block

    def attend_back_kernel(
        s, branch_in, q, k, v, probs, x, msg, w, vrow, wo, *refs
    ):
        extra = refs[0] if s == 0 else None
        back_o, grads_o, low_o, small_o = refs[-4:]
        gain, shift = vrow[0:1], vrow[1:2]
        here = lax.broadcasted_iota(jnp.int32, (rows, model), 0) == patch
        grad_mixed = nt(branch_in[...], wo[...]).astype(BF16)
        dq = jnp.zeros((rows, width), F32)
        dk = jnp.zeros((rows, width), F32)
        dv = jnp.zeros((rows, width), F32)
        for h, mask in enumerate(head_masks(rows)):
            grad_head = only(mask, grad_mixed)
            low_probs = probs[h]
            wide = low_probs.astype(F32)
            dv = dv + tn(low_probs, grad_head)
            grad_probs = nt(grad_head, v[...])
            inner = jnp.sum(wide * grad_probs, axis=-1, keepdims=True)
            grad_scores = (wide * (grad_probs - inner)).astype(BF16)
            dq = dq + only(mask, nn(grad_scores, k[...]))
            dk = dk + tn(grad_scores, only(mask, q[...]))
        dq = (dq * scale).astype(BF16)
        dk = (dk * scale).astype(BF16)
        dv = dv.astype(BF16)
        grads_o[0] = dq
        grads_o[1] = dk
        grads_o[2] = dv
        grad_low = nn(dq, w[0]) + nn(dk, w[1]) + nn(dv, w[2])
        token = jnp.where(here, msg[s : s + 1], x[...].astype(F32))
        normed, inverse = norm_parts(token)
        low_o[...] = (normed * gain + shift).astype(BF16)
        back = norm_back(grad_low, normed, inverse, gain)
        small_o[...] = jnp.zeros_like(small_o)
        small_o[0:1, :] = row_sum(only(here, back))
        small_o[1:2, :] = row_sum(grad_low * normed)
        small_o[2:3, :] = row_sum(grad_low)
        small_o[3:4, 0:width] = row_sum(dq.astype(F32))
        small_o[3:4, 256 : 256 + width] = row_sum(dv.astype(F32))
        if s == 0:
            back = back + extra[...]
        back_o[...] = back.astype(BF16)

    def attend_back(s, low_grad, kept):
        _, mixed, probs, k, v = kept
        ins = [low_grad, q_one[s], k, v, probs, x_slots[s], msg_rows, w_in, vec, w_out]
        return stage(
            functools.partial(attend_back_kernel, s),
            ins + ([grad_resid] if s == 0 else []),
            [
                near((rows, model), BF16),
                near((3, rows, width), BF16),
                near((rows, model), BF16),
                near((8, model), F32),
            ],
            flops=2 * rows * (4 * width * model + 4 * heads * rows * HEAD_DIM),
        )

    column_shapes = [near((2, 2, rows, 2 * width), BF16)] * 2

    def column_kernel(b0, b1, b2, b3, keep_o, send_o):
        for s, ref in enumerate((b0, b1, b2, b3)):
            column_out(ref[...], s, keep_o, send_o)

    def mlp_kernel(h0, h1, h2, h3, w, resid, vecs, *outs):
        for s, h in enumerate((h0, h1, h2, h3)):
            out = nn(h[...], w[...])
            if s == 0:
                out = out + resid[...] + vecs[4:5]
            outs[s][...] = out.astype(BF16)

    def far_columns(keep, got):
        def kernel(a, b, near_o, far_o):
            for i in range(2):
                near_o[i] = add(a[0, i], b[0, i]).astype(BF16)
                far_o[i ^ 1] = add(a[1, i], b[1, i]).astype(BF16)

        kept, send = stage(kernel, [keep, got], [near((2, rows, 2 * width), BF16)] * 2)
        return kept, x_swap(send)

    def frames_of(kept, far):
        low_pair = lax.axis_index("tensor") >> 1
        for i in range(2):
            total = add(kept[i], far[i])
            for side in range(2):
                yield (low_pair ^ i) * 2 + side, total[:, side * width : (side + 1) * width]

    def attend_weight_half_kernel(ga, gb, la, lb, ma, mb, ba, bb, out):
        for c in range(3):
            at = slice(c * width, (c + 1) * width)
            out[at, :] = tn(ga[c], la[...])
            out[at, :] += tn(gb[c], lb[...])
        out[3 * width :, :] = tn(ma[...], ba[...])
        out[3 * width :, :] += tn(mb[...], bb[...])

    def pack_kernel(s0, s1, s2, s3, two, p0, p1, p2, p3, out, acc):
        ten = lax.axis_index("tensor")
        acc[...] = jnp.zeros_like(acc)
        for s, ref in enumerate((s0, s1, s2, s3)):
            acc[pl.ds(ten ^ s, 1), :] = ref[0:1, :]
        acc[4:6, :] = s0[1:3, :] + s1[1:3, :] + s2[1:3, :] + s3[1:3, :]
        acc[6:10, :] = two[0:4, :]
        acc[pl.ds(10 + ten, 1), :] = p0[...] + p1[...] + p2[...] + p3[...]
        acc[pl.ds(14 + ten, 1), :] = s0[3:4, :] + s1[3:4, :] + s2[3:4, :] + s3[3:4, :]
        out[...] = acc[...].astype(BF16)

    def attend_weight_kernel(so_far, ga, gb, la, lb, ma, mb, ba, bb, keep, send, acc):
        for c in range(3):
            at = slice(c * width, (c + 1) * width)
            acc[at, :] = so_far[at, :] + tn(ga[c], la[...])
            acc[at, :] += tn(gb[c], lb[...])
        acc[3 * width :, :] = so_far[3 * width :, :] + tn(ma[...], ba[...])
        acc[3 * width :, :] += tn(mb[...], bb[...])
        halves_of(acc, keep, send)

    def merge_kernel(mine, other, out):
        a, b = mine[...].astype(F32), other[...].astype(F32)
        early = lax.axis_index("pipe") == 0
        out[...] = jnp.concatenate(
            [
                jnp.where(early, a[:half], b[:half]),
                jnp.where(early, b[:half], a[:half]),
                a[half : half + 24] + b[half : half + 24],
            ],
            axis=0,
        ).astype(BF16)

    def message_back(*refs):
        pack_refs, refs = refs[:pack_blocks], refs[pack_blocks:]
        (first, q, k, v, probs, w, wo, vrow, sent_o, grads_o, back_o) = refs
        sent = jnp.concatenate(
            [clip_block(pack_refs, c, pack_rows).astype(F32)[:frame_count] for c in range(clips)],
            axis=0,
        )
        low = sent.astype(BF16)
        sent_o[...] = sent
        grad_mixed = nt(low, wo[...]).astype(BF16)
        dq = jnp.zeros((all_rows, width), F32)
        dk = jnp.zeros((all_rows, width), F32)
        dv = jnp.zeros((all_rows, width), F32)
        for h, mask in enumerate(head_masks(all_rows)):
            grad_head = only(mask, grad_mixed)
            wide = probs[h]
            dv = dv + tn(wide.astype(BF16), grad_head)
            grad_probs = nt(grad_head, v[...])
            inner = jnp.sum(wide * grad_probs, axis=-1, keepdims=True)
            grad_scores = (wide * (grad_probs - inner)).astype(BF16)
            dq = dq + only(mask, nn(grad_scores, k[...]))
            dk = dk + tn(grad_scores, only(mask, q[...]))
        dq = (dq * scale).astype(BF16)
        dk = (dk * scale).astype(BF16)
        dv = dv.astype(BF16)
        grads_o[0] = dq
        grads_o[1] = dk
        grads_o[2] = dv
        grad_low = nn(dq, w[0]) + nn(dk, w[1]) + nn(dv, w[2])
        normed, inverse = norm_parts(first[...])
        back_msg = norm_back(grad_low, normed, inverse, vrow[0:1])
        back_o[0:all_rows, :] = back_msg.astype(BF16)
        tail = jnp.concatenate(
            [row_sum(grad_low * normed), row_sum(grad_low), jnp.zeros((14, model), F32)], axis=0
        )
        back_o[all_rows:, :] = tail.astype(BF16)

    def message_weight(sent, grads_in, low, mixed, in_o, out_o, qv_o, bias_o):
        for c in range(3):
            in_o[c] = tn(grads_in[c], low[...])
        out_o[...] = tn(mixed[...], sent[...].astype(BF16))
        qv_o[0:1, :] = row_sum(grads_in[0].astype(F32))
        qv_o[1:2, :] = row_sum(grads_in[2].astype(F32))
        bias_o[...] = row_sum(sent[...])

    def block_out_kernel(*refs):
        for at, total in frames_of(*refs[:-1]):
            refs[-1][at] = total.T[:, :patch].astype(BF16)

    def message_end(*refs):
        pack_refs, refs = refs[:pack_blocks], refs[pack_blocks:]
        cls_refs, refs = refs[:blocks], refs[blocks:]
        (sent, own, late, mw, qv_in, bias_in, w_o, cls_o, vec_o, qv_o, turned, sums) = refs
        sec, ten = lax.axis_index("pipe"), lax.axis_index("tensor")
        total = jnp.where(sec == 0, own[...].astype(F32), late[...].astype(F32))
        grad_first = sent[...] + total[:all_rows]
        at = pl.ds(pl.multiple_of(ten * width, width), width)
        mine = grad_first[:16]
        high = mine.astype(BF16)
        rest = (mine - high.astype(F32)).astype(BF16)
        mw_rows = mw[at, :]
        cls_o[...] = nt(high, mw_rows) + nt(rest, mw_rows)
        turned[...] = grad_first.T
        mine = turned[at, :]
        high = mine.astype(BF16)
        rest = (mine - high.astype(F32)).astype(BF16)
        cls = jnp.concatenate([clip_block(cls_refs, c, frame_count).astype(F32) for c in range(clips)])
        cls = cls.astype(BF16)
        w_o[...] = nn(high, cls) + nn(rest, cls)
        summed = clip_block(pack_refs, 0, pack_rows).astype(F32)
        for c in range(1, clips):
            summed = summed + clip_block(pack_refs, c, pack_rows).astype(F32)
        sums[...] = summed[frame_count:]
        first_one = sec == 0
        vec_o[0:1, :] = jnp.where(first_one, total[all_rows : all_rows + 1], sums[0:1])
        vec_o[1:2, :] = jnp.where(first_one, total[all_rows + 1 : all_rows + 2], sums[1:2])
        vec_o[2:3, :] = jnp.where(first_one, bias_in[...], sums[4:5])
        vec_o[3:4, :] = sums[2:3]
        vec_o[4:5, :] = sums[3:4]
        vec_o[5:6, :] = sums[5:6]
        vec_o[6:7, :] = sums[pl.ds(6 + ten, 1), :]
        vec_o[7:8, :] = row_sum(grad_first)
        qv_row = sums[pl.ds(10 + ten, 1), :]
        qv_o[0:1, :] = jnp.where(first_one, qv_in[0:1], qv_row[:, :width])
        qv_o[1:2, :] = jnp.where(first_one, qv_in[1:2], qv_row[:, 256 : 256 + width])

    def frames_grad_kernel(*refs):
        cls, out = refs[-2:]
        top = lax.broadcasted_iota(jnp.int32, (rows, width), 0) == 0
        for at, total in frames_of(*refs[:-2]):
            row = cls[pl.ds(lax.axis_index("pipe") * half + at, 1), :]
            out[at] = (total + jnp.where(top, row, 0.0)).T[:, :patch].astype(BF16)

    def attend_whole_kernel(keep, other, in_zero_ref, out_zero_ref, in_o, out_o, acc):
        @pl.when(lax.axis_index("pipe") == 0)
        def _():
            in_o[...] = in_zero_ref[...]
            out_o[...] = out_zero_ref[...]

        @pl.when(lax.axis_index("pipe") == 1)
        def _():
            put_halves(keep, other, acc)
            for c in range(3):
                in_o[c] = acc[c * width : (c + 1) * width, :]
            out_o[...] = acc[3 * width :, :]

    def pack_join_kernel(a, b, out):
        size = a.shape[0]
        out[0:size, :] = a[...]
        out[size:, :] = b[...]

    stage.cost = 0
    sent_out = y_early(own_out)
    cls_all = gather_clips(frames[0, :, 0, :])
    vectors, own_vec, near_in, in_and_vec = stage(
        small_kernel,
        [
            own_in, msg_bias, norm2_gain, norm2_shift, fc_in_bias, fc_out_bias,
            norm_gain, norm_shift, out_bias, qv_bias,
        ],
        [near((8, model), F32)] * 2 + [near(own_in.shape, BF16), near((3 * width + 16, model), BF16)],
        [pltpu.VMEM((model,), F32)] * 5
        + [pltpu.VMEM((1, model), F32)] * 3
        + [pltpu.VMEM((1, 2, width), F32), pltpu.SemaphoreType.DMA((13,))],
        far=10,
    )
    sent_in = y_early(in_and_vec)
    near_msg_w, near_out = stage(
        load_kernel, [msg_w, own_out], [near(msg_w.shape, BF16), near(own_out.shape, BF16)],
        [pltpu.SemaphoreType.DMA((2,))],
        far=2,
    )
    x_slots = slots(tokens, half)
    (first_msg, low_zero, q_zero, k_zero, v_zero, probs_zero, mixed_zero, part_zero) = stage(
        message_forward,
        [video_group, *cls_all, near_msg_w, vectors, own_vec, near_in, near_out],
        [
            near((all_rows, model), F32),
            near((all_rows, model), BF16),
            near((all_rows, width), BF16),
            near((all_rows, width), BF16),
            near((all_rows, width), BF16),
            near((heads, all_rows, all_rows), F32),
            near((all_rows, width), BF16),
            near((frame_count, model), F32),
        ],
        [pltpu.SMEM(video_group.shape, jnp.int32), pltpu.SemaphoreType.DMA],
        far=1,
    )
    from_core = core_swap(part_zero)
    (part_zero,) = adds((part_zero, from_core))
    from_x = x_swap(part_zero)
    (part_zero,) = adds((part_zero, from_x))
    part_late = y_late(part_zero)
    w_in, vec, *projected = stage(
        project_kernel, [*x_slots, near_in, sent_in, own_vec],
        [near(own_in.shape, BF16), near(own_vec.shape, F32)] + [near((rows, width), BF16)] * 12,
    )
    stage.cost = 0
    q_one, k_patch, v_patch = projected[:4], projected[4:8], projected[8:]
    msg_rows, k_msg, v_msg = stage(
        message_rows_kernel, [first_msg, part_zero, part_late, w_in, vec],
        [near((16, model), F32), near((16, width), F32), near((16, width), F32)],
    )

    at3 = (None, *attend(3))
    at2 = (None, *attend(2))
    pr3, w_out = stage(
        first_out_kernel, [at3[1], near_out, sent_out],
        [near((rows, model), BF16), near(own_out.shape, BF16)],
    )
    ac3 = core_swap(pr3)
    stage.cost = 4 * 10**9
    (pr2,) = stage(out_kernel, [at2[1], w_out], [near((rows, model), BF16)])
    two0, two1 = add_parts(pr2, ac3)
    ax0 = x_swap(two0)
    ax1 = x_swap(two1)
    at1 = attend(1, w_out)
    ac1 = core_swap(at1[0])
    at0 = attend(0, w_out)
    g_slots = slots(grads_in, 2 * half)
    (aown,) = adds((at0[0], ac1))
    resid0, low0 = stage(
        residual_first_kernel, [aown, ax0, x_slots[0], vec, vectors],
        [near((first_rows, model), F32), near((first_rows, model), BF16)],
    )
    lx0 = x_swap(low0)
    resid_own, low_own, low1 = stage(
        residual_last_kernel, [aown, ax1, x_slots[0], vec, vectors, resid0, low0],
        [near((rows, model), F32), near((rows, model), BF16), near((rows - first_rows, model), BF16)],
    )
    lx1 = x_swap(low1)
    l1 = core_swap(low_own)
    ly = y_swap(low_own)
    g_hidden = stage(
        grad_hidden_kernel, [*g_slots[:half], fc_out], [near((rows, hidden_width), BF16)] * half,
    )
    hid0, pre0, gp0, bs0 = feed(low_own, g_hidden[0])
    hid1, pre1, gp1, bs1 = feed(l1, g_hidden[1])
    fc1 = core_swap(gp1)
    fc_out_half = own_part(own_out_kernel, (half_rows, model), hid0, hid1, g_slots[0], g_slots[1])
    (fown,) = adds((gp0, fc1))
    l2 = join_parts(lx0, lx1)
    l3 = core_swap(l2)
    ly2 = y_swap(l2)
    hid2, pre2, gp2, bs2 = feed(l2, g_hidden[2])
    hid3, pre3, gp3, bs3 = feed(l3, g_hidden[3])
    fc3 = core_swap(gp3)
    m0 = relay(ly)
    m1 = core_swap(m0)
    two0, two1 = add_parts(gp2, fc3)
    fx0 = x_swap(two0)
    fx1 = x_swap(two1)
    ho0, po0 = feed_other(m0, g_slots[4])
    ho1, po1 = feed_other(m1, g_slots[5])
    block_parts = stage(
        mlp_kernel, [hid0, hid1, hid2, hid3, fc_out, resid_own, vectors],
        [near((rows, model), BF16)] * half,
    )
    fc_in_half = own_part(own_in_kernel, (model, half_rows), low_own, l1, pre0, pre1)
    grad0, glow0, small0 = stage(
        residual_back_first_kernel, [fown, fx0, resid_own, g_slots[0], vectors],
        [near((first_rows, model), F32), near((first_rows, model), BF16), near((8, model), F32)],
    )
    bx0 = x_swap(glow0)
    m2 = relay(ly2)
    m3 = core_swap(m2)
    grad_resid, grad_low, glow1, small_two = stage(
        residual_back_last_kernel,
        [fown, fx1, resid_own, g_slots[0], vectors, grad0, glow0, small0],
        [
            near((rows, model), F32), near((rows, model), BF16),
            near((rows - first_rows, model), BF16), near((8, model), F32),
        ],
    )
    bx1 = x_swap(glow1)
    b1 = core_swap(grad_low)
    ho2, po2 = feed_other(m2, g_slots[6])
    ho3, po3 = feed_other(m3, g_slots[7])
    p0 = whole_part(
        sum_out_kernel, fc_out_half, hid2, hid3, g_slots[2], g_slots[3], ho0, ho1, ho2, ho3, *g_slots[half:],
    )
    q0 = whole_part(
        sum_in_kernel, fc_in_half, l2, l3, pre2, pre3, m0, m1, m2, m3, po0, po1, po2, po3,
    )
    ba0, gr0, lo0, sm0 = attend_back(0, grad_low, at0)
    ba1, gr1, lo1, sm1 = attend_back(1, b1, at1)
    (attend_half,) = stage(
        attend_weight_half_kernel, [gr0, gr1, lo0, lo1, at0[1], at1[1], grad_low, b1],
        [near((4 * width, model), F32)],
    )
    b2 = join_parts(bx0, bx1)
    b3 = core_swap(b2)
    ba2, gr2, lo2, sm2 = attend_back(2, b2, at2)
    p1 = over_far_clip(*p0)
    ba3, gr3, lo3, sm3 = attend_back(3, b3, at3)
    (pk0,) = stage(
        pack_kernel, [sm0, sm1, sm2, sm3, small_two, bs0, bs1, bs2, bs3], [near((32, model), BF16)],
        [pltpu.VMEM((32, model), F32)],
    )
    pkc = core_swap(pk0)
    r0 = over_sections(
        *stage(
            attend_weight_kernel,
            [attend_half, gr2, gr3, lo2, lo3, at2[1], at3[1], b2, b3],
            half_shapes,
            [pltpu.VMEM((4 * width, model), F32)],
        )
    )
    (pk1,) = adds((pk0, pkc))
    pkx = x_swap(pk1)
    q1 = over_far_clip(*q0)
    p2 = to_far_clip(*p1)
    (pk2,) = adds((pk1, pkx))
    pky = y_swap(pk2)
    r1 = over_near_clip(*r0)
    q2 = to_far_clip(*q1)
    (pk3,) = stage(merge_kernel, [pk2, pky], [near((32, model), BF16)])
    pack_rows = pk3.shape[0]
    pkz = z_swap(pk3, 1) if ring else None
    p3 = to_near_clip(*p2)
    r2 = over_far_clip(*r1)
    if ring:
        (pk4,) = stage(pack_join_kernel, [pk3, pkz], [near((2 * pack_rows, model), BF16)])
        packs = [pk4, z_swap(pk4, 2)]
    else:
        packs = gather_clips(pk3)
    stage.cost = 0
    q3 = to_near_clip(*q2)
    stage.cost = 4 * 10**9
    p4 = to_other_section(*p3)
    sent_all, grads_zero, bz0 = stage(
        message_back,
        [*packs, first_msg, q_zero, k_zero, v_zero, probs_zero, near_in, near_out, own_vec],
        [
            near((all_rows, model), F32),
            near((3, all_rows, width), BF16),
            near((all_rows + 16, model), BF16),
        ],
    )
    bzc = core_swap(bz0)
    stage.cost = 10**10
    in_zero, out_zero, qv_zero, bias_zero = stage(
        message_weight, [sent_all, grads_zero, low_zero, mixed_zero],
        [
            near((3, width, model), F32),
            near((width, model), F32),
            near((2, width), F32),
            near((1, model), F32),
        ],
    )
    stage.cost = 4 * 10**9
    r3 = to_far_clip(*r2)
    (bz1,) = adds((bz0, bzc))
    bzx = x_swap(bz1)
    q4 = to_other_section(*q3)
    (bz2,) = adds((bz1, bzx))
    bzy = y_late(bz2)
    ck, send = stage(column_kernel, [ba0, ba1, ba2, ba3], column_shapes)
    cs = core_swap(send)
    msg_w_grad, cls_part, vec_grads, qv_grad = stage(
        message_end,
        [*packs, *cls_all, sent_all, bz2, bzy, near_msg_w, qv_zero, bias_zero],
        [
            shape_of((width, model), F32),
            near((16, width), F32),
            near((8, model), F32),
            near((2, width), F32),
        ],
        [pltpu.VMEM((model, all_rows), F32), pltpu.VMEM((24, model), F32)],
    )
    fc_out_grad = whole(*p4)
    kept, far = far_columns(ck, cs)
    bk, send = stage(column_kernel, block_parts, column_shapes)
    bcs = core_swap(send)
    r4 = to_near_clip(*r3)
    (frames_grad,) = stage(
        frames_grad_kernel, [kept, far, cls_part], [shape_of((half, width, patch), BF16)],
    )
    r5 = to_sections(*r4, move=y_late)
    bkept, bfar = far_columns(bk, bcs)
    fc_in_grad = whole_of_columns(*q4)
    (block_out,) = stage(
        block_out_kernel, [bkept, bfar], [shape_of((half, width, patch), BF16)],
    )
    attn_in_grad, attn_out_grad = stage(
        attend_whole_kernel, [*r5, in_zero, out_zero],
        [shape_of((3, width, model), F32), shape_of((width, model), F32)],
        [pltpu.VMEM((4 * width, model), F32)],
    )

    return (
        jnp.swapaxes(block_out, 1, 2)[None],
        jnp.swapaxes(frames_grad, 1, 2)[None],
        msg_w_grad.T,
        vec_grads[7],
        vec_grads[0:1],
        vec_grads[1:2],
        jnp.transpose(attn_in_grad, (2, 0, 1))[None],
        qv_grad[None],
        attn_out_grad[None],
        vec_grads[2:3],
        vec_grads[3],
        vec_grads[4],
        fc_in_grad,
        vec_grads[6],
        fc_out_grad,
        vec_grads[5],
    )


def solution(mesh):
    return jax.shard_map(
        body,
        mesh=mesh,
        in_specs=(
            P("dp", None, None, None),
            P(),
            P(),
            P(),
            P("pipe", None),
            P("pipe", None),
            P("pipe", None, None, "tensor"),
            P("pipe", None, "tensor"),
            P("pipe", "tensor", None),
            P("pipe", None),
            P(),
            P(),
            P(None, "tensor"),
            P("tensor"),
            P("tensor", None),
            P(),
            P("dp", None, None, None),
        ),
        out_specs=(
            P("dp", "pipe", None, "tensor"),
            P("dp", "pipe", None, "tensor"),
            P(None, "tensor"),
            P(),
            P("pipe", None),
            P("pipe", None),
            P("pipe", None, None, "tensor"),
            P("pipe", None, "tensor"),
            P("pipe", "tensor", None),
            P("pipe", None),
            P(),
            P(),
            P(None, "tensor"),
            P("tensor"),
            P("tensor", None),
            P(),
        ),
        check_vma=False,
    )
```
